32 devices in a mesh: lat: 4 (over y, core), wave: 8 (over z, x).
Axes of the slice: x: 2, y: 2, z: 4, core: 2. Of those that a mesh axis runs over, the one named last changes fastest.
Arguments:
- fourier: bfloat16 [256, 12, 1280], P(('lat', 'wave')), may hold values from -6 to 6
- wave_table: int32 [1280], replicated, may hold values from 0 to 1279, each once
- legendre: bfloat16 [1280, 128, 1280], P('wave', 'lat'), may hold values from -0.5 to 0.5
Outputs:
- spectral: float32 [1280, 12, 1280], P('wave', None, 'lat')
The draws below stay inside these ranges and needn't reach their ends.
Inputs may be any that keep to these rules, and one draw needn't show every extreme that they name: `wave_table`: every wavenumber 0 to 1279 stands in exactly one slot.
All inputs are finite; a program needn't handle non-finite values.
Results may differ from the reference program's by a relative error of at most 0.0031.
Values may be sent and summed in bfloat16 or wider, within the bound.
No kernel may reach another device: no remote copies, remote signals or barrier semaphores. Data moves between devices by JAX's collectives and lax.ppermute only.
A program may use at most 192 MiB of HBM per device.

```python
import jax
import jax.numpy as jnp
from jax import lax

M = 1280
N = 1280
PD = 32
COLS = 12
BANDS = 4
PAIRS = 128
ROWS = 256


def raised(values, stream_key, source, target, shards_of, factor):
    def block_of(axis_at):
        return (jnp.arange(values.shape[axis_at]) // (values.shape[axis_at] // shards_of)).reshape((-1,) + (1,) * (values.ndim - 1 - axis_at))

    one_side = jax.random.permutation(stream_key, shards_of)[block_of(target)]
    second = (block_of(target) + shards_of // 2) % shards_of
    return jnp.where((block_of(source) == one_side) | (block_of(source) == second), factor * values, values)


def steps_of(rng, shape, pieces, low, high):
    def one(position, shards_of):
        heights = jax.random.uniform(jax.random.fold_in(jax.random.fold_in(rng, 6), position), (shards_of,), jnp.float32, low / len(pieces), high / len(pieces))
        return jnp.repeat(jnp.exp(heights), shape[position] // shards_of).reshape((-1,) + (1,) * (len(shape) - position - 1))

    gain = one(*pieces[0])
    for cut in pieces[1:]:
        gain = gain * one(*cut)
    return gain


def gaussian(key, dims, width, most, split=(), held_as=jnp.bfloat16):
    level = steps_of(key, dims, split, -0.22, 0.18) if split else 1.0
    values = jax.random.normal(key, dims, jnp.float32) * width * level
    return jnp.minimum(jnp.maximum(values, -most), most).astype(held_as)


def heavy_noise(rng, extent, spread, limit, shards, heavy, kind=jnp.bfloat16):
    entries = spread * jax.random.normal(rng, extent, jnp.float32)
    if shards:
        entries = entries * steps_of(rng, extent, shards, -0.22, 0.18)
    return jnp.clip(raised(entries, jax.random.fold_in(rng, 3), *heavy), -limit, limit).astype(kind)


def setup_inputs(seed: int = 0) -> dict:
    keys = jax.random.split(jax.random.key(seed), 4)
    return {
        "fourier": gaussian(keys[0], (ROWS, COLS, M), 1.0, 6.0, ((0, 32),)),
        "wave_table": jax.random.permutation(keys[1], M).astype(jnp.int32),
        "legendre": heavy_noise(keys[2], (M, PAIRS, N), (2 * PAIRS) ** -0.5, 0.5, ((0, 8), (1, 4)), (1, 2, 4, 2.0)),
    }


def reference(fourier, wave_table, legendre):
    handled = jnp.arange(PAIRS, dtype=jnp.int32)
    band_block = handled // PD
    band_offset = handled % PD
    pair_index = jnp.where(band_block < BANDS // 2, 2 * PD * band_block + band_offset, 2 * PD * (BANDS - 1 - band_block) + PD + band_offset)
    south_index = ROWS - 1 - pair_index
    half_degrees = N // 2
    degree_slot = jnp.arange(N, dtype=jnp.int32)
    offsets = jnp.where(degree_slot < half_degrees, 2 * degree_slot, 2 * (degree_slot - half_degrees) + 1)

    def per_wave(inputs):
        wave_number, table = inputs
        wave_rows = lax.dynamic_index_in_dim(fourier, wave_number, 2, keepdims=False)
        north_rows = wave_rows[pair_index].astype(jnp.float32)
        south_rows = wave_rows[south_index].astype(jnp.float32)
        even_part = (north_rows + south_rows).astype(jnp.bfloat16)
        odd_part = (north_rows - south_rows).astype(jnp.bfloat16)
        even_out = jnp.dot(even_part.T, table[:, :half_degrees], preferred_element_type=jnp.float32)
        odd_out = jnp.dot(odd_part.T, table[:, half_degrees:], preferred_element_type=jnp.float32)
        result = jnp.concatenate([even_out, odd_out], axis=1)
        inside = offsets[None, :] < (N - wave_number)
        return jnp.where(inside, result, jnp.zeros_like(result))

    return lax.map(per_wave, (wave_table, legendre))
```

```python
import functools

import jax
import jax.numpy as jnp
import numpy as np
from jax import lax
from jax.experimental import pallas as pl
from jax.experimental.pallas import tpu as pltpu
from jax.sharding import PartitionSpec as P

LANES = 128
STEP = 16
VMEM = 48 * 1024 * 1024


def partner(block, axis, stride):
    count = lax.axis_size(axis)
    route = []
    for low in range(count):
        high = low | 1 << stride
        if high != low and high < count:
            route += [(low, high), (high, low)]
    return lax.ppermute(block, axis, route)


def plain(fourier, wave_table, legendre):
    slot_count, pair_count, degree_count = legendre.shape
    lat_count = lax.axis_size("lat")
    half_degrees = degree_count // 2
    slice_width = degree_count // lat_count
    lat_index = lax.axis_index("lat")
    ordered = jnp.take(fourier, wave_table, axis=2)
    arrived = lax.all_to_all(ordered, "wave", split_axis=2, concat_axis=0, tiled=True)
    local_rows = jnp.transpose(arrived, (2, 1, 0))
    kept_rows = local_rows[:, :, :pair_count]
    received = local_rows[:, :, pair_count:]
    for bit_number in range(lat_count.bit_length() - 1):
        received = partner(received, "lat", bit_number)
    northern = lat_index < lat_count // 2
    north_rows = jnp.where(northern, kept_rows, received).astype(jnp.float32)
    south_rows = jnp.where(northern, jnp.flip(received, 2), jnp.flip(kept_rows, 2)).astype(
        jnp.float32
    )
    even_part = (north_rows + south_rows).astype(jnp.bfloat16)
    odd_part = (north_rows - south_rows).astype(jnp.bfloat16)
    my_waves = lax.dynamic_slice_in_dim(wave_table, lax.axis_index("wave") * slot_count, slot_count)
    even_out = jnp.einsum(
        "mcp,mpk->mck", even_part, legendre[:, :, :half_degrees], preferred_element_type=jnp.float32
    )
    odd_out = jnp.einsum(
        "mcp,mpk->mck", odd_part, legendre[:, :, half_degrees:], preferred_element_type=jnp.float32
    )
    partial_terms = jnp.concatenate([even_out, odd_out], axis=2)
    spectral = lax.psum_scatter(partial_terms, "lat", scatter_dimension=2, tiled=True)
    degree_slot = lat_index * slice_width + jnp.arange(slice_width, dtype=jnp.int32)
    offsets = jnp.where(
        degree_slot < half_degrees, 2 * degree_slot, 2 * (degree_slot - half_degrees) + 1
    )
    inside = offsets[None, None, :] < (degree_count - my_waves)[:, None, None]
    return jnp.where(inside, spectral, jnp.zeros_like(spectral))


def gather_kernel(slots, cols, pad, table_ref, fourier_ref, *refs):
    outs, (rows, turned) = refs[:-2], refs[-2:]
    row_count, _, waves = fourier_ref.shape
    me = lax.axis_index("wave")
    rows[...] = jnp.zeros_like(rows)
    for row in range(row_count):
        rows[row * pad : row * pad + cols, :] = fourier_ref[row]
    width = 2 * LANES
    total = table_ref.shape[1]
    number = lax.broadcasted_iota(jnp.int32, (waves, width), 0)
    for start in range(0, total, width):
        chosen = (number == table_ref[:, start : start + width]).astype(jnp.bfloat16)
        got = jnp.dot(rows[...], chosen, preferred_element_type=jnp.float32)
        turned[start : start + width, :] = got.T.astype(jnp.bfloat16)
    for turn, out in enumerate(outs):
        first = pl.multiple_of((me ^ turn) * slots, STEP)
        out[...] = turned[pl.ds(first, slots), :]


def pack(terms, core, lane_low):
    rows = terms.shape[0]
    main = jnp.where(core == 0, terms[:, : 2 * LANES], terms[:, 3 * LANES :])
    mid = terms[:, 2 * LANES : 3 * LANES]
    turned = pltpu.roll(mid, LANES // 2, 1)
    part = rows // 4
    tails = []
    for j in range(2):
        low, high = slice(2 * j * part, (2 * j + 1) * part), slice((2 * j + 1) * part, (2 * j + 2) * part)
        zero = jnp.where(lane_low, mid[low], turned[high])
        one = jnp.where(lane_low, turned[low], mid[high])
        tails.append(jnp.where(core == 0, zero, one))
    return main, tails


def product_kernel(wave_count, lat_count, row_count, pad, cols, spread_ref, column_ref, diagonal_ref, leg_ref, *refs):
    sources = refs[:wave_count]
    far_out, far_own, near_out, near_own, place = refs[wave_count:]
    pairs = leg_ref.shape[1]
    half = leg_ref.shape[2] // 2
    lat, me = lax.axis_index("lat"), lax.axis_index("wave")
    northern = lat < lat_count // 2
    y, core = lat // 2, lat % 2
    lanes = row_count * pad

    @pl.when(pl.program_id(0) == 0)
    def _():
        row = lax.broadcasted_iota(jnp.int32, (lanes, 2 * LANES), 0) // pad
        col = lax.broadcasted_iota(jnp.int32, (lanes, 2 * LANES), 1)
        for turn in range(wave_count):
            source = me ^ turn
            ascending = (source < wave_count // 2) == northern
            position = (source % (wave_count // 2)) * row_count + row
            position = jnp.where(ascending, position, pairs - 1 - position)
            target = position + jnp.where(ascending, 0, LANES)
            place[turn * lanes : (turn + 1) * lanes, :] = (
                (col & (pairs - 1 | LANES)) == target
            ).astype(jnp.bfloat16)

    spread = spread_ref[...]
    column = column_ref[...]
    parts = [
        jnp.dot(spread, source[...], preferred_element_type=jnp.float32).astype(jnp.bfloat16) * column
        for source in sources
    ]
    both = jnp.dot(
        jnp.concatenate(parts, axis=1), place[...], preferred_element_type=jnp.float32
    )
    north, south = both[:, :LANES], both[:, LANES:]
    even, odd = north + south, north - south
    rows = STEP * cols
    group = 2 * LANES // pairs
    group_rows = group * cols
    lane_low = lax.broadcasted_iota(jnp.int32, (rows // 4, LANES), 1) < LANES // 2
    diagonal = diagonal_ref[...]
    for which, sent, kept in ((1 - y, far_out, far_own), (y, near_out, near_own)):
        coefs = jnp.where(which == 0, even, odd).astype(jnp.bfloat16)
        first = pl.multiple_of(which * half, LANES)
        done = []
        for g in range(STEP // group):
            block = coefs[g * group_rows : (g + 1) * group_rows]
            block = jnp.concatenate([block, block], axis=1) * diagonal
            table = leg_ref[g * group : (g + 1) * group, :, pl.ds(first, half)]
            done.append(
                jnp.dot(block, table.reshape(group * pairs, half), preferred_element_type=jnp.float32)
            )
        terms = jnp.concatenate(done, axis=0)
        for out, target in ((sent, 1 - core), (kept, core)):
            main, tails = pack(terms, target, lane_low)
            out[:rows, :] = main.astype(out.dtype)
            out[rows:, :LANES] = tails[0].astype(out.dtype)
            out[rows:, LANES:] = tails[1].astype(out.dtype)


def final_kernel(slots, base, degrees, cols, table_ref, own_ref, near_ref, far_ref, *refs):
    out = refs[-1]
    lat, me = lax.axis_index("lat"), lax.axis_index("wave")
    core = lat % 2
    half = degrees // 2
    width = out.shape[2]
    rows = STEP * cols
    part = rows // 4
    value = own_ref[...] + near_ref[...].astype(jnp.float32) + far_ref[...].astype(jnp.float32)
    main0, main1 = value[:rows, :LANES], value[:rows, LANES:]
    tails = []
    for j in range(4):
        tail = value[rows:, (j // 2) * LANES : (j // 2 + 1) * LANES]
        tails.append(pltpu.roll(tail, LANES // 2, 1) if j % 2 else tail)
    tail = jnp.concatenate(tails, axis=0)
    lane_low = lax.broadcasted_iota(jnp.int32, (rows, LANES), 1) < LANES // 2
    turn0, turn1 = pltpu.roll(main0, LANES // 2, 1), pltpu.roll(main1, LANES // 2, 1)
    first = core == 0
    ordered = jnp.concatenate(
        [
            jnp.where(first, main0, jnp.where(lane_low, tail, turn0)),
            jnp.where(first, main1, jnp.where(lane_low, turn0, turn1)),
            jnp.where(first, tail, turn1),
        ],
        axis=1,
    )
    slot = lat * width + lax.broadcasted_iota(jnp.int32, (cols, 3 * LANES), 1)
    offsets = jnp.where(slot < half, 2 * slot, 2 * (slot - half) + 1)
    start = me * slots + base + pl.program_id(0) * STEP
    for s in range(STEP):
        inside = offsets < degrees - table_ref[start + s]
        out[s] = jnp.where(inside, ordered[s * cols : (s + 1) * cols], 0.0)[:, :width]


def packed(fourier, wave_table, legendre, chunks):
    slots, pairs, degrees = legendre.shape
    row_count, cols, waves = fourier.shape
    wave_count, lat_count = lax.axis_size("wave"), lax.axis_size("lat")
    width = degrees // lat_count
    pad = LANES // row_count
    params = pltpu.CompilerParams(vmem_limit_bytes=VMEM)
    whole = pl.BlockSpec(memory_space=pltpu.VMEM)

    ordered = pl.pallas_call(
        functools.partial(gather_kernel, slots, cols, pad),
        out_shape=[jax.ShapeDtypeStruct((slots, LANES), jnp.bfloat16)] * wave_count,
        in_specs=[whole, whole],
        out_specs=[whole] * wave_count,
        scratch_shapes=[
            pltpu.VMEM((LANES, waves), jnp.bfloat16),
            pltpu.VMEM((slots * wave_count, LANES), jnp.bfloat16),
        ],
        compiler_params=params,
        name="gather",
    )(wave_table.reshape(1, -1), fourier)

    arrived = []
    for turn in range(wave_count):
        route = []
        for lat in range(lat_count):
            for wave in range(wave_count):
                to = lat if wave < wave_count // 2 else lat_count - 1 - lat
                route.append((lat * wave_count + wave, to * wave_count + (wave ^ turn)))
        arrived.append(lax.ppermute(ordered[turn], ("lat", "wave"), route))

    rows = STEP * cols
    step_rows = rows + rows // 4
    group = 2 * LANES // pairs
    at = np.arange(rows)
    spread = jnp.asarray(at[:, None] // cols == np.arange(STEP)[None, :], jnp.bfloat16)
    column = jnp.asarray(at[:, None] % cols == np.arange(LANES)[None, :] % pad, jnp.bfloat16)
    diagonal = jnp.asarray(
        at[: group * cols, None] // cols == np.arange(2 * LANES)[None, :] // pairs, jnp.bfloat16
    )

    core_route = [(lat, lat ^ 1) for lat in range(lat_count)]
    y_route = [(lat, lat ^ 2) for lat in range(lat_count)]
    out = None
    base = 0
    waiting = []
    for steps in chunks:
        message = (steps * step_rows, 2 * LANES)
        first = base // STEP
        block = pl.BlockSpec((step_rows, 2 * LANES), lambda g: (g, 0))
        far_out, far_own, near_out, near_own = pl.pallas_call(
            functools.partial(product_kernel, wave_count, lat_count, row_count, pad, cols),
            grid=(steps,),
            out_shape=[
                jax.ShapeDtypeStruct(message, jnp.bfloat16),
                jax.ShapeDtypeStruct(message, jnp.float32),
                jax.ShapeDtypeStruct(message, jnp.bfloat16),
                jax.ShapeDtypeStruct(message, jnp.float32),
            ],
            in_specs=[
                pl.BlockSpec(spread.shape, lambda g: (0, 0)),
                pl.BlockSpec(column.shape, lambda g: (0, 0)),
                pl.BlockSpec(diagonal.shape, lambda g: (0, 0)),
                pl.BlockSpec((STEP, pairs, degrees), lambda g, first=first: (first + g, 0, 0)),
            ]
            + [pl.BlockSpec((STEP, LANES), lambda g, first=first: (first + g, 0))] * wave_count,
            out_specs=[block] * 4,
            scratch_shapes=[pltpu.VMEM((wave_count * LANES, 2 * LANES), jnp.bfloat16)],
            compiler_params=params,
            cost_estimate=pl.CostEstimate(
                flops=2 * steps * STEP * pairs * group * cols * degrees,
                bytes_accessed=2 * steps * STEP * pairs * degrees,
                transcendentals=0,
            ),
            name="product",
        )(spread, column, diagonal, legendre, *arrived)
        far_in = lax.ppermute(far_out, "lat", core_route)
        near_in = lax.ppermute(near_out, "lat", core_route)
        across = (far_own + far_in.astype(jnp.float32)).astype(jnp.bfloat16)
        far_sum = lax.ppermute(across, "lat", y_route)
        waiting.append((steps, base, near_own, near_in, far_sum))
        base += steps * STEP

    for steps, base, near_own, near_in, far_sum in waiting:
        first = base // STEP
        block = pl.BlockSpec((step_rows, 2 * LANES), lambda g, table: (g, 0))
        carried = [] if out is None else [out]
        out = pl.pallas_call(
            functools.partial(final_kernel, slots, base, degrees, cols),
            grid_spec=pltpu.PrefetchScalarGridSpec(
                num_scalar_prefetch=1,
                grid=(steps,),
                in_specs=[block] * 3 + [pl.BlockSpec(memory_space=pl.ANY)] * len(carried),
                out_specs=pl.BlockSpec(
                    (STEP, cols, width), lambda g, table, first=first: (first + g, 0, 0)
                ),
            ),
            out_shape=jax.ShapeDtypeStruct((slots, cols, width), jnp.float32),
            input_output_aliases={4: 0} if carried else {},
            compiler_params=params,
            cost_estimate=pl.CostEstimate(
                flops=0, bytes_accessed=16 * steps * STEP * cols * width, transcendentals=0
            ),
            name="final",
        )(wave_table, near_own, near_in, far_sum, *carried)
    return out


def local(fourier, wave_table, legendre):
    slots, pairs, degrees = legendre.shape
    row_count, cols, waves = fourier.shape
    wave_count, lat_count = lax.axis_size("wave"), lax.axis_size("lat")
    half_tile = LANES // 2
    fits = (
        lat_count == 4
        and wave_count & (wave_count - 1) == 0
        and slots % STEP == 0
        and degrees // 2 == 5 * LANES
        and row_count * 2 * 8 == LANES
        and cols <= LANES // row_count
        and pairs == row_count * wave_count // 2
        and LANES % pairs == 0
        and STEP % (2 * LANES // pairs) == 0
        and STEP * cols % half_tile == 0
        and waves % (2 * LANES) == 0
    )
    if not fits:
        return plain(fourier, wave_table, legendre)
    steps = slots // STEP
    sizes = [steps // 4] * 4
    for extra in range(steps % 4):
        sizes[1 + extra] += 1
    return packed(fourier, wave_table, legendre, [size for size in sizes if size])


def solution(mesh):
    in_specs = (P(("lat", "wave"), None, None), P(), P("wave", "lat", None))
    out_specs = P("wave", None, "lat")
    return jax.shard_map(local, mesh=mesh, in_specs=in_specs, out_specs=out_specs, check_vma=False)
```

```python
import functools

import jax
import jax.numpy as jnp
from jax import lax
from jax.experimental import pallas as pl
from jax.experimental.pallas import tpu as pltpu
from jax.sharding import PartitionSpec as P

LANES = 128
STEP = 32
TILE = 8
VMEM = 48 * 1024 * 1024


def partner(block, axis, stride):
    count = lax.axis_size(axis)
    route = []
    for low in range(count):
        high = low | 1 << stride
        if high != low and high < count:
            route += [(low, high), (high, low)]
    return lax.ppermute(block, axis, route)


def plain(fourier, wave_table, legendre):
    slot_count, pair_count, degree_count = legendre.shape
    lat_count = lax.axis_size("lat")
    half_degrees = degree_count // 2
    slice_width = degree_count // lat_count
    lat_index = lax.axis_index("lat")
    ordered = jnp.take(fourier, wave_table, axis=2)
    arrived = lax.all_to_all(ordered, "wave", split_axis=2, concat_axis=0, tiled=True)
    local_rows = jnp.transpose(arrived, (2, 1, 0))
    kept_rows = local_rows[:, :, :pair_count]
    received = local_rows[:, :, pair_count:]
    for bit_number in range(lat_count.bit_length() - 1):
        received = partner(received, "lat", bit_number)
    northern = lat_index < lat_count // 2
    north_rows = jnp.where(northern, kept_rows, received).astype(jnp.float32)
    south_rows = jnp.where(northern, jnp.flip(received, 2), jnp.flip(kept_rows, 2)).astype(
        jnp.float32
    )
    even_part = (north_rows + south_rows).astype(jnp.bfloat16)
    odd_part = (north_rows - south_rows).astype(jnp.bfloat16)
    my_waves = lax.dynamic_slice_in_dim(wave_table, lax.axis_index("wave") * slot_count, slot_count)
    even_out = jnp.einsum(
        "mcp,mpk->mck", even_part, legendre[:, :, :half_degrees], preferred_element_type=jnp.float32
    )
    odd_out = jnp.einsum(
        "mcp,mpk->mck", odd_part, legendre[:, :, half_degrees:], preferred_element_type=jnp.float32
    )
    partial_terms = jnp.concatenate([even_out, odd_out], axis=2)
    spectral = lax.psum_scatter(partial_terms, "lat", scatter_dimension=2, tiled=True)
    degree_slot = lat_index * slice_width + jnp.arange(slice_width, dtype=jnp.int32)
    offsets = jnp.where(
        degree_slot < half_degrees, 2 * degree_slot, 2 * (degree_slot - half_degrees) + 1
    )
    inside = offsets[None, None, :] < (degree_count - my_waves)[:, None, None]
    return jnp.where(inside, spectral, jnp.zeros_like(spectral))


def gather_kernel(slots, table_ref, rows_ref, *refs):
    outs, turned = refs[:-1], refs[-1]
    count, waves = rows_ref.shape
    me = lax.axis_index("wave")
    rows = jnp.concatenate([rows_ref[...], jnp.zeros((LANES - count, waves), jnp.bfloat16)], axis=0)
    number = lax.broadcasted_iota(jnp.int32, (waves, LANES), 0)
    for j in range(0, table_ref.shape[0], 2):
        chosen = jnp.concatenate(
            [(number == table_ref[k : k + 1, :]).astype(jnp.bfloat16) for k in (j, j + 1)], axis=1
        )
        got = jnp.dot(rows, chosen, preferred_element_type=jnp.float32)
        turned[j * LANES : (j + 2) * LANES, :] = got.T.astype(jnp.bfloat16)
    for turn, out in enumerate(outs):
        first = pl.multiple_of((me ^ turn) * slots, STEP)
        out[...] = turned[pl.ds(first, slots), :]


def place_kernel(wave_count, lat_count, row_count, pairs, out):
    northern = lax.axis_index("lat") < lat_count // 2
    me = lax.axis_index("wave")
    row = lax.broadcasted_iota(jnp.int32, (LANES, 2 * LANES), 0) & (row_count - 1)
    col = lax.broadcasted_iota(jnp.int32, (LANES, 2 * LANES), 1) & (pairs - 1 | LANES)
    for turn in range(wave_count):
        source = me ^ turn
        ascending = (source < wave_count // 2) == northern
        position = (source % (wave_count // 2)) * row_count + row
        position = jnp.where(ascending, position, pairs - 1 - position)
        target = position + jnp.where(ascending, 0, LANES)
        out[turn * LANES : (turn + 1) * LANES, :] = (col == target).astype(jnp.bfloat16)


def product_kernel(base, row_count, cols, wave_count, place_ref, leg_ref, *refs):
    sources = refs[:wave_count]
    far_out, far_own, near_out, near_own, table, terms, sems = refs[wave_count:]
    pairs, degrees = leg_ref.shape[1:]
    half = degrees // 2
    group = 2 * LANES // pairs
    lat = lax.axis_index("lat")
    y, core = lat // 2, lat % 2
    copies = []
    for g in range(STEP // group):
        at = g * group
        copies.append(
            pltpu.make_async_copy(
                leg_ref.at[pl.ds(base + at, group)], table.at[pl.ds(at, group)], sems.at[g]
            )
        )
        copies[-1].start()
    held = lax.broadcasted_iota(jnp.int32, (STEP, LANES), 1) // row_count
    zero = jnp.zeros((STEP, LANES), jnp.bfloat16)
    parts = []
    for source in sources:
        value = source[base : base + STEP, :]
        parts.append(jnp.concatenate([jnp.where(held == c, value, zero) for c in range(cols)], axis=0))
    both = jnp.dot(
        jnp.concatenate(parts, axis=1), place_ref[...], preferred_element_type=jnp.float32
    )
    north, south = both[:, :LANES], both[:, LANES:]
    even, odd = north + south, north - south
    far, near = jnp.where(y == 0, odd, even), jnp.where(y == 0, even, odd)
    mask_shape = (cols * group, 2 * LANES)
    diagonal = (lax.broadcasted_iota(jnp.int32, mask_shape, 0) & (group - 1)) == (
        lax.broadcasted_iota(jnp.int32, mask_shape, 1) // pairs
    )
    blank = jnp.zeros(mask_shape, jnp.bfloat16)
    for side, coefs, which in ((0, far, 1 - y), (1, near, y)):
        first = pl.multiple_of(which * half, LANES)
        for g in range(STEP // group):
            if side == 0:
                copies[g].wait()
            block = jnp.concatenate(
                [coefs[c * STEP + g * group : c * STEP + (g + 1) * group] for c in range(cols)], axis=0
            ).astype(jnp.bfloat16)
            block = jnp.where(diagonal, jnp.concatenate([block, block], axis=1), blank)
            weights = table[g * group : (g + 1) * group, :, pl.ds(first, half)]
            got = jnp.dot(
                block, weights.reshape(group * pairs, half), preferred_element_type=jnp.float32
            )
            for c in range(cols):
                terms[side, pl.ds(c * STEP + g * group, group), :] = got[c * group : (c + 1) * group]
    rows = STEP * cols
    part = rows // 4
    lane_low = lax.broadcasted_iota(jnp.int32, (part, LANES), 1) < LANES // 2
    for side, sent, kept in ((0, far_out, far_own), (1, near_out, near_own)):
        for out, target in ((sent, 1 - core), (kept, core)):
            first = pl.multiple_of(target * 3 * LANES, LANES)
            out[:rows, :] = terms[side, :, pl.ds(first, 2 * LANES)].astype(out.dtype)
        for j in range(2):
            low = terms[side, pl.ds(2 * j * part, part), pl.ds(2 * LANES, LANES)]
            high = terms[side, pl.ds((2 * j + 1) * part, part), pl.ds(2 * LANES, LANES)]
            zeroth = jnp.where(lane_low, low, pltpu.roll(high, LANES // 2, 1))
            other = jnp.where(lane_low, pltpu.roll(low, LANES // 2, 1), high)
            for out, target in ((sent, 1 - core), (kept, core)):
                out[rows:, j * LANES : (j + 1) * LANES] = jnp.where(target == 0, zeroth, other).astype(
                    out.dtype
                )


def final_kernel(slots, base, degrees, cols, table_ref, own_ref, near_ref, far_ref, *refs):
    out = refs[-1]
    lat, me = lax.axis_index("lat"), lax.axis_index("wave")
    first = lat % 2 == 0
    half = degrees // 2
    width = out.shape[2]
    rows = STEP * cols
    value = own_ref[...] + near_ref[...].astype(jnp.float32) + far_ref[...].astype(jnp.float32)
    main0, main1 = value[:rows, :LANES], value[:rows, LANES:]
    tails = []
    for j in range(4):
        tail = value[rows:, (j // 2) * LANES : (j // 2 + 1) * LANES]
        tails.append(pltpu.roll(tail, LANES // 2, 1) if j % 2 else tail)
    tail = jnp.concatenate(tails, axis=0)
    lane_low = lax.broadcasted_iota(jnp.int32, (rows, LANES), 1) < LANES // 2
    turn0, turn1 = pltpu.roll(main0, LANES // 2, 1), pltpu.roll(main1, LANES // 2, 1)
    ordered = jnp.concatenate(
        [
            jnp.where(first, main0, jnp.where(lane_low, tail, turn0)),
            jnp.where(first, main1, jnp.where(lane_low, turn0, turn1)),
            jnp.where(first, tail, turn1),
        ],
        axis=1,
    )
    shape = (STEP, 3 * LANES)
    degree = lat * width + lax.broadcasted_iota(jnp.int32, shape, 1)
    offsets = jnp.where(degree < half, 2 * degree, 2 * (degree - half) + 1)
    line = lax.broadcasted_iota(jnp.int32, shape, 0)
    start = me * slots + base
    limits = jnp.zeros(shape, jnp.int32)
    for s in range(STEP):
        limits = jnp.where(line == s, degrees - table_ref[start + s], limits)
    inside = offsets < limits
    for c in range(cols):
        out[c] = jnp.where(inside, ordered[c * STEP : (c + 1) * STEP], 0.0)[:, :width]


def packed(fourier, wave_table, legendre):
    slots, pairs, degrees = legendre.shape
    row_count, cols, waves = fourier.shape
    wave_count, lat_count = lax.axis_size("wave"), lax.axis_size("lat")
    width = degrees // lat_count
    params = pltpu.CompilerParams(vmem_limit_bytes=VMEM)
    whole = pl.BlockSpec(memory_space=pltpu.VMEM)
    anywhere = pl.BlockSpec(memory_space=pl.ANY)

    ordered = pl.pallas_call(
        functools.partial(gather_kernel, slots),
        out_shape=[jax.ShapeDtypeStruct((slots, LANES), jnp.bfloat16)] * wave_count,
        in_specs=[whole, whole],
        out_specs=[whole] * wave_count,
        scratch_shapes=[pltpu.VMEM((slots * wave_count, LANES), jnp.bfloat16)],
        compiler_params=params,
        name="gather",
    )(
        wave_table.reshape(-1, LANES),
        jnp.transpose(fourier, (1, 0, 2)).reshape(cols * row_count, waves),
    )
    place = pl.pallas_call(
        functools.partial(place_kernel, wave_count, lat_count, row_count, pairs),
        out_shape=jax.ShapeDtypeStruct((wave_count * LANES, 2 * LANES), jnp.bfloat16),
        out_specs=whole,
        compiler_params=params,
        name="place",
    )()

    arrived = []
    for turn in range(wave_count):
        route = []
        for lat in range(lat_count):
            for wave in range(wave_count):
                to = lat if wave < wave_count // 2 else lat_count - 1 - lat
                route.append((lat * wave_count + wave, to * wave_count + (wave ^ turn)))
        arrived.append(lax.ppermute(ordered[turn], ("lat", "wave"), route))

    rows = STEP * cols
    message = (rows + rows // 4, 2 * LANES)
    group = 2 * LANES // pairs
    core_route = [(lat, lat ^ 1) for lat in range(lat_count)]
    y_route = [(lat, lat ^ 2) for lat in range(lat_count)]
    waiting, sent = [], []
    for base in range(0, slots, STEP):
        held = list(arrived)
        if len(sent) > 1:
            held, sent[-2] = lax.optimization_barrier((held, sent[-2]))
        far_out, far_own, near_out, near_own = pl.pallas_call(
            functools.partial(product_kernel, base, row_count, cols, wave_count),
            out_shape=[
                jax.ShapeDtypeStruct(message, jnp.bfloat16),
                jax.ShapeDtypeStruct(message, jnp.float32),
                jax.ShapeDtypeStruct(message, jnp.bfloat16),
                jax.ShapeDtypeStruct(message, jnp.float32),
            ],
            in_specs=[whole, anywhere] + [whole] * wave_count,
            out_specs=[whole] * 4,
            scratch_shapes=[
                pltpu.VMEM((STEP, pairs, degrees), jnp.bfloat16),
                pltpu.VMEM((2, rows, degrees // 2), jnp.float32),
                pltpu.SemaphoreType.DMA((STEP // group,)),
            ],
            compiler_params=params,
            cost_estimate=pl.CostEstimate(
                flops=2 * STEP * pairs * group * cols * degrees,
                bytes_accessed=2 * STEP * pairs * degrees,
                transcendentals=0,
            ),
            name="product",
        )(place, legendre, *held)
        far_in = lax.ppermute(far_out, "lat", core_route)
        sent.append((far_own + far_in.astype(jnp.float32)).astype(jnp.bfloat16))
        waiting.append((base, near_own, near_out))

    out = None
    for (base, near_own, near_out), across in zip(waiting, sent):
        near_in = lax.ppermute(near_out, "lat", core_route)
        far_sum = lax.ppermute(across, "lat", y_route)
        carried = [] if out is None else [out]
        out = pl.pallas_call(
            functools.partial(final_kernel, slots, base, degrees, cols),
            grid_spec=pltpu.PrefetchScalarGridSpec(
                num_scalar_prefetch=1,
                grid=(1,),
                in_specs=[pl.BlockSpec(message, lambda g, table: (0, 0))] * 3
                + [anywhere] * len(carried),
                out_specs=pl.BlockSpec(
                    (cols, STEP, width), lambda g, table, at=base // STEP: (0, at, 0)
                ),
            ),
            out_shape=jax.ShapeDtypeStruct((cols, slots, width), jnp.float32),
            input_output_aliases={4: 0} if carried else {},
            compiler_params=params,
            cost_estimate=pl.CostEstimate(
                flops=0, bytes_accessed=16 * STEP * cols * width, transcendentals=0
            ),
            name="final",
        )(wave_table, near_own, near_in, far_sum, *carried)
    return jnp.transpose(out, (1, 0, 2))


def local(fourier, wave_table, legendre):
    slots, pairs, degrees = legendre.shape
    row_count, cols, waves = fourier.shape
    wave_count, lat_count = lax.axis_size("wave"), lax.axis_size("lat")
    fits = (
        lat_count == 4
        and wave_count & (wave_count - 1) == 0
        and slots % STEP == 0
        and degrees // 2 == 5 * LANES
        and row_count & (row_count - 1) == 0
        and row_count * cols <= LANES
        and pairs == row_count * wave_count // 2
        and pairs * TILE == 2 * LANES
        and waves % (2 * LANES) == 0
    )
    if not fits:
        return plain(fourier, wave_table, legendre)
    return packed(fourier, wave_table, legendre)


def solution(mesh):
    in_specs = (P(("lat", "wave"), None, None), P(), P("wave", "lat", None))
    out_specs = P("wave", None, "lat")
    return jax.shard_map(local, mesh=mesh, in_specs=in_specs, out_specs=out_specs, check_vma=False)
```

```python
import functools

import jax
import jax.numpy as jnp
from jax import lax
from jax.experimental import pallas as pl
from jax.experimental.pallas import tpu as pltpu
from jax.sharding import PartitionSpec as P

LANES = 128
STEP = 32
TILE = 8
VMEM = 48 * 1024 * 1024


def partner(block, axis, stride):
    count = lax.axis_size(axis)
    route = []
    for low in range(count):
        high = low | 1 << stride
        if high != low and high < count:
            route += [(low, high), (high, low)]
    return lax.ppermute(block, axis, route)


def plain(fourier, wave_table, legendre):
    slot_count, pair_count, degree_count = legendre.shape
    lat_count = lax.axis_size("lat")
    half_degrees = degree_count // 2
    slice_width = degree_count // lat_count
    lat_index = lax.axis_index("lat")
    ordered = jnp.take(fourier, wave_table, axis=2)
    arrived = lax.all_to_all(ordered, "wave", split_axis=2, concat_axis=0, tiled=True)
    local_rows = jnp.transpose(arrived, (2, 1, 0))
    kept_rows = local_rows[:, :, :pair_count]
    received = local_rows[:, :, pair_count:]
    for bit_number in range(lat_count.bit_length() - 1):
        received = partner(received, "lat", bit_number)
    northern = lat_index < lat_count // 2
    north_rows = jnp.where(northern, kept_rows, received).astype(jnp.float32)
    south_rows = jnp.where(northern, jnp.flip(received, 2), jnp.flip(kept_rows, 2)).astype(
        jnp.float32
    )
    even_part = (north_rows + south_rows).astype(jnp.bfloat16)
    odd_part = (north_rows - south_rows).astype(jnp.bfloat16)
    my_waves = lax.dynamic_slice_in_dim(wave_table, lax.axis_index("wave") * slot_count, slot_count)
    even_out = jnp.einsum(
        "mcp,mpk->mck", even_part, legendre[:, :, :half_degrees], preferred_element_type=jnp.float32
    )
    odd_out = jnp.einsum(
        "mcp,mpk->mck", odd_part, legendre[:, :, half_degrees:], preferred_element_type=jnp.float32
    )
    partial_terms = jnp.concatenate([even_out, odd_out], axis=2)
    spectral = lax.psum_scatter(partial_terms, "lat", scatter_dimension=2, tiled=True)
    degree_slot = lat_index * slice_width + jnp.arange(slice_width, dtype=jnp.int32)
    offsets = jnp.where(
        degree_slot < half_degrees, 2 * degree_slot, 2 * (degree_slot - half_degrees) + 1
    )
    inside = offsets[None, None, :] < (degree_count - my_waves)[:, None, None]
    return jnp.where(inside, spectral, jnp.zeros_like(spectral))


def shift_of(block, used):
    return block * used // LANES, block * used % LANES


def gather_kernel(slots, table_ref, rows_ref, out, turned):
    used, waves = rows_ref.shape
    rows = jnp.concatenate([rows_ref[...], jnp.zeros((LANES - used, waves), jnp.bfloat16)], axis=0)
    number = lax.broadcasted_iota(jnp.int32, (waves, LANES), 0)
    for j in range(0, table_ref.shape[0], 2):
        chosen = jnp.concatenate(
            [(number == table_ref[k : k + 1, :]).astype(jnp.bfloat16) for k in (j, j + 1)], axis=1
        )
        got = jnp.dot(rows, chosen, preferred_element_type=jnp.float32)
        turned[j * LANES : (j + 2) * LANES, :] = got.T
    lane = lax.broadcasted_iota(jnp.int32, (STEP, LANES), 1)
    for wave in range(out.shape[0]):
        tiles = [jnp.zeros((STEP, LANES), jnp.float32)] * (out.shape[2] // LANES)
        for block in range(slots // STEP):
            tile, off = shift_of(block, used)
            first = wave * slots + block * STEP
            value = turned[first : first + STEP, :]
            value = pltpu.roll(value, off, 1) if off else value
            tiles[tile] = jnp.where(lane >= off, value, tiles[tile])
            if off + used > LANES:
                tiles[tile + 1] = jnp.where(lane < off + used - LANES, value, tiles[tile + 1])
        for k, tile in enumerate(tiles):
            out[wave, :, k * LANES : (k + 1) * LANES] = tile.astype(jnp.bfloat16)


def place_kernel(source_count, lat_count, row_count, pairs, out):
    northern = lax.axis_index("lat") < lat_count // 2
    row = lax.broadcasted_iota(jnp.int32, (LANES, 2 * LANES), 0) & (row_count - 1)
    col = lax.broadcasted_iota(jnp.int32, (LANES, 2 * LANES), 1) & (pairs - 1 | LANES)
    for source in range(source_count):
        ascending = (source < source_count // 2) == northern
        position = (source % (source_count // 2)) * row_count + row
        position = jnp.where(ascending, position, pairs - 1 - position)
        target = position + jnp.where(ascending, 0, LANES)
        out[source * LANES : (source + 1) * LANES, :] = (col == target).astype(jnp.bfloat16)


def fetch(base, which, leg_ref, table, sems):
    half = table.shape[2]
    group = 2 * LANES // table.shape[1]
    first = pl.multiple_of(which * half, LANES)
    copies = []
    for g in range(STEP // group):
        copies.append(
            pltpu.make_async_copy(
                leg_ref.at[pl.ds(base + g * group, group), :, pl.ds(first, half)],
                table.at[pl.ds(g * group, group)],
                sems.at[g],
            )
        )
        copies[-1].start()
    return copies


def multiply(copies, coefs, table, terms):
    pairs, half = table.shape[1:]
    group = 2 * LANES // pairs
    cols = coefs.shape[0] // STEP
    shape = (cols * group, 2 * LANES)
    diagonal = (lax.broadcasted_iota(jnp.int32, shape, 0) & (group - 1)) == (
        lax.broadcasted_iota(jnp.int32, shape, 1) // pairs
    )
    blank = jnp.zeros(shape, jnp.bfloat16)
    for g, copy in enumerate(copies):
        block = jnp.concatenate(
            [coefs[c * STEP + g * group : c * STEP + (g + 1) * group] for c in range(cols)], axis=0
        ).astype(jnp.bfloat16)
        block = jnp.where(diagonal, jnp.concatenate([block, block], axis=1), blank)
        copy.wait()
        weights = table[g * group : (g + 1) * group].reshape(group * pairs, half)
        got = jnp.dot(block, weights, preferred_element_type=jnp.float32)
        for c in range(cols):
            terms[pl.ds(c * STEP + g * group, group), :] = got[c * group : (c + 1) * group]


def pack(terms, core, sent, kept):
    rows = terms.shape[0]
    part = rows // 4
    lane_low = lax.broadcasted_iota(jnp.int32, (part, LANES), 1) < LANES // 2
    for out, target in ((sent, 1 - core), (kept, core)):
        first = pl.multiple_of(target * 3 * LANES, LANES)
        out[:rows, :] = terms[:, pl.ds(first, 2 * LANES)].astype(out.dtype)
    for j in range(2):
        low = terms[pl.ds(2 * j * part, part), pl.ds(2 * LANES, LANES)]
        high = terms[pl.ds((2 * j + 1) * part, part), pl.ds(2 * LANES, LANES)]
        zeroth = jnp.where(lane_low, low, pltpu.roll(high, LANES // 2, 1))
        other = jnp.where(lane_low, pltpu.roll(low, LANES // 2, 1), high)
        for out, target in ((sent, 1 - core), (kept, core)):
            out[rows:, j * LANES : (j + 1) * LANES] = jnp.where(target == 0, zeroth, other).astype(
                out.dtype
            )


def far_kernel(block, row_count, cols, place_ref, kept_ref, mirror_ref, leg_ref, *refs):
    sent, own, near_coefs, table, terms, sems = refs
    lat = lax.axis_index("lat")
    y, core = lat // 2, lat % 2
    copies = fetch(block * STEP, 1 - y, leg_ref, table, sems)
    tile, off = shift_of(block, row_count * cols)
    lane = lax.broadcasted_iota(jnp.int32, (STEP, LANES), 1)
    held = ((lane - off) & (LANES - 1)) // row_count
    zero = jnp.zeros((STEP, LANES), jnp.bfloat16)
    parts = []
    for source in (kept_ref, mirror_ref):
        for k in range(mirror_ref.shape[0]):
            value = source[k, :, tile * LANES : (tile + 1) * LANES]
            if off + row_count * cols > LANES:
                value = jnp.where(
                    lane >= off, value, source[k, :, (tile + 1) * LANES : (tile + 2) * LANES]
                )
            parts.append(
                jnp.concatenate([jnp.where(held == c, value, zero) for c in range(cols)], axis=0)
            )
    both = jnp.dot(
        jnp.concatenate(parts, axis=1), place_ref[...], preferred_element_type=jnp.float32
    )
    north, south = both[:, :LANES], both[:, LANES:]
    even, odd = north + south, north - south
    near_coefs[...] = jnp.where(y == 0, even, odd)
    multiply(copies, jnp.where(y == 0, odd, even), table, terms)
    pack(terms, core, sent, own)


def near_kernel(block, coefs_ref, leg_ref, *refs):
    sent, own, table, terms, sems = refs
    lat = lax.axis_index("lat")
    copies = fetch(block * STEP, lat // 2, leg_ref, table, sems)
    multiply(copies, coefs_ref[...], table, terms)
    pack(terms, lat % 2, sent, own)


def final_kernel(slots, base, degrees, cols, table_ref, near_ref, far_ref, *refs):
    out = refs[-1]
    lat, me = lax.axis_index("lat"), lax.axis_index("wave")
    first = lat % 2 == 0
    half = degrees // 2
    width = out.shape[2]
    rows = STEP * cols
    value = near_ref[...] + far_ref[...].astype(jnp.float32)
    main0, main1 = value[:rows, :LANES], value[:rows, LANES:]
    tails = []
    for j in range(4):
        tail = value[rows:, (j // 2) * LANES : (j // 2 + 1) * LANES]
        tails.append(pltpu.roll(tail, LANES // 2, 1) if j % 2 else tail)
    tail = jnp.concatenate(tails, axis=0)
    lane_low = lax.broadcasted_iota(jnp.int32, (rows, LANES), 1) < LANES // 2
    turn0, turn1 = pltpu.roll(main0, LANES // 2, 1), pltpu.roll(main1, LANES // 2, 1)
    ordered = jnp.concatenate(
        [
            jnp.where(first, main0, jnp.where(lane_low, tail, turn0)),
            jnp.where(first, main1, jnp.where(lane_low, turn0, turn1)),
            jnp.where(first, tail, turn1),
        ],
        axis=1,
    )
    shape = (STEP, 3 * LANES)
    degree = lat * width + lax.broadcasted_iota(jnp.int32, shape, 1)
    offsets = jnp.where(degree < half, 2 * degree, 2 * (degree - half) + 1)
    line = lax.broadcasted_iota(jnp.int32, shape, 0)
    start = me * slots + base
    limits = jnp.zeros(shape, jnp.int32)
    for s in range(STEP):
        limits = jnp.where(line == s, degrees - table_ref[start + s], limits)
    inside = offsets < limits
    for c in range(cols):
        out[c] = jnp.where(inside, ordered[c * STEP : (c + 1) * STEP], 0.0)[:, :width]


def packed(fourier, wave_table, legendre):
    slots, pairs, degrees = legendre.shape
    row_count, cols, waves = fourier.shape
    wave_count, lat_count = lax.axis_size("wave"), lax.axis_size("lat")
    width = degrees // lat_count
    used = row_count * cols
    params = pltpu.CompilerParams(vmem_limit_bytes=VMEM)
    whole = pl.BlockSpec(memory_space=pltpu.VMEM)
    anywhere = pl.BlockSpec(memory_space=pl.ANY)

    message = -(-(slots // STEP) * used // LANES) * LANES
    ordered = pl.pallas_call(
        functools.partial(gather_kernel, slots),
        out_shape=jax.ShapeDtypeStruct((wave_count, STEP, message), jnp.bfloat16),
        in_specs=[whole, whole],
        out_specs=whole,
        scratch_shapes=[pltpu.VMEM((slots * wave_count, LANES), jnp.float32)],
        compiler_params=params,
        name="gather",
    )(
        wave_table.reshape(-1, LANES),
        jnp.transpose(fourier, (1, 0, 2)).reshape(used, waves),
    )
    place = pl.pallas_call(
        functools.partial(place_kernel, wave_count, lat_count, row_count, pairs),
        out_shape=jax.ShapeDtypeStruct((wave_count * LANES, 2 * LANES), jnp.bfloat16),
        out_specs=whole,
        compiler_params=params,
        name="place",
    )()
    arrived = lax.all_to_all(ordered, "wave", split_axis=0, concat_axis=0, tiled=True)
    mirror = lax.ppermute(
        arrived[wave_count // 2 :], "lat", [(lat, lat_count - 1 - lat) for lat in range(lat_count)]
    )

    rows = STEP * cols
    shape = (rows + rows // 4, 2 * LANES)
    group = 2 * LANES // pairs
    core_route = [(lat, lat ^ 1) for lat in range(lat_count)]
    y_route = [(lat, lat ^ 2) for lat in range(lat_count)]
    scratch = [
        pltpu.VMEM((STEP, pairs, degrees // 2), jnp.bfloat16),
        pltpu.VMEM((rows, degrees // 2), jnp.float32),
        pltpu.SemaphoreType.DMA((STEP // group,)),
    ]
    cost = pl.CostEstimate(flops=0, bytes_accessed=1024, transcendentals=0)
    pair_of_sums = [
        jax.ShapeDtypeStruct(shape, jnp.bfloat16),
        jax.ShapeDtypeStruct(shape, jnp.float32),
    ]
    count = slots // STEP

    def far(block, sources):
        return pl.pallas_call(
            functools.partial(far_kernel, block, row_count, cols),
            out_shape=pair_of_sums + [jax.ShapeDtypeStruct((rows, LANES), jnp.float32)],
            in_specs=[whole] * 3 + [anywhere],
            out_specs=[whole] * 3,
            scratch_shapes=scratch,
            compiler_params=params,
            cost_estimate=cost,
            name="far",
        )(place, *sources, legendre)

    def near(block, coefs):
        return pl.pallas_call(
            functools.partial(near_kernel, block),
            out_shape=pair_of_sums,
            in_specs=[whole, anywhere],
            out_specs=[whole] * 2,
            scratch_shapes=scratch,
            compiler_params=params,
            cost_estimate=cost,
            name="near",
        )(coefs, legendre)

    def settle(pair):
        sent, kept = pair
        return kept + lax.ppermute(sent, "lat", core_route).astype(jnp.float32)

    def cross(pair):
        summed = settle(pair).astype(jnp.bfloat16)
        return summed, lax.ppermute(summed, "lat", y_route)

    sources = (arrived, mirror)
    crossed, settled = [], []
    ahead = [far(block, sources) for block in range(min(2, count))]
    for block in range(count):
        *pair, coefs = ahead[block]
        summed, far_sum = cross(pair)
        crossed.append(far_sum)
        ties = [summed] + settled[-1:]
        coefs, ties = lax.optimization_barrier((coefs, ties))
        pair = near(block, coefs)
        settled.append(settle(pair))
        if block + 2 < count:
            sources, pair = lax.optimization_barrier((sources, pair))
            ahead.append(far(block + 2, sources))

    out = None
    for block in range(count):
        carried = [] if out is None else [out]
        out = pl.pallas_call(
            functools.partial(final_kernel, slots, block * STEP, degrees, cols),
            grid_spec=pltpu.PrefetchScalarGridSpec(
                num_scalar_prefetch=1,
                grid=(1,),
                in_specs=[whole] * 2 + [anywhere] * len(carried),
                out_specs=pl.BlockSpec((cols, STEP, width), lambda g, table, at=block: (0, at, 0)),
            ),
            out_shape=jax.ShapeDtypeStruct((cols, slots, width), jnp.float32),
            input_output_aliases={3: 0} if carried else {},
            compiler_params=params,
            cost_estimate=cost,
            name="final",
        )(wave_table, settled[block], crossed[block], *carried)
    return jnp.transpose(out, (1, 0, 2))


def local(fourier, wave_table, legendre):
    slots, pairs, degrees = legendre.shape
    row_count, cols, waves = fourier.shape
    wave_count, lat_count = lax.axis_size("wave"), lax.axis_size("lat")
    fits = (
        lat_count == 4
        and wave_count & (wave_count - 1) == 0
        and slots % STEP == 0
        and degrees // 2 == 5 * LANES
        and row_count & (row_count - 1) == 0
        and LANES // 4 % row_count == 0
        and row_count * cols % (LANES // 4) == 0
        and row_count * cols <= LANES
        and pairs == row_count * wave_count // 2
        and pairs * TILE == 2 * LANES
        and waves % (2 * LANES) == 0
    )
    if not fits:
        return plain(fourier, wave_table, legendre)
    return packed(fourier, wave_table, legendre)


def solution(mesh):
    in_specs = (P(("lat", "wave"), None, None), P(), P("wave", "lat", None))
    out_specs = P("wave", None, "lat")
    return jax.shard_map(local, mesh=mesh, in_specs=in_specs, out_specs=out_specs, check_vma=False)
```

```python
import functools

import jax
import jax.numpy as jnp
from jax import lax
from jax.experimental import pallas as pl
from jax.experimental.pallas import tpu as pltpu
from jax.sharding import PartitionSpec as P

LANES = 128
STEP = 32
TILE = 8
VMEM = 48 * 1024 * 1024


def partner(block, axis, stride):
    count = lax.axis_size(axis)
    route = []
    for low in range(count):
        high = low | 1 << stride
        if high != low and high < count:
            route += [(low, high), (high, low)]
    return lax.ppermute(block, axis, route)


def plain(fourier, wave_table, legendre):
    slot_count, pair_count, degree_count = legendre.shape
    lat_count = lax.axis_size("lat")
    half_degrees = degree_count // 2
    slice_width = degree_count // lat_count
    lat_index = lax.axis_index("lat")
    ordered = jnp.take(fourier, wave_table, axis=2)
    arrived = lax.all_to_all(ordered, "wave", split_axis=2, concat_axis=0, tiled=True)
    local_rows = jnp.transpose(arrived, (2, 1, 0))
    kept_rows = local_rows[:, :, :pair_count]
    received = local_rows[:, :, pair_count:]
    for bit_number in range(lat_count.bit_length() - 1):
        received = partner(received, "lat", bit_number)
    northern = lat_index < lat_count // 2
    north_rows = jnp.where(northern, kept_rows, received).astype(jnp.float32)
    south_rows = jnp.where(northern, jnp.flip(received, 2), jnp.flip(kept_rows, 2)).astype(
        jnp.float32
    )
    even_part = (north_rows + south_rows).astype(jnp.bfloat16)
    odd_part = (north_rows - south_rows).astype(jnp.bfloat16)
    my_waves = lax.dynamic_slice_in_dim(wave_table, lax.axis_index("wave") * slot_count, slot_count)
    even_out = jnp.einsum(
        "mcp,mpk->mck", even_part, legendre[:, :, :half_degrees], preferred_element_type=jnp.float32
    )
    odd_out = jnp.einsum(
        "mcp,mpk->mck", odd_part, legendre[:, :, half_degrees:], preferred_element_type=jnp.float32
    )
    partial_terms = jnp.concatenate([even_out, odd_out], axis=2)
    spectral = lax.psum_scatter(partial_terms, "lat", scatter_dimension=2, tiled=True)
    degree_slot = lat_index * slice_width + jnp.arange(slice_width, dtype=jnp.int32)
    offsets = jnp.where(
        degree_slot < half_degrees, 2 * degree_slot, 2 * (degree_slot - half_degrees) + 1
    )
    inside = offsets[None, None, :] < (degree_count - my_waves)[:, None, None]
    return jnp.where(inside, spectral, jnp.zeros_like(spectral))


def shift_of(block, used):
    return block * used // LANES, block * used % LANES


def gather_kernel(slots, low, table_ref, rows_ref, *refs):
    outs, turned = refs[:-1], refs[-1]
    me = lax.axis_index("wave")
    used, waves = rows_ref.shape
    rows = jnp.concatenate([rows_ref[...], jnp.zeros((LANES - used, waves), jnp.bfloat16)], axis=0)
    number = lax.broadcasted_iota(jnp.int32, (waves, LANES), 0)
    for j in range(0, table_ref.shape[0], 2):
        chosen = jnp.concatenate(
            [(number == table_ref[k : k + 1, :]).astype(jnp.bfloat16) for k in (j, j + 1)], axis=1
        )
        got = jnp.dot(rows, chosen, preferred_element_type=jnp.float32)
        turned[j * LANES : (j + 2) * LANES, :] = got.T
    lane = lax.broadcasted_iota(jnp.int32, (STEP, LANES), 1)
    for t, out in enumerate(outs):
        for u in range(low):
            begin = (me ^ (t * low + u)) * slots
            tiles = [jnp.zeros((STEP, LANES), jnp.float32)] * (out.shape[2] // LANES)
            for block in range(slots // STEP):
                tile, off = shift_of(block, used)
                value = turned[pl.ds(pl.multiple_of(begin + block * STEP, STEP), STEP), :]
                value = pltpu.roll(value, off, 1) if off else value
                tiles[tile] = jnp.where(lane >= off, value, tiles[tile])
                if off + used > LANES:
                    tiles[tile + 1] = jnp.where(lane < off + used - LANES, value, tiles[tile + 1])
            for k, tile in enumerate(tiles):
                out[u, :, k * LANES : (k + 1) * LANES] = tile.astype(jnp.bfloat16)


def place_kernel(turns, lat_count, row_count, pairs, degrees, table_ref, out, limits):
    northern = lax.axis_index("lat") < lat_count // 2
    me = lax.axis_index("wave")
    row = lax.broadcasted_iota(jnp.int32, (LANES, 2 * LANES), 0) & (row_count - 1)
    col = lax.broadcasted_iota(jnp.int32, (LANES, 2 * LANES), 1) & (pairs - 1 | LANES)
    half = len(turns) // 2
    for k, turn in enumerate(turns):
        source = me ^ turn
        ascending = (source < half) == northern
        position = (source % half) * row_count + row
        position = jnp.where(ascending, position, pairs - 1 - position)
        target = position + jnp.where(ascending, 0, LANES)
        out[k * LANES : (k + 1) * LANES, :] = (col == target).astype(jnp.bfloat16)
    slots = limits.shape[0]
    line = lax.broadcasted_iota(jnp.int32, (TILE, LANES), 0)
    for first in range(0, slots, TILE):
        value = jnp.zeros((TILE, LANES), jnp.int32)
        for s in range(TILE):
            value = jnp.where(line == s, degrees - table_ref[me * slots + first + s], value)
        limits[first : first + TILE, :] = value


def multiply(coefs, table, first, half, terms):
    pairs = table.shape[1]
    group = 2 * LANES // pairs
    cols = coefs.shape[0] // STEP
    shape = (cols * group, 2 * LANES)
    diagonal = (lax.broadcasted_iota(jnp.int32, shape, 0) & (group - 1)) == (
        lax.broadcasted_iota(jnp.int32, shape, 1) // pairs
    )
    blank = jnp.zeros(shape, jnp.bfloat16)
    for g in range(STEP // group):
        block = jnp.concatenate(
            [coefs[c * STEP + g * group : c * STEP + (g + 1) * group] for c in range(cols)], axis=0
        ).astype(jnp.bfloat16)
        block = jnp.where(diagonal, jnp.concatenate([block, block], axis=1), blank)
        weights = table[g * group : (g + 1) * group, :, pl.ds(first, half)]
        got = jnp.dot(
            block, weights.reshape(group * pairs, half), preferred_element_type=jnp.float32
        )
        for c in range(cols):
            terms[pl.ds(c * STEP + g * group, group), :] = got[c * group : (c + 1) * group]


def pack(terms, core, sent, kept):
    rows = terms.shape[0]
    part = rows // 4
    lane_low = lax.broadcasted_iota(jnp.int32, (part, LANES), 1) < LANES // 2
    for out, target in ((sent, 1 - core), (kept, core)):
        first = pl.multiple_of(target * 3 * LANES, LANES)
        out[:rows, :] = terms[:, pl.ds(first, 2 * LANES)].astype(out.dtype)
    for j in range(2):
        low = terms[pl.ds(2 * j * part, part), pl.ds(2 * LANES, LANES)]
        high = terms[pl.ds((2 * j + 1) * part, part), pl.ds(2 * LANES, LANES)]
        zeroth = jnp.where(lane_low, low, pltpu.roll(high, LANES // 2, 1))
        other = jnp.where(lane_low, pltpu.roll(low, LANES // 2, 1), high)
        for out, target in ((sent, 1 - core), (kept, core)):
            out[rows:, j * LANES : (j + 1) * LANES] = jnp.where(target == 0, zeroth, other).astype(
                out.dtype
            )


def product_kernel(block, row_count, cols, place_ref, leg_ref, *refs):
    sources = refs[:-8]
    far_sent, far_own, near_sent, near_own, table, far, near, sem = refs[-8:]
    half = far.shape[1]
    lat = lax.axis_index("lat")
    y, core = lat // 2, lat % 2
    copy = pltpu.make_async_copy(leg_ref.at[pl.ds(block * STEP, STEP)], table, sem)
    copy.start()
    tile, off = shift_of(block, row_count * cols)
    lane = lax.broadcasted_iota(jnp.int32, (STEP, LANES), 1)
    held = ((lane - off) & (LANES - 1)) // row_count
    zero = jnp.zeros((STEP, LANES), jnp.bfloat16)
    parts = []
    for source in sources:
        for k in range(source.shape[0]):
            value = source[k, :, tile * LANES : (tile + 1) * LANES]
            if off + row_count * cols > LANES:
                value = jnp.where(
                    lane >= off, value, source[k, :, (tile + 1) * LANES : (tile + 2) * LANES]
                )
            parts.append(
                jnp.concatenate([jnp.where(held == c, value, zero) for c in range(cols)], axis=0)
            )
    both = jnp.dot(
        jnp.concatenate(parts, axis=1), place_ref[...], preferred_element_type=jnp.float32
    )
    north, south = both[:, :LANES], both[:, LANES:]
    even, odd = north + south, north - south
    far_coefs, near_coefs = jnp.where(y == 0, odd, even), jnp.where(y == 0, even, odd)
    copy.wait()
    multiply(far_coefs, table, pl.multiple_of((1 - y) * half, LANES), half, far)
    multiply(near_coefs, table, pl.multiple_of(y * half, LANES), half, near)
    pack(far, core, far_sent, far_own)
    pack(near, core, near_sent, near_own)


def final_kernel(base, degrees, cols, limits_ref, near_ref, far_ref, *refs):
    out = refs[-1]
    lat = lax.axis_index("lat")
    first = lat % 2 == 0
    half = degrees // 2
    width = out.shape[2]
    rows = STEP * cols
    value = near_ref[...] + far_ref[...].astype(jnp.float32)
    main0, main1 = value[:rows, :LANES], value[:rows, LANES:]
    tails = []
    for j in range(4):
        tail = value[rows:, (j // 2) * LANES : (j // 2 + 1) * LANES]
        tails.append(pltpu.roll(tail, LANES // 2, 1) if j % 2 else tail)
    tail = jnp.concatenate(tails, axis=0)
    lane_low = lax.broadcasted_iota(jnp.int32, (rows, LANES), 1) < LANES // 2
    turn0, turn1 = pltpu.roll(main0, LANES // 2, 1), pltpu.roll(main1, LANES // 2, 1)
    ordered = jnp.concatenate(
        [
            jnp.where(first, main0, jnp.where(lane_low, tail, turn0)),
            jnp.where(first, main1, jnp.where(lane_low, turn0, turn1)),
            jnp.where(first, tail, turn1),
        ],
        axis=1,
    )
    shape = (STEP, 3 * LANES)
    degree = lat * width + lax.broadcasted_iota(jnp.int32, shape, 1)
    offsets = jnp.where(degree < half, 2 * degree, 2 * (degree - half) + 1)
    limits = limits_ref[base : base + STEP, :]
    limits = jnp.concatenate([limits] * 3, axis=1)
    inside = offsets < limits
    for c in range(cols):
        out[c] = jnp.where(inside, ordered[c * STEP : (c + 1) * STEP], 0.0)[:, :width]


def packed(fourier, wave_table, legendre):
    slots, pairs, degrees = legendre.shape
    row_count, cols, waves = fourier.shape
    wave_count, lat_count = lax.axis_size("wave"), lax.axis_size("lat")
    width = degrees // lat_count
    used = row_count * cols
    params = pltpu.CompilerParams(vmem_limit_bytes=VMEM)
    whole = pl.BlockSpec(memory_space=pltpu.VMEM)
    anywhere = pl.BlockSpec(memory_space=pl.ANY)

    message = -(-(slots // STEP) * used // LANES) * LANES
    low = 2
    high = wave_count // low
    ordered = pl.pallas_call(
        functools.partial(gather_kernel, slots, low),
        out_shape=[jax.ShapeDtypeStruct((low, STEP, message), jnp.bfloat16)] * high,
        in_specs=[whole, whole],
        out_specs=[whole] * high,
        scratch_shapes=[pltpu.VMEM((slots * wave_count, LANES), jnp.float32)],
        compiler_params=params,
        name="gather",
    )(
        wave_table.reshape(-1, LANES),
        jnp.transpose(fourier, (1, 0, 2)).reshape(used, waves),
    )
    turns = [
        t * low + u
        for u in range(low)
        for side in (0, 1)
        for t in range(side * high // 2, (side + 1) * high // 2)
    ]
    place, limits = pl.pallas_call(
        functools.partial(place_kernel, turns, lat_count, row_count, pairs, degrees),
        out_shape=[
            jax.ShapeDtypeStruct((wave_count * LANES, 2 * LANES), jnp.bfloat16),
            jax.ShapeDtypeStruct((slots, LANES), jnp.int32),
        ],
        in_specs=[pl.BlockSpec(memory_space=pltpu.SMEM)],
        out_specs=[whole] * 2,
        compiler_params=params,
        name="place",
    )(wave_table)

    passed = [ordered[0]] + [
        lax.ppermute(ordered[t], "wave", [(w, w ^ t * low) for w in range(wave_count)])
        for t in range(1, high)
    ]
    sources = []
    for u in range(low):
        for side in (0, 1):
            block = jnp.stack([passed[t][u] for t in range(side * high // 2, (side + 1) * high // 2)])
            route = []
            for lat in range(lat_count):
                for wave in range(wave_count):
                    began = (wave >= wave_count // 2) != (side == 1)
                    to = lat_count - 1 - lat if began else lat
                    route.append((lat * wave_count + wave, to * wave_count + (wave ^ u)))
            sources.append(lax.ppermute(block, ("lat", "wave"), route))

    rows = STEP * cols
    shape = (rows + rows // 4, 2 * LANES)
    core_route = [(lat, lat ^ 1) for lat in range(lat_count)]
    y_route = [(lat, lat ^ 2) for lat in range(lat_count)]
    scratch = [
        pltpu.VMEM((STEP, pairs, degrees), jnp.bfloat16),
        pltpu.VMEM((rows, degrees // 2), jnp.float32),
        pltpu.VMEM((rows, degrees // 2), jnp.float32),
        pltpu.SemaphoreType.DMA,
    ]
    cost = pl.CostEstimate(flops=0, bytes_accessed=1024, transcendentals=0)
    pair_of_sums = [
        jax.ShapeDtypeStruct(shape, jnp.bfloat16),
        jax.ShapeDtypeStruct(shape, jnp.float32),
    ]
    count = slots // STEP

    def settle(sent, kept):
        return kept + lax.ppermute(sent, "lat", core_route).astype(jnp.float32)

    crossed, settled = [], []
    ties = []
    for block in range(count):
        sources, ties = lax.optimization_barrier((sources, ties))
        far_sent, far_own, near_sent, near_own = pl.pallas_call(
            functools.partial(product_kernel, block, row_count, cols),
            out_shape=pair_of_sums * 2,
            in_specs=[whole, anywhere] + [whole] * len(sources),
            out_specs=[whole] * 4,
            scratch_shapes=scratch,
            compiler_params=params,
            cost_estimate=cost,
            name="product",
        )(place, legendre, *sources)
        summed = settle(far_sent, far_own).astype(jnp.bfloat16)
        ties = [summed] + settled[-1:]
        crossed.append(lax.ppermute(summed, "lat", y_route))
        settled.append(settle(near_sent, near_own))

    out = None
    for block in range(count):
        carried = [] if out is None else [out]
        out = pl.pallas_call(
            functools.partial(final_kernel, block * STEP, degrees, cols),
            grid=(1,),
            in_specs=[whole] * 3 + [anywhere] * len(carried),
            out_specs=pl.BlockSpec((cols, STEP, width), lambda g, at=block: (0, at, 0)),
            out_shape=jax.ShapeDtypeStruct((cols, slots, width), jnp.float32),
            input_output_aliases={3: 0} if carried else {},
            compiler_params=params,
            cost_estimate=cost,
            name="final",
        )(limits, settled[block], crossed[block], *carried)
    return jnp.transpose(out, (1, 0, 2))


def local(fourier, wave_table, legendre):
    slots, pairs, degrees = legendre.shape
    row_count, cols, waves = fourier.shape
    wave_count, lat_count = lax.axis_size("wave"), lax.axis_size("lat")
    fits = (
        lat_count == 4
        and wave_count & (wave_count - 1) == 0
        and slots % STEP == 0
        and degrees // 2 == 5 * LANES
        and row_count & (row_count - 1) == 0
        and LANES // 4 % row_count == 0
        and row_count * cols % (LANES // 4) == 0
        and row_count * cols <= LANES
        and pairs == row_count * wave_count // 2
        and pairs * TILE == 2 * LANES
        and waves % (2 * LANES) == 0
    )
    if not fits:
        return plain(fourier, wave_table, legendre)
    return packed(fourier, wave_table, legendre)


def solution(mesh):
    in_specs = (P(("lat", "wave"), None, None), P(), P("wave", "lat", None))
    out_specs = P("wave", None, "lat")
    return jax.shard_map(local, mesh=mesh, in_specs=in_specs, out_specs=out_specs, check_vma=False)
```

```python
import functools

import jax
import jax.numpy as jnp
from jax import lax
from jax.experimental import pallas as pl
from jax.experimental.pallas import tpu as pltpu
from jax.sharding import PartitionSpec as P

LANES = 128
STEP = 32
TILE = 8
VMEM = 20 * 1024 * 1024


def partner(block, axis, stride):
    count = lax.axis_size(axis)
    route = []
    for low in range(count):
        high = low | 1 << stride
        if high != low and high < count:
            route += [(low, high), (high, low)]
    return lax.ppermute(block, axis, route)


def plain(fourier, wave_table, legendre):
    slot_count, pair_count, degree_count = legendre.shape
    lat_count = lax.axis_size("lat")
    half_degrees = degree_count // 2
    slice_width = degree_count // lat_count
    lat_index = lax.axis_index("lat")
    ordered = jnp.take(fourier, wave_table, axis=2)
    arrived = lax.all_to_all(ordered, "wave", split_axis=2, concat_axis=0, tiled=True)
    local_rows = jnp.transpose(arrived, (2, 1, 0))
    kept_rows = local_rows[:, :, :pair_count]
    received = local_rows[:, :, pair_count:]
    for bit_number in range(lat_count.bit_length() - 1):
        received = partner(received, "lat", bit_number)
    northern = lat_index < lat_count // 2
    north_rows = jnp.where(northern, kept_rows, received).astype(jnp.float32)
    south_rows = jnp.where(northern, jnp.flip(received, 2), jnp.flip(kept_rows, 2)).astype(
        jnp.float32
    )
    even_part = (north_rows + south_rows).astype(jnp.bfloat16)
    odd_part = (north_rows - south_rows).astype(jnp.bfloat16)
    my_waves = lax.dynamic_slice_in_dim(wave_table, lax.axis_index("wave") * slot_count, slot_count)
    even_out = jnp.einsum(
        "mcp,mpk->mck", even_part, legendre[:, :, :half_degrees], preferred_element_type=jnp.float32
    )
    odd_out = jnp.einsum(
        "mcp,mpk->mck", odd_part, legendre[:, :, half_degrees:], preferred_element_type=jnp.float32
    )
    partial_terms = jnp.concatenate([even_out, odd_out], axis=2)
    spectral = lax.psum_scatter(partial_terms, "lat", scatter_dimension=2, tiled=True)
    degree_slot = lat_index * slice_width + jnp.arange(slice_width, dtype=jnp.int32)
    offsets = jnp.where(
        degree_slot < half_degrees, 2 * degree_slot, 2 * (degree_slot - half_degrees) + 1
    )
    inside = offsets[None, None, :] < (degree_count - my_waves)[:, None, None]
    return jnp.where(inside, spectral, jnp.zeros_like(spectral))


def shift_of(block, used):
    return block * used // LANES, block * used % LANES


def gather_kernel(slots, low, table_ref, rows_ref, *refs):
    outs, turned = refs[:-1], refs[-1]
    me = lax.axis_index("wave")
    used, waves = rows_ref.shape
    rows = jnp.concatenate([rows_ref[...], jnp.zeros((LANES - used, waves), jnp.bfloat16)], axis=0)
    number = lax.broadcasted_iota(jnp.int32, (waves, LANES), 0)
    for j in range(0, table_ref.shape[0], 2):
        chosen = jnp.concatenate(
            [(number == table_ref[k : k + 1, :]).astype(jnp.bfloat16) for k in (j, j + 1)], axis=1
        )
        got = jnp.dot(rows, chosen, preferred_element_type=jnp.float32)
        turned[j * LANES : (j + 2) * LANES, :] = got.T
    lane = lax.broadcasted_iota(jnp.int32, (STEP, LANES), 1)
    for t, out in enumerate(outs):
        for u in range(low):
            begin = (me ^ (t * low + u)) * slots
            tiles = [jnp.zeros((STEP, LANES), jnp.float32)] * (out.shape[2] // LANES)
            for block in range(slots // STEP):
                tile, off = shift_of(block, used)
                value = turned[pl.ds(pl.multiple_of(begin + block * STEP, STEP), STEP), :]
                value = pltpu.roll(value, off, 1) if off else value
                tiles[tile] = jnp.where(lane >= off, value, tiles[tile])
                if off + used > LANES:
                    tiles[tile + 1] = jnp.where(lane < off + used - LANES, value, tiles[tile + 1])
            for k, tile in enumerate(tiles):
                out[u, :, k * LANES : (k + 1) * LANES] = tile.astype(jnp.bfloat16)


def place_kernel(turns, lat_count, row_count, pairs, degrees, table_ref, leg_ref, out, limits):
    northern = lax.axis_index("lat") < lat_count // 2
    me = lax.axis_index("wave")
    row = lax.broadcasted_iota(jnp.int32, (LANES, 2 * LANES), 0) & (row_count - 1)
    col = lax.broadcasted_iota(jnp.int32, (LANES, 2 * LANES), 1) & (pairs - 1 | LANES)
    half = len(turns) // 2
    for k, turn in enumerate(turns):
        source = me ^ turn
        ascending = (source < half) == northern
        position = (source % half) * row_count + row
        position = jnp.where(ascending, position, pairs - 1 - position)
        target = position + jnp.where(ascending, 0, LANES)
        out[k * LANES : (k + 1) * LANES, :] = (col == target).astype(jnp.bfloat16)
    slots = limits.shape[0]
    line = lax.broadcasted_iota(jnp.int32, (TILE, LANES), 0)
    for first in range(0, slots, TILE):
        value = jnp.zeros((TILE, LANES), jnp.int32)
        for s in range(TILE):
            value = jnp.where(line == s, degrees - table_ref[me * slots + first + s], value)
        limits[first : first + TILE, :] = value


def multiply(coefs, table, first, half, terms):
    pairs = table.shape[1]
    group = 2 * LANES // pairs
    cols = coefs.shape[0] // STEP
    shape = (cols * group, 2 * LANES)
    diagonal = (lax.broadcasted_iota(jnp.int32, shape, 0) & (group - 1)) == (
        lax.broadcasted_iota(jnp.int32, shape, 1) // pairs
    )
    blank = jnp.zeros(shape, jnp.bfloat16)
    for g in range(STEP // group):
        block = jnp.concatenate(
            [coefs[c * STEP + g * group : c * STEP + (g + 1) * group] for c in range(cols)], axis=0
        ).astype(jnp.bfloat16)
        block = jnp.where(diagonal, jnp.concatenate([block, block], axis=1), blank)
        weights = table[g * group : (g + 1) * group, :, pl.ds(first, half)]
        got = jnp.dot(
            block, weights.reshape(group * pairs, half), preferred_element_type=jnp.float32
        )
        for c in range(cols):
            terms[pl.ds(c * STEP + g * group, group), :] = got[c * group : (c + 1) * group]


def pack(terms, core, sent, kept):
    rows = terms.shape[0]
    part = rows // 4
    lane_low = lax.broadcasted_iota(jnp.int32, (part, LANES), 1) < LANES // 2
    for out, target in ((sent, 1 - core), (kept, core)):
        first = pl.multiple_of(target * 3 * LANES, LANES)
        out[:rows, :] = terms[:, pl.ds(first, 2 * LANES)].astype(out.dtype)
    for j in range(2):
        low = terms[pl.ds(2 * j * part, part), pl.ds(2 * LANES, LANES)]
        high = terms[pl.ds((2 * j + 1) * part, part), pl.ds(2 * LANES, LANES)]
        zeroth = jnp.where(lane_low, low, pltpu.roll(high, LANES // 2, 1))
        other = jnp.where(lane_low, pltpu.roll(low, LANES // 2, 1), high)
        for out, target in ((sent, 1 - core), (kept, core)):
            out[rows:, j * LANES : (j + 1) * LANES] = jnp.where(target == 0, zeroth, other).astype(
                out.dtype
            )


def product_kernel(block, row_count, cols, place_ref, leg_ref, *refs):
    sources = refs[:-6]
    far_sent, far_own, near_sent, near_own, far, near = refs[-6:]
    half = far.shape[1]
    table = leg_ref.at[block * STEP : (block + 1) * STEP]
    lat = lax.axis_index("lat")
    y, core = lat // 2, lat % 2
    tile, off = shift_of(block, row_count * cols)
    lane = lax.broadcasted_iota(jnp.int32, (STEP, LANES), 1)
    held = ((lane - off) & (LANES - 1)) // row_count
    zero = jnp.zeros((STEP, LANES), jnp.bfloat16)
    parts = []
    for source in sources:
        for k in range(source.shape[0]):
            value = source[k, :, tile * LANES : (tile + 1) * LANES]
            if off + row_count * cols > LANES:
                value = jnp.where(
                    lane >= off, value, source[k, :, (tile + 1) * LANES : (tile + 2) * LANES]
                )
            parts.append(
                jnp.concatenate([jnp.where(held == c, value, zero) for c in range(cols)], axis=0)
            )
    both = jnp.dot(
        jnp.concatenate(parts, axis=1), place_ref[...], preferred_element_type=jnp.float32
    )
    north, south = both[:, :LANES], both[:, LANES:]
    even, odd = north + south, north - south
    far_coefs, near_coefs = jnp.where(y == 0, odd, even), jnp.where(y == 0, even, odd)
    multiply(far_coefs, table, pl.multiple_of((1 - y) * half, LANES), half, far)
    multiply(near_coefs, table, pl.multiple_of(y * half, LANES), half, near)
    pack(far, core, far_sent, far_own)
    pack(near, core, near_sent, near_own)


def final_kernel(base, degrees, cols, limits_ref, near_ref, far_ref, *refs):
    out = refs[-1]
    lat = lax.axis_index("lat")
    first = lat % 2 == 0
    half = degrees // 2
    width = out.shape[2]
    rows = STEP * cols
    value = near_ref[...] + far_ref[...].astype(jnp.float32)
    main0, main1 = value[:rows, :LANES], value[:rows, LANES:]
    tails = []
    for j in range(4):
        tail = value[rows:, (j // 2) * LANES : (j // 2 + 1) * LANES]
        tails.append(pltpu.roll(tail, LANES // 2, 1) if j % 2 else tail)
    tail = jnp.concatenate(tails, axis=0)
    lane_low = lax.broadcasted_iota(jnp.int32, (rows, LANES), 1) < LANES // 2
    turn0, turn1 = pltpu.roll(main0, LANES // 2, 1), pltpu.roll(main1, LANES // 2, 1)
    ordered = jnp.concatenate(
        [
            jnp.where(first, main0, jnp.where(lane_low, tail, turn0)),
            jnp.where(first, main1, jnp.where(lane_low, turn0, turn1)),
            jnp.where(first, tail, turn1),
        ],
        axis=1,
    )
    shape = (STEP, 3 * LANES)
    degree = lat * width + lax.broadcasted_iota(jnp.int32, shape, 1)
    offsets = jnp.where(degree < half, 2 * degree, 2 * (degree - half) + 1)
    limits = limits_ref[base : base + STEP, :]
    limits = jnp.concatenate([limits] * 3, axis=1)
    inside = offsets < limits
    for c in range(cols):
        out[c] = jnp.where(inside, ordered[c * STEP : (c + 1) * STEP], 0.0)[:, :width]


def packed(fourier, wave_table, legendre):
    slots, pairs, degrees = legendre.shape
    row_count, cols, waves = fourier.shape
    wave_count, lat_count = lax.axis_size("wave"), lax.axis_size("lat")
    width = degrees // lat_count
    used = row_count * cols
    params = pltpu.CompilerParams(vmem_limit_bytes=VMEM)
    whole = pl.BlockSpec(memory_space=pltpu.VMEM)
    anywhere = pl.BlockSpec(memory_space=pl.ANY)

    message = -(-(slots // STEP) * used // LANES) * LANES
    low = 2
    high = wave_count // low
    ordered = pl.pallas_call(
        functools.partial(gather_kernel, slots, low),
        out_shape=[jax.ShapeDtypeStruct((low, STEP, message), jnp.bfloat16)] * high,
        in_specs=[whole, whole],
        out_specs=[whole] * high,
        scratch_shapes=[pltpu.VMEM((slots * wave_count, LANES), jnp.float32)],
        compiler_params=params,
        name="gather",
    )(
        wave_table.reshape(-1, LANES),
        jnp.transpose(fourier, (1, 0, 2)).reshape(used, waves),
    )
    turns = [
        t * low + u
        for u in range(low)
        for side in (0, 1)
        for t in range(side * high // 2, (side + 1) * high // 2)
    ]
    place, limits = pl.pallas_call(
        functools.partial(place_kernel, turns, lat_count, row_count, pairs, degrees),
        out_shape=[
            jax.ShapeDtypeStruct((wave_count * LANES, 2 * LANES), jnp.bfloat16),
            jax.ShapeDtypeStruct((slots, LANES), jnp.int32),
        ],
        in_specs=[pl.BlockSpec(memory_space=pltpu.SMEM), anywhere],
        out_specs=[whole] * 2,
        compiler_params=params,
        name="place",
    )(wave_table, legendre)

    passed = [ordered[0]] + [
        lax.ppermute(ordered[t], "wave", [(w, w ^ t * low) for w in range(wave_count)])
        for t in range(1, high)
    ]
    sources = []
    for u in range(low):
        for side in (0, 1):
            block = jnp.stack([passed[t][u] for t in range(side * high // 2, (side + 1) * high // 2)])
            route = []
            for lat in range(lat_count):
                for wave in range(wave_count):
                    began = (wave >= wave_count // 2) != (side == 1)
                    to = lat_count - 1 - lat if began else lat
                    route.append((lat * wave_count + wave, to * wave_count + (wave ^ u)))
            block, place = lax.optimization_barrier((block, place))
            sources.append(lax.ppermute(block, ("lat", "wave"), route))

    rows = STEP * cols
    shape = (rows + rows // 4, 2 * LANES)
    core_route = [(lat, lat ^ 1) for lat in range(lat_count)]
    y_route = [(lat, lat ^ 2) for lat in range(lat_count)]
    scratch = [
        pltpu.VMEM((rows, degrees // 2), jnp.float32),
        pltpu.VMEM((rows, degrees // 2), jnp.float32),
    ]
    cost = pl.CostEstimate(flops=0, bytes_accessed=1024, transcendentals=0)
    pair_of_sums = [
        jax.ShapeDtypeStruct(shape, jnp.bfloat16),
        jax.ShapeDtypeStruct(shape, jnp.float32),
    ]
    count = slots // STEP

    def settle(sent, kept):
        return kept + lax.ppermute(sent, "lat", core_route).astype(jnp.float32)

    crossed, settled = [], []
    ties = []
    for block in range(count):
        sources, ties = lax.optimization_barrier((sources, ties))
        far_sent, far_own, near_sent, near_own = pl.pallas_call(
            functools.partial(product_kernel, block, row_count, cols),
            out_shape=pair_of_sums * 2,
            in_specs=[whole] * (2 + len(sources)),
            out_specs=[whole] * 4,
            scratch_shapes=scratch,
            compiler_params=params,
            cost_estimate=cost,
            name="product",
        )(place, legendre, *sources)
        summed = settle(far_sent, far_own).astype(jnp.bfloat16)
        ties = [summed] + settled[-1:]
        crossed.append(lax.ppermute(summed, "lat", y_route))
        settled.append(settle(near_sent, near_own))

    out = None
    for block in range(count):
        carried = [] if out is None else [out]
        out = pl.pallas_call(
            functools.partial(final_kernel, block * STEP, degrees, cols),
            grid=(1,),
            in_specs=[whole] * 3 + [anywhere] * len(carried),
            out_specs=pl.BlockSpec((cols, STEP, width), lambda g, at=block: (0, at, 0)),
            out_shape=jax.ShapeDtypeStruct((cols, slots, width), jnp.float32),
            input_output_aliases={3: 0} if carried else {},
            compiler_params=params,
            cost_estimate=cost,
            name="final",
        )(limits, settled[block], crossed[block], *carried)
    return jnp.transpose(out, (1, 0, 2))


def local(fourier, wave_table, legendre):
    slots, pairs, degrees = legendre.shape
    row_count, cols, waves = fourier.shape
    wave_count, lat_count = lax.axis_size("wave"), lax.axis_size("lat")
    fits = (
        lat_count == 4
        and wave_count & (wave_count - 1) == 0
        and slots % STEP == 0
        and degrees // 2 == 5 * LANES
        and row_count & (row_count - 1) == 0
        and LANES // 4 % row_count == 0
        and row_count * cols % (LANES // 4) == 0
        and row_count * cols <= LANES
        and pairs == row_count * wave_count // 2
        and pairs * TILE == 2 * LANES
        and waves % (2 * LANES) == 0
    )
    if not fits:
        return plain(fourier, wave_table, legendre)
    return packed(fourier, wave_table, legendre)


def solution(mesh):
    in_specs = (P(("lat", "wave"), None, None), P(), P("wave", "lat", None))
    out_specs = P("wave", None, "lat")
    return jax.shard_map(local, mesh=mesh, in_specs=in_specs, out_specs=out_specs, check_vma=False)
```

```python
import functools

import jax
import jax.numpy as jnp
from jax import lax
from jax.experimental import pallas as pl
from jax.experimental.pallas import tpu as pltpu
from jax.sharding import PartitionSpec as P

LANES = 128
STEP = 32
TILE = 8
VMEM = 20 * 1024 * 1024


def partner(block, axis, stride):
    count = lax.axis_size(axis)
    route = []
    for low in range(count):
        high = low | 1 << stride
        if high != low and high < count:
            route += [(low, high), (high, low)]
    return lax.ppermute(block, axis, route)


def plain(fourier, wave_table, legendre):
    slot_count, pair_count, degree_count = legendre.shape
    lat_count = lax.axis_size("lat")
    half_degrees = degree_count // 2
    slice_width = degree_count // lat_count
    lat_index = lax.axis_index("lat")
    ordered = jnp.take(fourier, wave_table, axis=2)
    arrived = lax.all_to_all(ordered, "wave", split_axis=2, concat_axis=0, tiled=True)
    local_rows = jnp.transpose(arrived, (2, 1, 0))
    kept_rows = local_rows[:, :, :pair_count]
    received = local_rows[:, :, pair_count:]
    for bit_number in range(lat_count.bit_length() - 1):
        received = partner(received, "lat", bit_number)
    northern = lat_index < lat_count // 2
    north_rows = jnp.where(northern, kept_rows, received).astype(jnp.float32)
    south_rows = jnp.where(northern, jnp.flip(received, 2), jnp.flip(kept_rows, 2)).astype(
        jnp.float32
    )
    even_part = (north_rows + south_rows).astype(jnp.bfloat16)
    odd_part = (north_rows - south_rows).astype(jnp.bfloat16)
    my_waves = lax.dynamic_slice_in_dim(wave_table, lax.axis_index("wave") * slot_count, slot_count)
    even_out = jnp.einsum(
        "mcp,mpk->mck", even_part, legendre[:, :, :half_degrees], preferred_element_type=jnp.float32
    )
    odd_out = jnp.einsum(
        "mcp,mpk->mck", odd_part, legendre[:, :, half_degrees:], preferred_element_type=jnp.float32
    )
    partial_terms = jnp.concatenate([even_out, odd_out], axis=2)
    spectral = lax.psum_scatter(partial_terms, "lat", scatter_dimension=2, tiled=True)
    degree_slot = lat_index * slice_width + jnp.arange(slice_width, dtype=jnp.int32)
    offsets = jnp.where(
        degree_slot < half_degrees, 2 * degree_slot, 2 * (degree_slot - half_degrees) + 1
    )
    inside = offsets[None, None, :] < (degree_count - my_waves)[:, None, None]
    return jnp.where(inside, spectral, jnp.zeros_like(spectral))


def shift_of(block, used):
    return block * used // LANES, block * used % LANES


def gather_kernel(slots, table_ref, rows_ref, *refs):
    outs, turned = refs[:-1], refs[-1]
    me = lax.axis_index("wave")
    used, waves = rows_ref.shape
    rows = jnp.concatenate([rows_ref[...], jnp.zeros((LANES - used, waves), jnp.bfloat16)], axis=0)
    number = lax.broadcasted_iota(jnp.int32, (waves, LANES), 0)
    for j in range(0, table_ref.shape[0], 2):
        chosen = jnp.concatenate(
            [(number == table_ref[k : k + 1, :]).astype(jnp.bfloat16) for k in (j, j + 1)], axis=1
        )
        got = jnp.dot(rows, chosen, preferred_element_type=jnp.float32)
        turned[j * LANES : (j + 2) * LANES, :] = got.T
    lane = lax.broadcasted_iota(jnp.int32, (STEP, LANES), 1)
    for t, out in enumerate(outs):
        for u in range(out.shape[0]):
            begin = (me ^ (t * out.shape[0] + u)) * slots
            tiles = [jnp.zeros((STEP, LANES), jnp.float32)] * (out.shape[2] // LANES)
            for block in range(slots // STEP):
                tile, off = shift_of(block, used)
                value = turned[pl.ds(pl.multiple_of(begin + block * STEP, STEP), STEP), :]
                value = pltpu.roll(value, off, 1) if off else value
                tiles[tile] = jnp.where(lane >= off, value, tiles[tile])
                if off + used > LANES:
                    tiles[tile + 1] = jnp.where(lane < off + used - LANES, value, tiles[tile + 1])
            for k, tile in enumerate(tiles):
                out[u, :, k * LANES : (k + 1) * LANES] = tile.astype(jnp.bfloat16)


def place_kernel(turns, lat_count, row_count, pairs, degrees, table_ref, leg_ref, out, limits):
    northern = lax.axis_index("lat") < lat_count // 2
    me = lax.axis_index("wave")
    row = lax.broadcasted_iota(jnp.int32, (LANES, 2 * LANES), 0) & (row_count - 1)
    col = lax.broadcasted_iota(jnp.int32, (LANES, 2 * LANES), 1) & (pairs - 1 | LANES)
    half = len(turns) // 2
    for k, turn in enumerate(turns):
        source = me ^ turn
        ascending = (source < half) == northern
        position = (source % half) * row_count + row
        position = jnp.where(ascending, position, pairs - 1 - position)
        target = position + jnp.where(ascending, 0, LANES)
        out[k * LANES : (k + 1) * LANES, :] = (col == target).astype(jnp.bfloat16)
    slots = limits.shape[0]
    line = lax.broadcasted_iota(jnp.int32, (TILE, LANES), 0)
    for first in range(0, slots, TILE):
        value = jnp.zeros((TILE, LANES), jnp.int32)
        for s in range(TILE):
            value = jnp.where(line == s, degrees - table_ref[me * slots + first + s], value)
        limits[first : first + TILE, :] = value


def multiply(coefs, table, first, half, terms):
    pairs = table.shape[1]
    group = 2 * LANES // pairs
    cols = coefs.shape[0] // STEP
    shape = (cols * group, 2 * LANES)
    diagonal = (lax.broadcasted_iota(jnp.int32, shape, 0) & (group - 1)) == (
        lax.broadcasted_iota(jnp.int32, shape, 1) // pairs
    )
    blank = jnp.zeros(shape, jnp.bfloat16)
    for g in range(STEP // group):
        block = jnp.concatenate(
            [coefs[c * STEP + g * group : c * STEP + (g + 1) * group] for c in range(cols)], axis=0
        ).astype(jnp.bfloat16)
        block = jnp.where(diagonal, jnp.concatenate([block, block], axis=1), blank)
        weights = table[g * group : (g + 1) * group, :, pl.ds(first, half)]
        got = jnp.dot(
            block, weights.reshape(group * pairs, half), preferred_element_type=jnp.float32
        )
        for c in range(cols):
            terms[pl.ds(c * STEP + g * group, group), :] = got[c * group : (c + 1) * group]


def pack(terms, core, sent, kept):
    rows = terms.shape[0]
    part = rows // 4
    lane_low = lax.broadcasted_iota(jnp.int32, (part, LANES), 1) < LANES // 2
    for out, target in ((sent, 1 - core), (kept, core)):
        first = pl.multiple_of(target * 3 * LANES, LANES)
        out[:rows, :] = terms[:, pl.ds(first, 2 * LANES)].astype(out.dtype)
    for j in range(2):
        low = terms[pl.ds(2 * j * part, part), pl.ds(2 * LANES, LANES)]
        high = terms[pl.ds((2 * j + 1) * part, part), pl.ds(2 * LANES, LANES)]
        zeroth = jnp.where(lane_low, low, pltpu.roll(high, LANES // 2, 1))
        other = jnp.where(lane_low, pltpu.roll(low, LANES // 2, 1), high)
        for out, target in ((sent, 1 - core), (kept, core)):
            out[rows:, j * LANES : (j + 1) * LANES] = jnp.where(target == 0, zeroth, other).astype(
                out.dtype
            )


def product_kernel(block, row_count, cols, place_ref, leg_ref, *refs):
    sources = refs[:-6]
    far_sent, far_own, near_sent, near_own, far, near = refs[-6:]
    half = far.shape[1]
    table = leg_ref.at[block * STEP : (block + 1) * STEP]
    lat = lax.axis_index("lat")
    y, core = lat // 2, lat % 2
    tile, off = shift_of(block, row_count * cols)
    lane = lax.broadcasted_iota(jnp.int32, (STEP, LANES), 1)
    held = ((lane - off) & (LANES - 1)) // row_count
    zero = jnp.zeros((STEP, LANES), jnp.bfloat16)
    parts = []
    for source in sources:
        for k in range(source.shape[0]):
            value = source[k, :, tile * LANES : (tile + 1) * LANES]
            if off + row_count * cols > LANES:
                value = jnp.where(
                    lane >= off, value, source[k, :, (tile + 1) * LANES : (tile + 2) * LANES]
                )
            parts.append(
                jnp.concatenate([jnp.where(held == c, value, zero) for c in range(cols)], axis=0)
            )
    both = jnp.dot(
        jnp.concatenate(parts, axis=1), place_ref[...], preferred_element_type=jnp.float32
    )
    north, south = both[:, :LANES], both[:, LANES:]
    even, odd = north + south, north - south
    far_coefs, near_coefs = jnp.where(y == 0, odd, even), jnp.where(y == 0, even, odd)
    multiply(far_coefs, table, pl.multiple_of((1 - y) * half, LANES), half, far)
    multiply(near_coefs, table, pl.multiple_of(y * half, LANES), half, near)
    pack(far, core, far_sent, far_own)
    pack(near, core, near_sent, near_own)


def final_kernel(base, degrees, cols, limits_ref, near_ref, far_ref, *refs):
    out = refs[-1]
    lat = lax.axis_index("lat")
    first = lat % 2 == 0
    half = degrees // 2
    width = out.shape[2]
    rows = STEP * cols
    value = near_ref[...] + far_ref[...].astype(jnp.float32)
    main0, main1 = value[:rows, :LANES], value[:rows, LANES:]
    tails = []
    for j in range(4):
        tail = value[rows:, (j // 2) * LANES : (j // 2 + 1) * LANES]
        tails.append(pltpu.roll(tail, LANES // 2, 1) if j % 2 else tail)
    tail = jnp.concatenate(tails, axis=0)
    lane_low = lax.broadcasted_iota(jnp.int32, (rows, LANES), 1) < LANES // 2
    turn0, turn1 = pltpu.roll(main0, LANES // 2, 1), pltpu.roll(main1, LANES // 2, 1)
    ordered = jnp.concatenate(
        [
            jnp.where(first, main0, jnp.where(lane_low, tail, turn0)),
            jnp.where(first, main1, jnp.where(lane_low, turn0, turn1)),
            jnp.where(first, tail, turn1),
        ],
        axis=1,
    )
    shape = (STEP, 3 * LANES)
    degree = lat * width + lax.broadcasted_iota(jnp.int32, shape, 1)
    offsets = jnp.where(degree < half, 2 * degree, 2 * (degree - half) + 1)
    limits = limits_ref[base : base + STEP, :]
    limits = jnp.concatenate([limits] * 3, axis=1)
    inside = offsets < limits
    for c in range(cols):
        out[c] = jnp.where(inside, ordered[c * STEP : (c + 1) * STEP], 0.0)[:, :width]


def packed(fourier, wave_table, legendre):
    slots, pairs, degrees = legendre.shape
    row_count, cols, waves = fourier.shape
    wave_count, lat_count = lax.axis_size("wave"), lax.axis_size("lat")
    width = degrees // lat_count
    used = row_count * cols
    params = pltpu.CompilerParams(vmem_limit_bytes=VMEM)
    whole = pl.BlockSpec(memory_space=pltpu.VMEM)
    anywhere = pl.BlockSpec(memory_space=pl.ANY)

    message = -(-(slots // STEP) * used // LANES) * LANES
    upper = wave_count // 2
    ordered = pl.pallas_call(
        functools.partial(gather_kernel, slots),
        out_shape=[jax.ShapeDtypeStruct((upper, STEP, message), jnp.bfloat16)] * 2,
        in_specs=[whole, whole],
        out_specs=[whole] * 2,
        scratch_shapes=[pltpu.VMEM((slots * wave_count, LANES), jnp.float32)],
        compiler_params=params,
        name="gather",
    )(
        wave_table.reshape(-1, LANES),
        jnp.transpose(fourier, (1, 0, 2)).reshape(used, waves),
    )
    turns = [u + side * upper for u in range(upper) for side in (0, 1)]
    place, limits = pl.pallas_call(
        functools.partial(place_kernel, turns, lat_count, row_count, pairs, degrees),
        out_shape=[
            jax.ShapeDtypeStruct((wave_count * LANES, 2 * LANES), jnp.bfloat16),
            jax.ShapeDtypeStruct((slots, LANES), jnp.int32),
        ],
        in_specs=[pl.BlockSpec(memory_space=pltpu.SMEM), whole],
        out_specs=[whole] * 2,
        compiler_params=params,
        name="place",
    )(wave_table, legendre)

    passed = []
    for side in (0, 1):
        route = []
        for lat in range(lat_count):
            for wave in range(wave_count):
                to = lat if wave < upper else lat_count - 1 - lat
                route.append((lat * wave_count + wave, to * wave_count + (wave ^ side * upper)))
        passed.append(lax.ppermute(ordered[side], ("lat", "wave"), route))
    sources = []
    for u in range(upper):
        block = jnp.stack([passed[0][u], passed[1][u]])
        block, place = lax.optimization_barrier((block, place))
        if u:
            block = lax.ppermute(block, "wave", [(w, w ^ u) for w in range(wave_count)])
        sources.append(block)

    rows = STEP * cols
    shape = (rows + rows // 4, 2 * LANES)
    core_route = [(lat, lat ^ 1) for lat in range(lat_count)]
    y_route = [(lat, lat ^ 2) for lat in range(lat_count)]
    scratch = [
        pltpu.VMEM((rows, degrees // 2), jnp.float32),
        pltpu.VMEM((rows, degrees // 2), jnp.float32),
    ]
    cost = pl.CostEstimate(flops=0, bytes_accessed=1024, transcendentals=0)
    pair_of_sums = [
        jax.ShapeDtypeStruct(shape, jnp.bfloat16),
        jax.ShapeDtypeStruct(shape, jnp.float32),
    ]
    count = slots // STEP

    def settle(sent, kept):
        return kept + lax.ppermute(sent, "lat", core_route).astype(jnp.float32)

    crossed, settled = [], []
    ties = []
    for block in range(count):
        sources, ties = lax.optimization_barrier((sources, ties))
        far_sent, far_own, near_sent, near_own = pl.pallas_call(
            functools.partial(product_kernel, block, row_count, cols),
            out_shape=pair_of_sums * 2,
            in_specs=[whole] * (2 + len(sources)),
            out_specs=[whole] * 4,
            scratch_shapes=scratch,
            compiler_params=params,
            cost_estimate=cost,
            name="product",
        )(place, legendre, *sources)
        summed = settle(far_sent, far_own).astype(jnp.bfloat16)
        ties = [summed] + settled[-1:]
        crossed.append(lax.ppermute(summed, "lat", y_route))
        settled.append(settle(near_sent, near_own))

    out = None
    for block in range(count):
        carried = [] if out is None else [out]
        out = pl.pallas_call(
            functools.partial(final_kernel, block * STEP, degrees, cols),
            grid=(1,),
            in_specs=[whole] * 3 + [anywhere] * len(carried),
            out_specs=pl.BlockSpec((cols, STEP, width), lambda g, at=block: (0, at, 0)),
            out_shape=jax.ShapeDtypeStruct((cols, slots, width), jnp.float32),
            input_output_aliases={3: 0} if carried else {},
            compiler_params=params,
            cost_estimate=cost,
            name="final",
        )(limits, settled[block], crossed[block], *carried)
    return jnp.transpose(out, (1, 0, 2))


def local(fourier, wave_table, legendre):
    slots, pairs, degrees = legendre.shape
    row_count, cols, waves = fourier.shape
    wave_count, lat_count = lax.axis_size("wave"), lax.axis_size("lat")
    fits = (
        lat_count == 4
        and wave_count & (wave_count - 1) == 0
        and slots % STEP == 0
        and degrees // 2 == 5 * LANES
        and row_count & (row_count - 1) == 0
        and LANES // 4 % row_count == 0
        and row_count * cols % (LANES // 4) == 0
        and row_count * cols <= LANES
        and pairs == row_count * wave_count // 2
        and pairs * TILE == 2 * LANES
        and waves % (2 * LANES) == 0
    )
    if not fits:
        return plain(fourier, wave_table, legendre)
    return packed(fourier, wave_table, legendre)


def solution(mesh):
    in_specs = (P(("lat", "wave"), None, None), P(), P("wave", "lat", None))
    out_specs = P("wave", None, "lat")
    return jax.shard_map(local, mesh=mesh, in_specs=in_specs, out_specs=out_specs, check_vma=False)
```

```python
import functools

import jax
import jax.numpy as jnp
from jax import lax
from jax.experimental import pallas as pl
from jax.experimental.pallas import tpu as pltpu
from jax.sharding import PartitionSpec as P

LANES = 128
STEP = 32
TILE = 8
VMEM = 32 * 1024 * 1024


def partner(block, axis, stride):
    count = lax.axis_size(axis)
    route = []
    for low in range(count):
        high = low | 1 << stride
        if high != low and high < count:
            route += [(low, high), (high, low)]
    return lax.ppermute(block, axis, route)


def plain(fourier, wave_table, legendre):
    slot_count, pair_count, degree_count = legendre.shape
    lat_count = lax.axis_size("lat")
    half_degrees = degree_count // 2
    slice_width = degree_count // lat_count
    lat_index = lax.axis_index("lat")
    ordered = jnp.take(fourier, wave_table, axis=2)
    arrived = lax.all_to_all(ordered, "wave", split_axis=2, concat_axis=0, tiled=True)
    local_rows = jnp.transpose(arrived, (2, 1, 0))
    kept_rows = local_rows[:, :, :pair_count]
    received = local_rows[:, :, pair_count:]
    for bit_number in range(lat_count.bit_length() - 1):
        received = partner(received, "lat", bit_number)
    northern = lat_index < lat_count // 2
    north_rows = jnp.where(northern, kept_rows, received).astype(jnp.float32)
    south_rows = jnp.where(northern, jnp.flip(received, 2), jnp.flip(kept_rows, 2)).astype(
        jnp.float32
    )
    even_part = (north_rows + south_rows).astype(jnp.bfloat16)
    odd_part = (north_rows - south_rows).astype(jnp.bfloat16)
    my_waves = lax.dynamic_slice_in_dim(wave_table, lax.axis_index("wave") * slot_count, slot_count)
    even_out = jnp.einsum(
        "mcp,mpk->mck", even_part, legendre[:, :, :half_degrees], preferred_element_type=jnp.float32
    )
    odd_out = jnp.einsum(
        "mcp,mpk->mck", odd_part, legendre[:, :, half_degrees:], preferred_element_type=jnp.float32
    )
    partial_terms = jnp.concatenate([even_out, odd_out], axis=2)
    spectral = lax.psum_scatter(partial_terms, "lat", scatter_dimension=2, tiled=True)
    degree_slot = lat_index * slice_width + jnp.arange(slice_width, dtype=jnp.int32)
    offsets = jnp.where(
        degree_slot < half_degrees, 2 * degree_slot, 2 * (degree_slot - half_degrees) + 1
    )
    inside = offsets[None, None, :] < (degree_count - my_waves)[:, None, None]
    return jnp.where(inside, spectral, jnp.zeros_like(spectral))


def shift_of(block, used):
    return block * used // LANES, block * used % LANES


def gather_kernel(slots, low, table_ref, rows_ref, *refs):
    outs, turned = refs[:-1], refs[-1]
    me = lax.axis_index("wave")
    used, waves = rows_ref.shape
    rows = jnp.concatenate([rows_ref[...], jnp.zeros((LANES - used, waves), jnp.bfloat16)], axis=0)
    number = lax.broadcasted_iota(jnp.int32, (waves, LANES), 0)
    for j in range(0, table_ref.shape[0], 2):
        chosen = jnp.concatenate(
            [(number == table_ref[k : k + 1, :]).astype(jnp.bfloat16) for k in (j, j + 1)], axis=1
        )
        got = jnp.dot(rows, chosen, preferred_element_type=jnp.float32)
        turned[j * LANES : (j + 2) * LANES, :] = got.T
    lane = lax.broadcasted_iota(jnp.int32, (STEP, LANES), 1)
    for t, out in enumerate(outs):
        for u in range(low):
            begin = (me ^ (t * low + u)) * slots
            tiles = [jnp.zeros((STEP, LANES), jnp.float32)] * (out.shape[2] // LANES)
            for block in range(slots // STEP):
                tile, off = shift_of(block, used)
                value = turned[pl.ds(pl.multiple_of(begin + block * STEP, STEP), STEP), :]
                value = pltpu.roll(value, off, 1) if off else value
                tiles[tile] = jnp.where(lane >= off, value, tiles[tile])
                if off + used > LANES:
                    tiles[tile + 1] = jnp.where(lane < off + used - LANES, value, tiles[tile + 1])
            for k, tile in enumerate(tiles):
                out[u, :, k * LANES : (k + 1) * LANES] = tile.astype(jnp.bfloat16)


def place_kernel(turns, lat_count, row_count, pairs, degrees, table_ref, out, limits):
    northern = lax.axis_index("lat") < lat_count // 2
    me = lax.axis_index("wave")
    row = lax.broadcasted_iota(jnp.int32, (LANES, 2 * LANES), 0) & (row_count - 1)
    col = lax.broadcasted_iota(jnp.int32, (LANES, 2 * LANES), 1) & (pairs - 1 | LANES)
    half = len(turns) // 2
    for k, turn in enumerate(turns):
        source = me ^ turn
        ascending = (source < half) == northern
        position = (source % half) * row_count + row
        position = jnp.where(ascending, position, pairs - 1 - position)
        target = position + jnp.where(ascending, 0, LANES)
        out[k * LANES : (k + 1) * LANES, :] = (col == target).astype(jnp.bfloat16)
    slots = limits.shape[0]
    line = lax.broadcasted_iota(jnp.int32, (TILE, LANES), 0)
    for first in range(0, slots, TILE):
        value = jnp.zeros((TILE, LANES), jnp.int32)
        for s in range(TILE):
            value = jnp.where(line == s, degrees - table_ref[me * slots + first + s], value)
        limits[first : first + TILE, :] = value


def multiply(coefs, table, first, half, terms):
    pairs = table.shape[1]
    group = 2 * LANES // pairs
    cols = coefs.shape[0] // STEP
    shape = (cols * group, 2 * LANES)
    diagonal = (lax.broadcasted_iota(jnp.int32, shape, 0) & (group - 1)) == (
        lax.broadcasted_iota(jnp.int32, shape, 1) // pairs
    )
    blank = jnp.zeros(shape, jnp.bfloat16)
    for g in range(STEP // group):
        block = jnp.concatenate(
            [coefs[c * STEP + g * group : c * STEP + (g + 1) * group] for c in range(cols)], axis=0
        ).astype(jnp.bfloat16)
        block = jnp.where(diagonal, jnp.concatenate([block, block], axis=1), blank)
        weights = table[g * group : (g + 1) * group, :, pl.ds(first, half)]
        got = jnp.dot(
            block, weights.reshape(group * pairs, half), preferred_element_type=jnp.float32
        )
        for c in range(cols):
            terms[pl.ds(c * STEP + g * group, group), :] = got[c * group : (c + 1) * group]


def pack(terms, core, sent, kept):
    rows = terms.shape[0]
    part = rows // 4
    lane_low = lax.broadcasted_iota(jnp.int32, (part, LANES), 1) < LANES // 2
    for out, target in ((sent, 1 - core), (kept, core)):
        first = pl.multiple_of(target * 3 * LANES, LANES)
        out[:rows, :] = terms[:, pl.ds(first, 2 * LANES)].astype(out.dtype)
    for j in range(2):
        low = terms[pl.ds(2 * j * part, part), pl.ds(2 * LANES, LANES)]
        high = terms[pl.ds((2 * j + 1) * part, part), pl.ds(2 * LANES, LANES)]
        zeroth = jnp.where(lane_low, low, pltpu.roll(high, LANES // 2, 1))
        other = jnp.where(lane_low, pltpu.roll(low, LANES // 2, 1), high)
        for out, target in ((sent, 1 - core), (kept, core)):
            out[rows:, j * LANES : (j + 1) * LANES] = jnp.where(target == 0, zeroth, other).astype(
                out.dtype
            )


def product_kernel(block, row_count, cols, place_ref, leg_ref, *refs):
    sources = refs[:-6]
    far_sent, far_own, near_sent, near_own, far, near = refs[-6:]
    half = far.shape[1]
    lat = lax.axis_index("lat")
    y, core = lat // 2, lat % 2
    tile, off = shift_of(block, row_count * cols)
    lane = lax.broadcasted_iota(jnp.int32, (STEP, LANES), 1)
    held = ((lane - off) & (LANES - 1)) // row_count
    zero = jnp.zeros((STEP, LANES), jnp.bfloat16)
    parts = []
    for source in sources:
        for k in range(source.shape[0]):
            value = source[k, :, tile * LANES : (tile + 1) * LANES]
            if off + row_count * cols > LANES:
                value = jnp.where(
                    lane >= off, value, source[k, :, (tile + 1) * LANES : (tile + 2) * LANES]
                )
            parts.append(
                jnp.concatenate([jnp.where(held == c, value, zero) for c in range(cols)], axis=0)
            )
    both = jnp.dot(
        jnp.concatenate(parts, axis=1), place_ref[...], preferred_element_type=jnp.float32
    )
    north, south = both[:, :LANES], both[:, LANES:]
    even, odd = north + south, north - south
    far_coefs, near_coefs = jnp.where(y == 0, odd, even), jnp.where(y == 0, even, odd)
    multiply(far_coefs, leg_ref, pl.multiple_of((1 - y) * half, LANES), half, far)
    multiply(near_coefs, leg_ref, pl.multiple_of(y * half, LANES), half, near)
    pack(far, core, far_sent, far_own)
    pack(near, core, near_sent, near_own)


def final_kernel(base, degrees, cols, limits_ref, near_ref, far_ref, *refs):
    out = refs[-1]
    lat = lax.axis_index("lat")
    first = lat % 2 == 0
    half = degrees // 2
    width = out.shape[2]
    rows = STEP * cols
    value = near_ref[...] + far_ref[...].astype(jnp.float32)
    main0, main1 = value[:rows, :LANES], value[:rows, LANES:]
    tails = []
    for j in range(4):
        tail = value[rows:, (j // 2) * LANES : (j // 2 + 1) * LANES]
        tails.append(pltpu.roll(tail, LANES // 2, 1) if j % 2 else tail)
    tail = jnp.concatenate(tails, axis=0)
    lane_low = lax.broadcasted_iota(jnp.int32, (rows, LANES), 1) < LANES // 2
    turn0, turn1 = pltpu.roll(main0, LANES // 2, 1), pltpu.roll(main1, LANES // 2, 1)
    ordered = jnp.concatenate(
        [
            jnp.where(first, main0, jnp.where(lane_low, tail, turn0)),
            jnp.where(first, main1, jnp.where(lane_low, turn0, turn1)),
            jnp.where(first, tail, turn1),
        ],
        axis=1,
    )
    shape = (STEP, 3 * LANES)
    degree = lat * width + lax.broadcasted_iota(jnp.int32, shape, 1)
    offsets = jnp.where(degree < half, 2 * degree, 2 * (degree - half) + 1)
    limits = limits_ref[base : base + STEP, :]
    limits = jnp.concatenate([limits] * 3, axis=1)
    inside = offsets < limits
    for c in range(cols):
        out[c] = jnp.where(inside, ordered[c * STEP : (c + 1) * STEP], 0.0)[:, :width]


def packed(fourier, wave_table, legendre):
    slots, pairs, degrees = legendre.shape
    row_count, cols, waves = fourier.shape
    wave_count, lat_count = lax.axis_size("wave"), lax.axis_size("lat")
    width = degrees // lat_count
    used = row_count * cols
    params = pltpu.CompilerParams(vmem_limit_bytes=VMEM)
    whole = pl.BlockSpec(memory_space=pltpu.VMEM)
    anywhere = pl.BlockSpec(memory_space=pl.ANY)

    message = -(-(slots // STEP) * used // LANES) * LANES
    low = 2
    high = wave_count // low
    ordered = pl.pallas_call(
        functools.partial(gather_kernel, slots, low),
        out_shape=[jax.ShapeDtypeStruct((low, STEP, message), jnp.bfloat16)] * high,
        in_specs=[whole, whole],
        out_specs=[whole] * high,
        scratch_shapes=[pltpu.VMEM((slots * wave_count, LANES), jnp.float32)],
        compiler_params=params,
        name="gather",
    )(
        wave_table.reshape(-1, LANES),
        jnp.transpose(fourier, (1, 0, 2)).reshape(used, waves),
    )
    turns = [
        t * low + u
        for u in range(low)
        for side in (0, 1)
        for t in range(side * high // 2, (side + 1) * high // 2)
    ]
    place, limits = pl.pallas_call(
        functools.partial(place_kernel, turns, lat_count, row_count, pairs, degrees),
        out_shape=[
            jax.ShapeDtypeStruct((wave_count * LANES, 2 * LANES), jnp.bfloat16),
            jax.ShapeDtypeStruct((slots, LANES), jnp.int32),
        ],
        in_specs=[pl.BlockSpec(memory_space=pltpu.SMEM)],
        out_specs=[whole] * 2,
        compiler_params=params,
        name="place",
    )(wave_table)

    passed = [ordered[0]] + [
        lax.ppermute(ordered[t], "wave", [(w, w ^ t * low) for w in range(wave_count)])
        for t in range(1, high)
    ]
    count = slots // STEP
    early = count - count // 2
    tables = [legendre[block * STEP : (block + 1) * STEP] for block in range(early)]
    sources = []
    for u in range(low):
        for side in (0, 1):
            block = jnp.stack([passed[t][u] for t in range(side * high // 2, (side + 1) * high // 2)])
            route = []
            for lat in range(lat_count):
                for wave in range(wave_count):
                    began = (wave >= wave_count // 2) != (side == 1)
                    to = lat_count - 1 - lat if began else lat
                    route.append((lat * wave_count + wave, to * wave_count + (wave ^ u)))
            block, tables = lax.optimization_barrier((block, tables))
            if side == 0 and u == 0:
                later, block = lax.optimization_barrier((legendre, block))
            sources.append(lax.ppermute(block, ("lat", "wave"), route))

    tables += [later[block * STEP : (block + 1) * STEP] for block in range(early, count)]
    sources, tables = lax.optimization_barrier((sources, tables))

    rows = STEP * cols
    shape = (rows + rows // 4, 2 * LANES)
    core_route = [(lat, lat ^ 1) for lat in range(lat_count)]
    y_route = [(lat, lat ^ 2) for lat in range(lat_count)]
    scratch = [
        pltpu.VMEM((rows, degrees // 2), jnp.float32),
        pltpu.VMEM((rows, degrees // 2), jnp.float32),
    ]
    cost = pl.CostEstimate(flops=0, bytes_accessed=1024, transcendentals=0)
    pair_of_sums = [
        jax.ShapeDtypeStruct(shape, jnp.bfloat16),
        jax.ShapeDtypeStruct(shape, jnp.float32),
    ]
    def settle(sent, kept):
        return kept + lax.ppermute(sent, "lat", core_route).astype(jnp.float32)

    crossed, settled = [], []
    ties = []
    for block in range(count):
        sources, ties = lax.optimization_barrier((sources, ties))
        far_sent, far_own, near_sent, near_own = pl.pallas_call(
            functools.partial(product_kernel, block, row_count, cols),
            out_shape=pair_of_sums * 2,
            in_specs=[whole] * (2 + len(sources)),
            out_specs=[whole] * 4,
            scratch_shapes=scratch,
            compiler_params=params,
            cost_estimate=cost,
            name="product",
        )(place, tables[block], *sources)
        summed = settle(far_sent, far_own).astype(jnp.bfloat16)
        ties = [summed] + settled[-1:]
        crossed.append(lax.ppermute(summed, "lat", y_route))
        settled.append(settle(near_sent, near_own))

    out = None
    for block in range(count):
        carried = [] if out is None else [out]
        out = pl.pallas_call(
            functools.partial(final_kernel, block * STEP, degrees, cols),
            grid=(1,),
            in_specs=[whole] * 3 + [anywhere] * len(carried),
            out_specs=pl.BlockSpec((cols, STEP, width), lambda g, at=block: (0, at, 0)),
            out_shape=jax.ShapeDtypeStruct((cols, slots, width), jnp.float32),
            input_output_aliases={3: 0} if carried else {},
            compiler_params=params,
            cost_estimate=cost,
            name="final",
        )(limits, settled[block], crossed[block], *carried)
    return jnp.transpose(out, (1, 0, 2))


def local(fourier, wave_table, legendre):
    slots, pairs, degrees = legendre.shape
    row_count, cols, waves = fourier.shape
    wave_count, lat_count = lax.axis_size("wave"), lax.axis_size("lat")
    fits = (
        lat_count == 4
        and wave_count & (wave_count - 1) == 0
        and slots % STEP == 0
        and degrees // 2 == 5 * LANES
        and row_count & (row_count - 1) == 0
        and LANES // 4 % row_count == 0
        and row_count * cols % (LANES // 4) == 0
        and row_count * cols <= LANES
        and pairs == row_count * wave_count // 2
        and pairs * TILE == 2 * LANES
        and waves % (2 * LANES) == 0
    )
    if not fits:
        return plain(fourier, wave_table, legendre)
    return packed(fourier, wave_table, legendre)


def solution(mesh):
    in_specs = (P(("lat", "wave"), None, None), P(), P("wave", "lat", None))
    out_specs = P("wave", None, "lat")
    return jax.shard_map(local, mesh=mesh, in_specs=in_specs, out_specs=out_specs, check_vma=False)
```

```python
import functools

import jax
import jax.numpy as jnp
from jax import lax
from jax.experimental import pallas as pl
from jax.experimental.pallas import tpu as pltpu
from jax.sharding import PartitionSpec as P

LANES = 128
STEP = 32
TILE = 8
VMEM = 20 * 1024 * 1024


def partner(block, axis, stride):
    count = lax.axis_size(axis)
    route = []
    for low in range(count):
        high = low | 1 << stride
        if high != low and high < count:
            route += [(low, high), (high, low)]
    return lax.ppermute(block, axis, route)


def plain(fourier, wave_table, legendre):
    slot_count, pair_count, degree_count = legendre.shape
    lat_count = lax.axis_size("lat")
    half_degrees = degree_count // 2
    slice_width = degree_count // lat_count
    lat_index = lax.axis_index("lat")
    ordered = jnp.take(fourier, wave_table, axis=2)
    arrived = lax.all_to_all(ordered, "wave", split_axis=2, concat_axis=0, tiled=True)
    local_rows = jnp.transpose(arrived, (2, 1, 0))
    kept_rows = local_rows[:, :, :pair_count]
    received = local_rows[:, :, pair_count:]
    for bit_number in range(lat_count.bit_length() - 1):
        received = partner(received, "lat", bit_number)
    northern = lat_index < lat_count // 2
    north_rows = jnp.where(northern, kept_rows, received).astype(jnp.float32)
    south_rows = jnp.where(northern, jnp.flip(received, 2), jnp.flip(kept_rows, 2)).astype(
        jnp.float32
    )
    even_part = (north_rows + south_rows).astype(jnp.bfloat16)
    odd_part = (north_rows - south_rows).astype(jnp.bfloat16)
    my_waves = lax.dynamic_slice_in_dim(wave_table, lax.axis_index("wave") * slot_count, slot_count)
    even_out = jnp.einsum(
        "mcp,mpk->mck", even_part, legendre[:, :, :half_degrees], preferred_element_type=jnp.float32
    )
    odd_out = jnp.einsum(
        "mcp,mpk->mck", odd_part, legendre[:, :, half_degrees:], preferred_element_type=jnp.float32
    )
    partial_terms = jnp.concatenate([even_out, odd_out], axis=2)
    spectral = lax.psum_scatter(partial_terms, "lat", scatter_dimension=2, tiled=True)
    degree_slot = lat_index * slice_width + jnp.arange(slice_width, dtype=jnp.int32)
    offsets = jnp.where(
        degree_slot < half_degrees, 2 * degree_slot, 2 * (degree_slot - half_degrees) + 1
    )
    inside = offsets[None, None, :] < (degree_count - my_waves)[:, None, None]
    return jnp.where(inside, spectral, jnp.zeros_like(spectral))


def shift_of(block, used):
    return block * used // LANES, block * used % LANES


def gather_kernel(slots, low, table_ref, rows_ref, *refs):
    outs, turned = refs[:-1], refs[-1]
    me = lax.axis_index("wave")
    used, waves = rows_ref.shape
    rows = jnp.concatenate([rows_ref[...], jnp.zeros((LANES - used, waves), jnp.bfloat16)], axis=0)
    number = lax.broadcasted_iota(jnp.int32, (waves, LANES), 0)
    for j in range(0, table_ref.shape[0], 2):
        chosen = jnp.concatenate(
            [(number == table_ref[k : k + 1, :]).astype(jnp.bfloat16) for k in (j, j + 1)], axis=1
        )
        got = jnp.dot(rows, chosen, preferred_element_type=jnp.float32)
        turned[j * LANES : (j + 2) * LANES, :] = got.T
    lane = lax.broadcasted_iota(jnp.int32, (STEP, LANES), 1)
    for t, out in enumerate(outs):
        for u in range(low):
            begin = (me ^ (t * low + u)) * slots
            tiles = [jnp.zeros((STEP, LANES), jnp.float32)] * (out.shape[2] // LANES)
            for block in range(slots // STEP):
                tile, off = shift_of(block, used)
                value = turned[pl.ds(pl.multiple_of(begin + block * STEP, STEP), STEP), :]
                value = pltpu.roll(value, off, 1) if off else value
                tiles[tile] = jnp.where(lane >= off, value, tiles[tile])
                if off + used > LANES:
                    tiles[tile + 1] = jnp.where(lane < off + used - LANES, value, tiles[tile + 1])
            for k, tile in enumerate(tiles):
                out[u, :, k * LANES : (k + 1) * LANES] = tile.astype(jnp.bfloat16)


def touch_kernel(leg_ref, out):
    out[...] = leg_ref[0, : out.shape[0], : out.shape[1]]


def place_kernel(turns, lat_count, row_count, pairs, degrees, table_ref, token_ref, out, limits):
    northern = lax.axis_index("lat") < lat_count // 2
    me = lax.axis_index("wave")
    row = lax.broadcasted_iota(jnp.int32, (LANES, 2 * LANES), 0) & (row_count - 1)
    col = lax.broadcasted_iota(jnp.int32, (LANES, 2 * LANES), 1) & (pairs - 1 | LANES)
    half = len(turns)
    for k in range(2 * half):
        ascending = northern if k < half else jnp.logical_not(northern)
        position = ((me ^ turns[k % half]) % half) * row_count + row
        position = jnp.where(ascending, position, pairs - 1 - position)
        target = position + jnp.where(ascending, 0, LANES)
        out[k * LANES : (k + 1) * LANES, :] = (col == target).astype(jnp.bfloat16)
    slots = limits.shape[0]
    line = lax.broadcasted_iota(jnp.int32, (TILE, LANES), 0)
    for first in range(0, slots, TILE):
        value = jnp.zeros((TILE, LANES), jnp.int32)
        for s in range(TILE):
            value = jnp.where(line == s, degrees - table_ref[me * slots + first + s], value)
        limits[first : first + TILE, :] = value


def multiply(coefs, table, first, half, terms):
    pairs = table.shape[1]
    group = 2 * LANES // pairs
    cols = coefs.shape[0] // STEP
    shape = (cols * group, 2 * LANES)
    diagonal = (lax.broadcasted_iota(jnp.int32, shape, 0) & (group - 1)) == (
        lax.broadcasted_iota(jnp.int32, shape, 1) // pairs
    )
    blank = jnp.zeros(shape, jnp.bfloat16)
    for g in range(STEP // group):
        block = jnp.concatenate(
            [coefs[c * STEP + g * group : c * STEP + (g + 1) * group] for c in range(cols)], axis=0
        ).astype(jnp.bfloat16)
        block = jnp.where(diagonal, jnp.concatenate([block, block], axis=1), blank)
        weights = table[g * group : (g + 1) * group, :, pl.ds(first, half)]
        got = jnp.dot(
            block, weights.reshape(group * pairs, half), preferred_element_type=jnp.float32
        )
        for c in range(cols):
            terms[pl.ds(c * STEP + g * group, group), :] = got[c * group : (c + 1) * group]


def pack(terms, core, sent, kept):
    rows = terms.shape[0]
    part = rows // 4
    lane_low = lax.broadcasted_iota(jnp.int32, (part, LANES), 1) < LANES // 2
    for out, target in ((sent, 1 - core), (kept, core)):
        first = pl.multiple_of(target * 3 * LANES, LANES)
        out[:rows, :] = terms[:, pl.ds(first, 2 * LANES)].astype(out.dtype)
    for j in range(2):
        low = terms[pl.ds(2 * j * part, part), pl.ds(2 * LANES, LANES)]
        high = terms[pl.ds((2 * j + 1) * part, part), pl.ds(2 * LANES, LANES)]
        zeroth = jnp.where(lane_low, low, pltpu.roll(high, LANES // 2, 1))
        other = jnp.where(lane_low, pltpu.roll(low, LANES // 2, 1), high)
        for out, target in ((sent, 1 - core), (kept, core)):
            out[rows:, j * LANES : (j + 1) * LANES] = jnp.where(target == 0, zeroth, other).astype(
                out.dtype
            )


def product_kernel(block, row_count, cols, place_ref, leg_ref, *refs):
    sources = refs[:-6]
    far_sent, far_own, near_sent, near_own, far, near = refs[-6:]
    half = far.shape[1]
    table = leg_ref.at[block * STEP : (block + 1) * STEP]
    lat = lax.axis_index("lat")
    y, core = lat // 2, lat % 2
    tile, off = shift_of(block, row_count * cols)
    lane = lax.broadcasted_iota(jnp.int32, (STEP, LANES), 1)
    held = ((lane - off) & (LANES - 1)) // row_count
    zero = jnp.zeros((STEP, LANES), jnp.bfloat16)
    parts = []
    for source in sources:
        for k in range(source.shape[0]):
            value = source[k, :, tile * LANES : (tile + 1) * LANES]
            if off + row_count * cols > LANES:
                value = jnp.where(
                    lane >= off, value, source[k, :, (tile + 1) * LANES : (tile + 2) * LANES]
                )
            parts.append(
                jnp.concatenate([jnp.where(held == c, value, zero) for c in range(cols)], axis=0)
            )
    both = jnp.dot(
        jnp.concatenate(parts, axis=1), place_ref[...], preferred_element_type=jnp.float32
    )
    north, south = both[:, :LANES], both[:, LANES:]
    even, odd = north + south, north - south
    far_coefs, near_coefs = jnp.where(y == 0, odd, even), jnp.where(y == 0, even, odd)
    multiply(far_coefs, table, pl.multiple_of((1 - y) * half, LANES), half, far)
    multiply(near_coefs, table, pl.multiple_of(y * half, LANES), half, near)
    pack(far, core, far_sent, far_own)
    pack(near, core, near_sent, near_own)


def final_kernel(base, degrees, cols, limits_ref, near_ref, far_ref, *refs):
    out = refs[-1]
    lat = lax.axis_index("lat")
    first = lat % 2 == 0
    half = degrees // 2
    width = out.shape[2]
    rows = STEP * cols
    value = near_ref[...] + far_ref[...].astype(jnp.float32)
    main0, main1 = value[:rows, :LANES], value[:rows, LANES:]
    tails = []
    for j in range(4):
        tail = value[rows:, (j // 2) * LANES : (j // 2 + 1) * LANES]
        tails.append(pltpu.roll(tail, LANES // 2, 1) if j % 2 else tail)
    tail = jnp.concatenate(tails, axis=0)
    lane_low = lax.broadcasted_iota(jnp.int32, (rows, LANES), 1) < LANES // 2
    turn0, turn1 = pltpu.roll(main0, LANES // 2, 1), pltpu.roll(main1, LANES // 2, 1)
    ordered = jnp.concatenate(
        [
            jnp.where(first, main0, jnp.where(lane_low, tail, turn0)),
            jnp.where(first, main1, jnp.where(lane_low, turn0, turn1)),
            jnp.where(first, tail, turn1),
        ],
        axis=1,
    )
    shape = (STEP, 3 * LANES)
    degree = lat * width + lax.broadcasted_iota(jnp.int32, shape, 1)
    offsets = jnp.where(degree < half, 2 * degree, 2 * (degree - half) + 1)
    limits = limits_ref[base : base + STEP, :]
    limits = jnp.concatenate([limits] * 3, axis=1)
    inside = offsets < limits
    for c in range(cols):
        out[c] = jnp.where(inside, ordered[c * STEP : (c + 1) * STEP], 0.0)[:, :width]


def packed(fourier, wave_table, legendre):
    slots, pairs, degrees = legendre.shape
    row_count, cols, waves = fourier.shape
    wave_count, lat_count = lax.axis_size("wave"), lax.axis_size("lat")
    width = degrees // lat_count
    used = row_count * cols
    params = pltpu.CompilerParams(vmem_limit_bytes=VMEM)
    whole = pl.BlockSpec(memory_space=pltpu.VMEM)
    anywhere = pl.BlockSpec(memory_space=pl.ANY)

    message = -(-(slots // STEP) * used // LANES) * LANES
    low = 2
    high = wave_count // low
    ordered = pl.pallas_call(
        functools.partial(gather_kernel, slots, low),
        out_shape=[jax.ShapeDtypeStruct((low, STEP, message), jnp.bfloat16)] * high,
        in_specs=[whole, whole],
        out_specs=[whole] * high,
        scratch_shapes=[pltpu.VMEM((slots * wave_count, LANES), jnp.float32)],
        compiler_params=params,
        name="gather",
    )(
        wave_table.reshape(-1, LANES),
        jnp.transpose(fourier, (1, 0, 2)).reshape(used, waves),
    )
    token = pl.pallas_call(
        touch_kernel,
        out_shape=jax.ShapeDtypeStruct((2 * TILE, LANES), legendre.dtype),
        in_specs=[whole],
        out_specs=whole,
        compiler_params=params,
        name="touch",
    )(legendre)
    turns = [t * low + u for u in range(low) for t in range(high // 2)]
    passed = [ordered[0]] + [
        lax.ppermute(ordered[t], "wave", [(w, w ^ t * low) for w in range(wave_count)])
        for t in range(1, high)
    ]
    lower = lax.axis_index("wave") < wave_count // 2
    sources = []
    for mirrored in (False, True):
        for u in range(low):
            sides = [
                jnp.stack([passed[t][u] for t in range(side * high // 2, (side + 1) * high // 2)])
                for side in (0, 1)
            ]
            block = jnp.where(lower != mirrored, sides[0], sides[1])
            block, token = lax.optimization_barrier((block, token))
            route = []
            for lat in range(lat_count):
                for wave in range(wave_count):
                    to = lat_count - 1 - lat if mirrored else lat
                    route.append((lat * wave_count + wave, to * wave_count + (wave ^ u)))
            if mirrored or u:
                block = lax.ppermute(block, ("lat", "wave"), route)
            sources.append(block)

    place, limits = pl.pallas_call(
        functools.partial(place_kernel, turns, lat_count, row_count, pairs, degrees),
        out_shape=[
            jax.ShapeDtypeStruct((wave_count * LANES, 2 * LANES), jnp.bfloat16),
            jax.ShapeDtypeStruct((slots, LANES), jnp.int32),
        ],
        in_specs=[pl.BlockSpec(memory_space=pltpu.SMEM), whole],
        out_specs=[whole] * 2,
        compiler_params=params,
        name="place",
    )(wave_table, token)

    rows = STEP * cols
    shape = (rows + rows // 4, 2 * LANES)
    core_route = [(lat, lat ^ 1) for lat in range(lat_count)]
    y_route = [(lat, lat ^ 2) for lat in range(lat_count)]
    scratch = [
        pltpu.VMEM((rows, degrees // 2), jnp.float32),
        pltpu.VMEM((rows, degrees // 2), jnp.float32),
    ]
    cost = pl.CostEstimate(flops=0, bytes_accessed=1024, transcendentals=0)
    pair_of_sums = [
        jax.ShapeDtypeStruct(shape, jnp.bfloat16),
        jax.ShapeDtypeStruct(shape, jnp.float32),
    ]
    count = slots // STEP

    def settle(sent, kept):
        return kept + lax.ppermute(sent, "lat", core_route).astype(jnp.float32)

    crossed, settled = [], []
    ties = []
    for block in range(count):
        sources, ties = lax.optimization_barrier((sources, ties))
        far_sent, far_own, near_sent, near_own = pl.pallas_call(
            functools.partial(product_kernel, block, row_count, cols),
            out_shape=pair_of_sums * 2,
            in_specs=[whole] * (2 + len(sources)),
            out_specs=[whole] * 4,
            scratch_shapes=scratch,
            compiler_params=params,
            cost_estimate=cost,
            name="product",
        )(place, legendre, *sources)
        summed = settle(far_sent, far_own).astype(jnp.bfloat16)
        ties = [summed] + settled[-1:]
        crossed.append(lax.ppermute(summed, "lat", y_route))
        settled.append(settle(near_sent, near_own))

    out = None
    for block in range(count):
        carried = [] if out is None else [out]
        out = pl.pallas_call(
            functools.partial(final_kernel, block * STEP, degrees, cols),
            grid=(1,),
            in_specs=[whole] * 3 + [anywhere] * len(carried),
            out_specs=pl.BlockSpec((cols, STEP, width), lambda g, at=block: (0, at, 0)),
            out_shape=jax.ShapeDtypeStruct((cols, slots, width), jnp.float32),
            input_output_aliases={3: 0} if carried else {},
            compiler_params=params,
            cost_estimate=cost,
            name="final",
        )(limits, settled[block], crossed[block], *carried)
    return jnp.transpose(out, (1, 0, 2))


def local(fourier, wave_table, legendre):
    slots, pairs, degrees = legendre.shape
    row_count, cols, waves = fourier.shape
    wave_count, lat_count = lax.axis_size("wave"), lax.axis_size("lat")
    fits = (
        lat_count == 4
        and wave_count & (wave_count - 1) == 0
        and slots % STEP == 0
        and degrees // 2 == 5 * LANES
        and row_count & (row_count - 1) == 0
        and LANES // 4 % row_count == 0
        and row_count * cols % (LANES // 4) == 0
        and row_count * cols <= LANES
        and pairs == row_count * wave_count // 2
        and pairs * TILE == 2 * LANES
        and waves % (2 * LANES) == 0
    )
    if not fits:
        return plain(fourier, wave_table, legendre)
    return packed(fourier, wave_table, legendre)


def solution(mesh):
    in_specs = (P(("lat", "wave"), None, None), P(), P("wave", "lat", None))
    out_specs = P("wave", None, "lat")
    return jax.shard_map(local, mesh=mesh, in_specs=in_specs, out_specs=out_specs, check_vma=False)
```

```python
import functools

import jax
import jax.numpy as jnp
from jax import lax
from jax.experimental import pallas as pl
from jax.experimental.pallas import tpu as pltpu
from jax.sharding import PartitionSpec as P

LANES = 128
STEP = 32
TILE = 8
VMEM = 32 * 1024 * 1024


def partner(block, axis, stride):
    count = lax.axis_size(axis)
    route = []
    for low in range(count):
        high = low | 1 << stride
        if high != low and high < count:
            route += [(low, high), (high, low)]
    return lax.ppermute(block, axis, route)


def plain(fourier, wave_table, legendre):
    slot_count, pair_count, degree_count = legendre.shape
    lat_count = lax.axis_size("lat")
    half_degrees = degree_count // 2
    slice_width = degree_count // lat_count
    lat_index = lax.axis_index("lat")
    ordered = jnp.take(fourier, wave_table, axis=2)
    arrived = lax.all_to_all(ordered, "wave", split_axis=2, concat_axis=0, tiled=True)
    local_rows = jnp.transpose(arrived, (2, 1, 0))
    kept_rows = local_rows[:, :, :pair_count]
    received = local_rows[:, :, pair_count:]
    for bit_number in range(lat_count.bit_length() - 1):
        received = partner(received, "lat", bit_number)
    northern = lat_index < lat_count // 2
    north_rows = jnp.where(northern, kept_rows, received).astype(jnp.float32)
    south_rows = jnp.where(northern, jnp.flip(received, 2), jnp.flip(kept_rows, 2)).astype(
        jnp.float32
    )
    even_part = (north_rows + south_rows).astype(jnp.bfloat16)
    odd_part = (north_rows - south_rows).astype(jnp.bfloat16)
    my_waves = lax.dynamic_slice_in_dim(wave_table, lax.axis_index("wave") * slot_count, slot_count)
    even_out = jnp.einsum(
        "mcp,mpk->mck", even_part, legendre[:, :, :half_degrees], preferred_element_type=jnp.float32
    )
    odd_out = jnp.einsum(
        "mcp,mpk->mck", odd_part, legendre[:, :, half_degrees:], preferred_element_type=jnp.float32
    )
    partial_terms = jnp.concatenate([even_out, odd_out], axis=2)
    spectral = lax.psum_scatter(partial_terms, "lat", scatter_dimension=2, tiled=True)
    degree_slot = lat_index * slice_width + jnp.arange(slice_width, dtype=jnp.int32)
    offsets = jnp.where(
        degree_slot < half_degrees, 2 * degree_slot, 2 * (degree_slot - half_degrees) + 1
    )
    inside = offsets[None, None, :] < (degree_count - my_waves)[:, None, None]
    return jnp.where(inside, spectral, jnp.zeros_like(spectral))


def shift_of(block, used):
    return block * used // LANES, block * used % LANES


def gather_kernel(slots, low, table_ref, rows_ref, *refs):
    outs, turned = refs[:-1], refs[-1]
    me = lax.axis_index("wave")
    used, waves = rows_ref.shape
    rows = jnp.concatenate([rows_ref[...], jnp.zeros((LANES - used, waves), jnp.bfloat16)], axis=0)
    number = lax.broadcasted_iota(jnp.int32, (waves, LANES), 0)
    for j in range(0, table_ref.shape[0], 2):
        chosen = jnp.concatenate(
            [(number == table_ref[k : k + 1, :]).astype(jnp.bfloat16) for k in (j, j + 1)], axis=1
        )
        got = jnp.dot(rows, chosen, preferred_element_type=jnp.float32)
        turned[j * LANES : (j + 2) * LANES, :] = got.T
    lane = lax.broadcasted_iota(jnp.int32, (STEP, LANES), 1)
    for t, out in enumerate(outs):
        for u in range(low):
            begin = (me ^ (t * low + u)) * slots
            tiles = [jnp.zeros((STEP, LANES), jnp.float32)] * (out.shape[2] // LANES)
            for block in range(slots // STEP):
                tile, off = shift_of(block, used)
                value = turned[pl.ds(pl.multiple_of(begin + block * STEP, STEP), STEP), :]
                value = pltpu.roll(value, off, 1) if off else value
                tiles[tile] = jnp.where(lane >= off, value, tiles[tile])
                if off + used > LANES:
                    tiles[tile + 1] = jnp.where(lane < off + used - LANES, value, tiles[tile + 1])
            for k, tile in enumerate(tiles):
                out[u, :, k * LANES : (k + 1) * LANES] = tile.astype(jnp.bfloat16)


def place_kernel(turns, lat_count, row_count, pairs, degrees, table_ref, out, limits):
    northern = lax.axis_index("lat") < lat_count // 2
    me = lax.axis_index("wave")
    row = lax.broadcasted_iota(jnp.int32, (LANES, 2 * LANES), 0) & (row_count - 1)
    col = lax.broadcasted_iota(jnp.int32, (LANES, 2 * LANES), 1) & (pairs - 1 | LANES)
    half = len(turns)
    for k in range(2 * half):
        ascending = northern if k < half else jnp.logical_not(northern)
        position = ((me ^ turns[k % half]) % half) * row_count + row
        position = jnp.where(ascending, position, pairs - 1 - position)
        target = position + jnp.where(ascending, 0, LANES)
        out[k * LANES : (k + 1) * LANES, :] = (col == target).astype(jnp.bfloat16)
    slots = limits.shape[0]
    line = lax.broadcasted_iota(jnp.int32, (TILE, LANES), 0)
    for first in range(0, slots, TILE):
        value = jnp.zeros((TILE, LANES), jnp.int32)
        for s in range(TILE):
            value = jnp.where(line == s, degrees - table_ref[me * slots + first + s], value)
        limits[first : first + TILE, :] = value


def multiply(coefs, table, first, half, terms):
    pairs = table.shape[1]
    group = 2 * LANES // pairs
    cols = coefs.shape[0] // STEP
    shape = (cols * group, 2 * LANES)
    diagonal = (lax.broadcasted_iota(jnp.int32, shape, 0) & (group - 1)) == (
        lax.broadcasted_iota(jnp.int32, shape, 1) // pairs
    )
    blank = jnp.zeros(shape, jnp.bfloat16)
    for g in range(STEP // group):
        block = jnp.concatenate(
            [coefs[c * STEP + g * group : c * STEP + (g + 1) * group] for c in range(cols)], axis=0
        ).astype(jnp.bfloat16)
        block = jnp.where(diagonal, jnp.concatenate([block, block], axis=1), blank)
        weights = table[g * group : (g + 1) * group, :, pl.ds(first, half)]
        got = jnp.dot(
            block, weights.reshape(group * pairs, half), preferred_element_type=jnp.float32
        )
        for c in range(cols):
            terms[pl.ds(c * STEP + g * group, group), :] = got[c * group : (c + 1) * group]


def pack(terms, core, sent, kept):
    rows = terms.shape[0]
    part = rows // 4
    lane_low = lax.broadcasted_iota(jnp.int32, (part, LANES), 1) < LANES // 2
    for out, target in ((sent, 1 - core), (kept, core)):
        first = pl.multiple_of(target * 3 * LANES, LANES)
        out[:rows, :] = terms[:, pl.ds(first, 2 * LANES)].astype(out.dtype)
    for j in range(2):
        low = terms[pl.ds(2 * j * part, part), pl.ds(2 * LANES, LANES)]
        high = terms[pl.ds((2 * j + 1) * part, part), pl.ds(2 * LANES, LANES)]
        zeroth = jnp.where(lane_low, low, pltpu.roll(high, LANES // 2, 1))
        other = jnp.where(lane_low, pltpu.roll(low, LANES // 2, 1), high)
        for out, target in ((sent, 1 - core), (kept, core)):
            out[rows:, j * LANES : (j + 1) * LANES] = jnp.where(target == 0, zeroth, other).astype(
                out.dtype
            )


def product_kernel(block, row_count, cols, place_ref, leg_ref, *refs):
    sources = refs[:-6]
    far_sent, far_own, near_sent, near_own, far, near = refs[-6:]
    half = far.shape[1]
    lat = lax.axis_index("lat")
    y, core = lat // 2, lat % 2
    tile, off = shift_of(block, row_count * cols)
    lane = lax.broadcasted_iota(jnp.int32, (STEP, LANES), 1)
    held = ((lane - off) & (LANES - 1)) // row_count
    zero = jnp.zeros((STEP, LANES), jnp.bfloat16)
    parts = []
    for source in sources:
        for k in range(source.shape[0]):
            value = source[k, :, tile * LANES : (tile + 1) * LANES]
            if off + row_count * cols > LANES:
                value = jnp.where(
                    lane >= off, value, source[k, :, (tile + 1) * LANES : (tile + 2) * LANES]
                )
            parts.append(
                jnp.concatenate([jnp.where(held == c, value, zero) for c in range(cols)], axis=0)
            )
    both = jnp.dot(
        jnp.concatenate(parts, axis=1), place_ref[...], preferred_element_type=jnp.float32
    )
    north, south = both[:, :LANES], both[:, LANES:]
    even, odd = north + south, north - south
    far_coefs, near_coefs = jnp.where(y == 0, odd, even), jnp.where(y == 0, even, odd)
    multiply(far_coefs, leg_ref, pl.multiple_of((1 - y) * half, LANES), half, far)
    multiply(near_coefs, leg_ref, pl.multiple_of(y * half, LANES), half, near)
    pack(far, core, far_sent, far_own)
    pack(near, core, near_sent, near_own)


def final_kernel(base, degrees, cols, limits_ref, near_ref, far_ref, *refs):
    out = refs[-1]
    lat = lax.axis_index("lat")
    first = lat % 2 == 0
    half = degrees // 2
    width = out.shape[2]
    rows = STEP * cols
    value = near_ref[...] + far_ref[...].astype(jnp.float32)
    main0, main1 = value[:rows, :LANES], value[:rows, LANES:]
    tails = []
    for j in range(4):
        tail = value[rows:, (j // 2) * LANES : (j // 2 + 1) * LANES]
        tails.append(pltpu.roll(tail, LANES // 2, 1) if j % 2 else tail)
    tail = jnp.concatenate(tails, axis=0)
    lane_low = lax.broadcasted_iota(jnp.int32, (rows, LANES), 1) < LANES // 2
    turn0, turn1 = pltpu.roll(main0, LANES // 2, 1), pltpu.roll(main1, LANES // 2, 1)
    ordered = jnp.concatenate(
        [
            jnp.where(first, main0, jnp.where(lane_low, tail, turn0)),
            jnp.where(first, main1, jnp.where(lane_low, turn0, turn1)),
            jnp.where(first, tail, turn1),
        ],
        axis=1,
    )
    shape = (STEP, 3 * LANES)
    degree = lat * width + lax.broadcasted_iota(jnp.int32, shape, 1)
    offsets = jnp.where(degree < half, 2 * degree, 2 * (degree - half) + 1)
    limits = limits_ref[base : base + STEP, :]
    limits = jnp.concatenate([limits] * 3, axis=1)
    inside = offsets < limits
    for c in range(cols):
        out[c] = jnp.where(inside, ordered[c * STEP : (c + 1) * STEP], 0.0)[:, :width]


def packed(fourier, wave_table, legendre):
    slots, pairs, degrees = legendre.shape
    row_count, cols, waves = fourier.shape
    wave_count, lat_count = lax.axis_size("wave"), lax.axis_size("lat")
    width = degrees // lat_count
    used = row_count * cols
    params = pltpu.CompilerParams(vmem_limit_bytes=VMEM)
    whole = pl.BlockSpec(memory_space=pltpu.VMEM)
    anywhere = pl.BlockSpec(memory_space=pl.ANY)

    message = -(-(slots // STEP) * used // LANES) * LANES
    low = 2
    high = wave_count // low
    ordered = pl.pallas_call(
        functools.partial(gather_kernel, slots, low),
        out_shape=[jax.ShapeDtypeStruct((low, STEP, message), jnp.bfloat16)] * high,
        in_specs=[whole, whole],
        out_specs=[whole] * high,
        scratch_shapes=[pltpu.VMEM((slots * wave_count, LANES), jnp.float32)],
        compiler_params=params,
        name="gather",
    )(
        wave_table.reshape(-1, LANES),
        jnp.transpose(fourier, (1, 0, 2)).reshape(used, waves),
    )
    turns = [t * low + u for u in range(low) for t in range(high // 2)]
    passed = [ordered[0]] + [
        lax.ppermute(ordered[t], "wave", [(w, w ^ t * low) for w in range(wave_count)])
        for t in range(1, high)
    ]
    lower = lax.axis_index("wave") < wave_count // 2
    count = slots // STEP
    early = count - count // 2
    tables = [legendre[block * STEP : (block + 1) * STEP] for block in range(early)]
    sources = []
    for mirrored in (False, True):
        for u in range(low):
            sides = [
                jnp.stack([passed[t][u] for t in range(side * high // 2, (side + 1) * high // 2)])
                for side in (0, 1)
            ]
            block = jnp.where(lower != mirrored, sides[0], sides[1])
            block, tables = lax.optimization_barrier((block, tables))
            route = []
            for lat in range(lat_count):
                for wave in range(wave_count):
                    to = lat_count - 1 - lat if mirrored else lat
                    route.append((lat * wave_count + wave, to * wave_count + (wave ^ u)))
            if mirrored or u:
                block = lax.ppermute(block, ("lat", "wave"), route)
            sources.append(block)

    place, limits = pl.pallas_call(
        functools.partial(place_kernel, turns, lat_count, row_count, pairs, degrees),
        out_shape=[
            jax.ShapeDtypeStruct((wave_count * LANES, 2 * LANES), jnp.bfloat16),
            jax.ShapeDtypeStruct((slots, LANES), jnp.int32),
        ],
        in_specs=[pl.BlockSpec(memory_space=pltpu.SMEM)],
        out_specs=[whole] * 2,
        compiler_params=params,
        name="place",
    )(wave_table)

    rows = STEP * cols
    shape = (rows + rows // 4, 2 * LANES)
    core_route = [(lat, lat ^ 1) for lat in range(lat_count)]
    y_route = [(lat, lat ^ 2) for lat in range(lat_count)]
    scratch = [
        pltpu.VMEM((rows, degrees // 2), jnp.float32),
        pltpu.VMEM((rows, degrees // 2), jnp.float32),
    ]
    cost = pl.CostEstimate(flops=0, bytes_accessed=1024, transcendentals=0)
    pair_of_sums = [
        jax.ShapeDtypeStruct(shape, jnp.bfloat16),
        jax.ShapeDtypeStruct(shape, jnp.float32),
    ]
    def settle(sent, kept):
        return kept + lax.ppermute(sent, "lat", core_route).astype(jnp.float32)

    crossed, settled = [], []
    ties = []
    for block in range(count):
        if block == early - 1:
            legendre, sources, ties = lax.optimization_barrier((legendre, sources, ties))
            tables = tables + [legendre[k * STEP : (k + 1) * STEP] for k in range(early, count)]
        else:
            sources, ties = lax.optimization_barrier((sources, ties))
        far_sent, far_own, near_sent, near_own = pl.pallas_call(
            functools.partial(product_kernel, block, row_count, cols),
            out_shape=pair_of_sums * 2,
            in_specs=[whole] * (2 + len(sources)),
            out_specs=[whole] * 4,
            scratch_shapes=scratch,
            compiler_params=params,
            cost_estimate=cost,
            name="product",
        )(place, tables[block], *sources)
        summed = settle(far_sent, far_own).astype(jnp.bfloat16)
        ties = [summed] + settled[-1:]
        crossed.append(lax.ppermute(summed, "lat", y_route))
        settled.append(settle(near_sent, near_own))

    out = None
    for block in range(count):
        carried = [] if out is None else [out]
        out = pl.pallas_call(
            functools.partial(final_kernel, block * STEP, degrees, cols),
            grid=(1,),
            in_specs=[whole] * 3 + [anywhere] * len(carried),
            out_specs=pl.BlockSpec((cols, STEP, width), lambda g, at=block: (0, at, 0)),
            out_shape=jax.ShapeDtypeStruct((cols, slots, width), jnp.float32),
            input_output_aliases={3: 0} if carried else {},
            compiler_params=params,
            cost_estimate=cost,
            name="final",
        )(limits, settled[block], crossed[block], *carried)
    return jnp.transpose(out, (1, 0, 2))


def local(fourier, wave_table, legendre):
    slots, pairs, degrees = legendre.shape
    row_count, cols, waves = fourier.shape
    wave_count, lat_count = lax.axis_size("wave"), lax.axis_size("lat")
    fits = (
        lat_count == 4
        and wave_count & (wave_count - 1) == 0
        and slots % STEP == 0
        and degrees // 2 == 5 * LANES
        and row_count & (row_count - 1) == 0
        and LANES // 4 % row_count == 0
        and row_count * cols % (LANES // 4) == 0
        and row_count * cols <= LANES
        and pairs == row_count * wave_count // 2
        and pairs * TILE == 2 * LANES
        and waves % (2 * LANES) == 0
    )
    if not fits:
        return plain(fourier, wave_table, legendre)
    return packed(fourier, wave_table, legendre)


def solution(mesh):
    in_specs = (P(("lat", "wave"), None, None), P(), P("wave", "lat", None))
    out_specs = P("wave", None, "lat")
    return jax.shard_map(local, mesh=mesh, in_specs=in_specs, out_specs=out_specs, check_vma=False)
```

```python
import functools

import jax
import jax.numpy as jnp
from jax import lax
from jax.experimental import pallas as pl
from jax.experimental.pallas import tpu as pltpu
from jax.sharding import PartitionSpec as P

LANES = 128
STEP = 32
TILE = 8
VMEM = 20 * 1024 * 1024


def partner(block, axis, stride):
    count = lax.axis_size(axis)
    route = []
    for low in range(count):
        high = low | 1 << stride
        if high != low and high < count:
            route += [(low, high), (high, low)]
    return lax.ppermute(block, axis, route)


def plain(fourier, wave_table, legendre):
    slot_count, pair_count, degree_count = legendre.shape
    lat_count = lax.axis_size("lat")
    half_degrees = degree_count // 2
    slice_width = degree_count // lat_count
    lat_index = lax.axis_index("lat")
    ordered = jnp.take(fourier, wave_table, axis=2)
    arrived = lax.all_to_all(ordered, "wave", split_axis=2, concat_axis=0, tiled=True)
    local_rows = jnp.transpose(arrived, (2, 1, 0))
    kept_rows = local_rows[:, :, :pair_count]
    received = local_rows[:, :, pair_count:]
    for bit_number in range(lat_count.bit_length() - 1):
        received = partner(received, "lat", bit_number)
    northern = lat_index < lat_count // 2
    north_rows = jnp.where(northern, kept_rows, received).astype(jnp.float32)
    south_rows = jnp.where(northern, jnp.flip(received, 2), jnp.flip(kept_rows, 2)).astype(
        jnp.float32
    )
    even_part = (north_rows + south_rows).astype(jnp.bfloat16)
    odd_part = (north_rows - south_rows).astype(jnp.bfloat16)
    my_waves = lax.dynamic_slice_in_dim(wave_table, lax.axis_index("wave") * slot_count, slot_count)
    even_out = jnp.einsum(
        "mcp,mpk->mck", even_part, legendre[:, :, :half_degrees], preferred_element_type=jnp.float32
    )
    odd_out = jnp.einsum(
        "mcp,mpk->mck", odd_part, legendre[:, :, half_degrees:], preferred_element_type=jnp.float32
    )
    partial_terms = jnp.concatenate([even_out, odd_out], axis=2)
    spectral = lax.psum_scatter(partial_terms, "lat", scatter_dimension=2, tiled=True)
    degree_slot = lat_index * slice_width + jnp.arange(slice_width, dtype=jnp.int32)
    offsets = jnp.where(
        degree_slot < half_degrees, 2 * degree_slot, 2 * (degree_slot - half_degrees) + 1
    )
    inside = offsets[None, None, :] < (degree_count - my_waves)[:, None, None]
    return jnp.where(inside, spectral, jnp.zeros_like(spectral))


def shift_of(block, used):
    return block * used // LANES, block * used % LANES


def gather_kernel(slots, low, table_ref, rows_ref, *refs):
    outs, turned = refs[:-1], refs[-1]
    me = lax.axis_index("wave")
    used, waves = rows_ref.shape
    rows = jnp.concatenate([rows_ref[...], jnp.zeros((LANES - used, waves), jnp.bfloat16)], axis=0)
    number = lax.broadcasted_iota(jnp.int32, (waves, LANES), 0)
    for j in range(0, table_ref.shape[0], 2):
        chosen = jnp.concatenate(
            [(number == table_ref[k : k + 1, :]).astype(jnp.bfloat16) for k in (j, j + 1)], axis=1
        )
        got = jnp.dot(rows, chosen, preferred_element_type=jnp.float32)
        turned[j * LANES : (j + 2) * LANES, :] = got.T
    lane = lax.broadcasted_iota(jnp.int32, (STEP, LANES), 1)
    for t, out in enumerate(outs):
        for u in range(low):
            begin = (me ^ (t * low + u)) * slots
            tiles = [jnp.zeros((STEP, LANES), jnp.float32)] * (out.shape[2] // LANES)
            for block in range(slots // STEP):
                tile, off = shift_of(block, used)
                value = turned[pl.ds(pl.multiple_of(begin + block * STEP, STEP), STEP), :]
                value = pltpu.roll(value, off, 1) if off else value
                tiles[tile] = jnp.where(lane >= off, value, tiles[tile])
                if off + used > LANES:
                    tiles[tile + 1] = jnp.where(lane < off + used - LANES, value, tiles[tile + 1])
            for k, tile in enumerate(tiles):
                out[u, :, k * LANES : (k + 1) * LANES] = tile.astype(jnp.bfloat16)


def place_kernel(turns, lat_count, row_count, pairs, degrees, table_ref, out, limits):
    northern = lax.axis_index("lat") < lat_count // 2
    me = lax.axis_index("wave")
    row = lax.broadcasted_iota(jnp.int32, (LANES, 2 * LANES), 0) & (row_count - 1)
    col = lax.broadcasted_iota(jnp.int32, (LANES, 2 * LANES), 1) & (pairs - 1 | LANES)
    half = len(turns)
    for k in range(2 * half):
        ascending = northern if k < half else jnp.logical_not(northern)
        position = ((me ^ turns[k % half]) % half) * row_count + row
        position = jnp.where(ascending, position, pairs - 1 - position)
        target = position + jnp.where(ascending, 0, LANES)
        out[k * LANES : (k + 1) * LANES, :] = (col == target).astype(jnp.bfloat16)
    slots = limits.shape[0]
    line = lax.broadcasted_iota(jnp.int32, (TILE, LANES), 0)
    for first in range(0, slots, TILE):
        value = jnp.zeros((TILE, LANES), jnp.int32)
        for s in range(TILE):
            value = jnp.where(line == s, degrees - table_ref[me * slots + first + s], value)
        limits[first : first + TILE, :] = value


def multiply(coefs, table, first, half, terms):
    pairs = table.shape[1]
    group = 2 * LANES // pairs
    cols = coefs.shape[0] // STEP
    shape = (cols * group, 2 * LANES)
    diagonal = (lax.broadcasted_iota(jnp.int32, shape, 0) & (group - 1)) == (
        lax.broadcasted_iota(jnp.int32, shape, 1) // pairs
    )
    blank = jnp.zeros(shape, jnp.bfloat16)
    for g in range(STEP // group):
        block = jnp.concatenate(
            [coefs[c * STEP + g * group : c * STEP + (g + 1) * group] for c in range(cols)], axis=0
        ).astype(jnp.bfloat16)
        block = jnp.where(diagonal, jnp.concatenate([block, block], axis=1), blank)
        weights = table[g * group : (g + 1) * group, :, pl.ds(first, half)]
        got = jnp.dot(
            block, weights.reshape(group * pairs, half), preferred_element_type=jnp.float32
        )
        for c in range(cols):
            terms[pl.ds(c * STEP + g * group, group), :] = got[c * group : (c + 1) * group]


def pack(terms, core, sent, kept):
    rows = terms.shape[0]
    part = rows // 4
    lane_low = lax.broadcasted_iota(jnp.int32, (part, LANES), 1) < LANES // 2
    for out, target in ((sent, 1 - core), (kept, core)):
        first = pl.multiple_of(target * 3 * LANES, LANES)
        out[:rows, :] = terms[:, pl.ds(first, 2 * LANES)].astype(out.dtype)
    for j in range(2):
        low = terms[pl.ds(2 * j * part, part), pl.ds(2 * LANES, LANES)]
        high = terms[pl.ds((2 * j + 1) * part, part), pl.ds(2 * LANES, LANES)]
        zeroth = jnp.where(lane_low, low, pltpu.roll(high, LANES // 2, 1))
        other = jnp.where(lane_low, pltpu.roll(low, LANES // 2, 1), high)
        for out, target in ((sent, 1 - core), (kept, core)):
            out[rows:, j * LANES : (j + 1) * LANES] = jnp.where(target == 0, zeroth, other).astype(
                out.dtype
            )


def product_kernel(block, row_count, cols, place_ref, leg_ref, *refs):
    sources = refs[:-6]
    far_sent, far_own, near_sent, near_own, far, near = refs[-6:]
    half = far.shape[1]
    lat = lax.axis_index("lat")
    y, core = lat // 2, lat % 2
    tile, off = shift_of(block, row_count * cols)
    lane = lax.broadcasted_iota(jnp.int32, (STEP, LANES), 1)
    held = ((lane - off) & (LANES - 1)) // row_count
    zero = jnp.zeros((STEP, LANES), jnp.bfloat16)
    parts = []
    for source in sources:
        for k in range(source.shape[0]):
            value = source[k, :, tile * LANES : (tile + 1) * LANES]
            if off + row_count * cols > LANES:
                value = jnp.where(
                    lane >= off, value, source[k, :, (tile + 1) * LANES : (tile + 2) * LANES]
                )
            parts.append(
                jnp.concatenate([jnp.where(held == c, value, zero) for c in range(cols)], axis=0)
            )
    both = jnp.dot(
        jnp.concatenate(parts, axis=1), place_ref[...], preferred_element_type=jnp.float32
    )
    north, south = both[:, :LANES], both[:, LANES:]
    even, odd = north + south, north - south
    far_coefs, near_coefs = jnp.where(y == 0, odd, even), jnp.where(y == 0, even, odd)
    multiply(far_coefs, leg_ref, pl.multiple_of((1 - y) * half, LANES), half, far)
    multiply(near_coefs, leg_ref, pl.multiple_of(y * half, LANES), half, near)
    pack(far, core, far_sent, far_own)
    pack(near, core, near_sent, near_own)


def final_kernel(base, degrees, cols, limits_ref, near_ref, far_ref, *refs):
    out = refs[-1]
    lat = lax.axis_index("lat")
    first = lat % 2 == 0
    half = degrees // 2
    width = out.shape[2]
    rows = STEP * cols
    value = near_ref[...] + far_ref[...].astype(jnp.float32)
    main0, main1 = value[:rows, :LANES], value[:rows, LANES:]
    tails = []
    for j in range(4):
        tail = value[rows:, (j // 2) * LANES : (j // 2 + 1) * LANES]
        tails.append(pltpu.roll(tail, LANES // 2, 1) if j % 2 else tail)
    tail = jnp.concatenate(tails, axis=0)
    lane_low = lax.broadcasted_iota(jnp.int32, (rows, LANES), 1) < LANES // 2
    turn0, turn1 = pltpu.roll(main0, LANES // 2, 1), pltpu.roll(main1, LANES // 2, 1)
    ordered = jnp.concatenate(
        [
            jnp.where(first, main0, jnp.where(lane_low, tail, turn0)),
            jnp.where(first, main1, jnp.where(lane_low, turn0, turn1)),
            jnp.where(first, tail, turn1),
        ],
        axis=1,
    )
    shape = (STEP, 3 * LANES)
    degree = lat * width + lax.broadcasted_iota(jnp.int32, shape, 1)
    offsets = jnp.where(degree < half, 2 * degree, 2 * (degree - half) + 1)
    limits = limits_ref[base : base + STEP, :]
    limits = jnp.concatenate([limits] * 3, axis=1)
    inside = offsets < limits
    for c in range(cols):
        out[c] = jnp.where(inside, ordered[c * STEP : (c + 1) * STEP], 0.0)[:, :width]


def packed(fourier, wave_table, legendre):
    slots, pairs, degrees = legendre.shape
    row_count, cols, waves = fourier.shape
    wave_count, lat_count = lax.axis_size("wave"), lax.axis_size("lat")
    width = degrees // lat_count
    used = row_count * cols
    params = pltpu.CompilerParams(vmem_limit_bytes=VMEM)
    whole = pl.BlockSpec(memory_space=pltpu.VMEM)
    anywhere = pl.BlockSpec(memory_space=pl.ANY)

    message = -(-(slots // STEP) * used // LANES) * LANES
    low = 2
    high = wave_count // low
    ordered = pl.pallas_call(
        functools.partial(gather_kernel, slots, low),
        out_shape=[jax.ShapeDtypeStruct((low, STEP, message), jnp.bfloat16)] * high,
        in_specs=[whole, whole],
        out_specs=[whole] * high,
        scratch_shapes=[pltpu.VMEM((slots * wave_count, LANES), jnp.float32)],
        compiler_params=params,
        name="gather",
    )(
        wave_table.reshape(-1, LANES),
        jnp.transpose(fourier, (1, 0, 2)).reshape(used, waves),
    )
    turns = [t * low + u for u in range(low) for t in range(high // 2)]
    passed = [ordered[0]] + [
        lax.ppermute(ordered[t], "wave", [(w, w ^ t * low) for w in range(wave_count)])
        for t in range(1, high)
    ]
    lower = lax.axis_index("wave") < wave_count // 2
    count = slots // STEP
    early = count - count // 2
    tables = [legendre[block * STEP : (block + 1) * STEP] for block in range(early)]
    sources = []
    for mirrored in (False, True):
        for u in range(low):
            sides = [
                jnp.stack([passed[t][u] for t in range(side * high // 2, (side + 1) * high // 2)])
                for side in (0, 1)
            ]
            block = jnp.where(lower != mirrored, sides[0], sides[1])
            block, tables = lax.optimization_barrier((block, tables))
            route = []
            for lat in range(lat_count):
                for wave in range(wave_count):
                    to = lat_count - 1 - lat if mirrored else lat
                    route.append((lat * wave_count + wave, to * wave_count + (wave ^ u)))
            if mirrored or u:
                block = lax.ppermute(block, ("lat", "wave"), route)
            sources.append(block)

    place, limits = pl.pallas_call(
        functools.partial(place_kernel, turns, lat_count, row_count, pairs, degrees),
        out_shape=[
            jax.ShapeDtypeStruct((wave_count * LANES, 2 * LANES), jnp.bfloat16),
            jax.ShapeDtypeStruct((slots, LANES), jnp.int32),
        ],
        in_specs=[pl.BlockSpec(memory_space=pltpu.SMEM)],
        out_specs=[whole] * 2,
        compiler_params=params,
        name="place",
    )(wave_table)

    rows = STEP * cols
    shape = (rows + rows // 4, 2 * LANES)
    core_route = [(lat, lat ^ 1) for lat in range(lat_count)]
    y_route = [(lat, lat ^ 2) for lat in range(lat_count)]
    scratch = [
        pltpu.VMEM((rows, degrees // 2), jnp.float32),
        pltpu.VMEM((rows, degrees // 2), jnp.float32),
    ]
    cost = pl.CostEstimate(flops=0, bytes_accessed=1024, transcendentals=0)
    pair_of_sums = [
        jax.ShapeDtypeStruct(shape, jnp.bfloat16),
        jax.ShapeDtypeStruct(shape, jnp.float32),
    ]
    def settle(sent, kept):
        return kept + lax.ppermute(sent, "lat", core_route).astype(jnp.float32)

    crossed, settled = [], []
    ties = []
    for block in range(count):
        if block == early - 1:
            legendre, sources, ties = lax.optimization_barrier((legendre, sources, ties))
            tables = tables + [legendre[k * STEP : (k + 1) * STEP] for k in range(early, count)]
        else:
            sources, ties = lax.optimization_barrier((sources, ties))
        far_sent, far_own, near_sent, near_own = pl.pallas_call(
            functools.partial(product_kernel, block, row_count, cols),
            out_shape=pair_of_sums * 2,
            in_specs=[whole] * (2 + len(sources)),
            out_specs=[whole] * 4,
            scratch_shapes=scratch,
            compiler_params=params,
            cost_estimate=cost,
            name="product",
        )(place, tables[block], *sources)
        summed = settle(far_sent, far_own).astype(jnp.bfloat16)
        ties = [summed] + settled[-1:]
        crossed.append(lax.ppermute(summed, "lat", y_route))
        settled.append(settle(near_sent, near_own))

    out = None
    for block in range(count):
        carried = [] if out is None else [out]
        out = pl.pallas_call(
            functools.partial(final_kernel, block * STEP, degrees, cols),
            grid=(1,),
            in_specs=[whole] * 3 + [anywhere] * len(carried),
            out_specs=pl.BlockSpec((cols, STEP, width), lambda g, at=block: (0, at, 0)),
            out_shape=jax.ShapeDtypeStruct((cols, slots, width), jnp.float32),
            input_output_aliases={3: 0} if carried else {},
            compiler_params=params,
            cost_estimate=cost,
            name="final",
        )(limits, settled[block], crossed[block], *carried)
    return jnp.transpose(out, (1, 0, 2))


def local(fourier, wave_table, legendre):
    slots, pairs, degrees = legendre.shape
    row_count, cols, waves = fourier.shape
    wave_count, lat_count = lax.axis_size("wave"), lax.axis_size("lat")
    fits = (
        lat_count == 4
        and wave_count & (wave_count - 1) == 0
        and slots % STEP == 0
        and degrees // 2 == 5 * LANES
        and row_count & (row_count - 1) == 0
        and LANES // 4 % row_count == 0
        and row_count * cols % (LANES // 4) == 0
        and row_count * cols <= LANES
        and pairs == row_count * wave_count // 2
        and pairs * TILE == 2 * LANES
        and waves % (2 * LANES) == 0
    )
    if not fits:
        return plain(fourier, wave_table, legendre)
    return packed(fourier, wave_table, legendre)


def solution(mesh):
    in_specs = (P(("lat", "wave"), None, None), P(), P("wave", "lat", None))
    out_specs = P("wave", None, "lat")
    return jax.shard_map(local, mesh=mesh, in_specs=in_specs, out_specs=out_specs, check_vma=False)
```

```python
import functools

import jax
import jax.numpy as jnp
from jax import lax
from jax.experimental import pallas as pl
from jax.experimental.pallas import tpu as pltpu
from jax.sharding import PartitionSpec as P

LANES = 128
STEP = 32
TILE = 8
VMEM = 20 * 1024 * 1024


def partner(block, axis, stride):
    count = lax.axis_size(axis)
    route = []
    for low in range(count):
        high = low | 1 << stride
        if high != low and high < count:
            route += [(low, high), (high, low)]
    return lax.ppermute(block, axis, route)


def plain(fourier, wave_table, legendre):
    slot_count, pair_count, degree_count = legendre.shape
    lat_count = lax.axis_size("lat")
    half_degrees = degree_count // 2
    slice_width = degree_count // lat_count
    lat_index = lax.axis_index("lat")
    ordered = jnp.take(fourier, wave_table, axis=2)
    arrived = lax.all_to_all(ordered, "wave", split_axis=2, concat_axis=0, tiled=True)
    local_rows = jnp.transpose(arrived, (2, 1, 0))
    kept_rows = local_rows[:, :, :pair_count]
    received = local_rows[:, :, pair_count:]
    for bit_number in range(lat_count.bit_length() - 1):
        received = partner(received, "lat", bit_number)
    northern = lat_index < lat_count // 2
    north_rows = jnp.where(northern, kept_rows, received).astype(jnp.float32)
    south_rows = jnp.where(northern, jnp.flip(received, 2), jnp.flip(kept_rows, 2)).astype(
        jnp.float32
    )
    even_part = (north_rows + south_rows).astype(jnp.bfloat16)
    odd_part = (north_rows - south_rows).astype(jnp.bfloat16)
    my_waves = lax.dynamic_slice_in_dim(wave_table, lax.axis_index("wave") * slot_count, slot_count)
    even_out = jnp.einsum(
        "mcp,mpk->mck", even_part, legendre[:, :, :half_degrees], preferred_element_type=jnp.float32
    )
    odd_out = jnp.einsum(
        "mcp,mpk->mck", odd_part, legendre[:, :, half_degrees:], preferred_element_type=jnp.float32
    )
    partial_terms = jnp.concatenate([even_out, odd_out], axis=2)
    spectral = lax.psum_scatter(partial_terms, "lat", scatter_dimension=2, tiled=True)
    degree_slot = lat_index * slice_width + jnp.arange(slice_width, dtype=jnp.int32)
    offsets = jnp.where(
        degree_slot < half_degrees, 2 * degree_slot, 2 * (degree_slot - half_degrees) + 1
    )
    inside = offsets[None, None, :] < (degree_count - my_waves)[:, None, None]
    return jnp.where(inside, spectral, jnp.zeros_like(spectral))


def shift_of(block, used):
    return block * used // LANES, block * used % LANES


def gather_kernel(slots, low, table_ref, rows_ref, *refs):
    outs, turned = refs[:-1], refs[-1]
    me = lax.axis_index("wave")
    used, waves = rows_ref.shape
    rows = jnp.concatenate([rows_ref[...], jnp.zeros((LANES - used, waves), jnp.bfloat16)], axis=0)
    number = lax.broadcasted_iota(jnp.int32, (waves, LANES), 0)
    for j in range(0, table_ref.shape[0], 2):
        chosen = jnp.concatenate(
            [(number == table_ref[k : k + 1, :]).astype(jnp.bfloat16) for k in (j, j + 1)], axis=1
        )
        got = jnp.dot(rows, chosen, preferred_element_type=jnp.float32)
        turned[j * LANES : (j + 2) * LANES, :] = got.T
    lane = lax.broadcasted_iota(jnp.int32, (STEP, LANES), 1)
    for t, out in enumerate(outs):
        for u in range(low):
            begin = (me ^ (t * low + u)) * slots
            tiles = [jnp.zeros((STEP, LANES), jnp.float32)] * (out.shape[2] // LANES)
            for block in range(slots // STEP):
                tile, off = shift_of(block, used)
                value = turned[pl.ds(pl.multiple_of(begin + block * STEP, STEP), STEP), :]
                value = pltpu.roll(value, off, 1) if off else value
                tiles[tile] = jnp.where(lane >= off, value, tiles[tile])
                if off + used > LANES:
                    tiles[tile + 1] = jnp.where(lane < off + used - LANES, value, tiles[tile + 1])
            for k, tile in enumerate(tiles):
                out[u, :, k * LANES : (k + 1) * LANES] = tile.astype(jnp.bfloat16)


def place_kernel(turns, lat_count, row_count, pairs, degrees, table_ref, leg_ref, out, limits):
    northern = lax.axis_index("lat") < lat_count // 2
    me = lax.axis_index("wave")
    row = lax.broadcasted_iota(jnp.int32, (LANES, 2 * LANES), 0) & (row_count - 1)
    col = lax.broadcasted_iota(jnp.int32, (LANES, 2 * LANES), 1) & (pairs - 1 | LANES)
    half = len(turns)
    for k in range(2 * half):
        ascending = northern if k < half else jnp.logical_not(northern)
        position = ((me ^ turns[k % half]) % half) * row_count + row
        position = jnp.where(ascending, position, pairs - 1 - position)
        target = position + jnp.where(ascending, 0, LANES)
        out[k * LANES : (k + 1) * LANES, :] = (col == target).astype(jnp.bfloat16)
    slots = limits.shape[0]
    line = lax.broadcasted_iota(jnp.int32, (TILE, LANES), 0)
    for first in range(0, slots, TILE):
        value = jnp.zeros((TILE, LANES), jnp.int32)
        for s in range(TILE):
            value = jnp.where(line == s, degrees - table_ref[me * slots + first + s], value)
        limits[first : first + TILE, :] = value


def multiply(coefs, table, first, half, terms):
    pairs = table.shape[1]
    group = 2 * LANES // pairs
    cols = coefs.shape[0] // STEP
    shape = (cols * group, 2 * LANES)
    diagonal = (lax.broadcasted_iota(jnp.int32, shape, 0) & (group - 1)) == (
        lax.broadcasted_iota(jnp.int32, shape, 1) // pairs
    )
    blank = jnp.zeros(shape, jnp.bfloat16)
    for g in range(STEP // group):
        block = jnp.concatenate(
            [coefs[c * STEP + g * group : c * STEP + (g + 1) * group] for c in range(cols)], axis=0
        ).astype(jnp.bfloat16)
        block = jnp.where(diagonal, jnp.concatenate([block, block], axis=1), blank)
        weights = table[g * group : (g + 1) * group, :, pl.ds(first, half)]
        got = jnp.dot(
            block, weights.reshape(group * pairs, half), preferred_element_type=jnp.float32
        )
        for c in range(cols):
            terms[pl.ds(c * STEP + g * group, group), :] = got[c * group : (c + 1) * group]


def pack(terms, core, sent, kept):
    rows = terms.shape[0]
    part = rows // 4
    lane_low = lax.broadcasted_iota(jnp.int32, (part, LANES), 1) < LANES // 2
    for out, target in ((sent, 1 - core), (kept, core)):
        first = pl.multiple_of(target * 3 * LANES, LANES)
        out[:rows, :] = terms[:, pl.ds(first, 2 * LANES)].astype(out.dtype)
    for j in range(2):
        low = terms[pl.ds(2 * j * part, part), pl.ds(2 * LANES, LANES)]
        high = terms[pl.ds((2 * j + 1) * part, part), pl.ds(2 * LANES, LANES)]
        zeroth = jnp.where(lane_low, low, pltpu.roll(high, LANES // 2, 1))
        other = jnp.where(lane_low, pltpu.roll(low, LANES // 2, 1), high)
        for out, target in ((sent, 1 - core), (kept, core)):
            out[rows:, j * LANES : (j + 1) * LANES] = jnp.where(target == 0, zeroth, other).astype(
                out.dtype
            )


def product_kernel(block, row_count, cols, place_ref, leg_ref, *refs):
    sources = refs[:-6]
    far_sent, far_own, near_sent, near_own, far, near = refs[-6:]
    half = far.shape[1]
    table = leg_ref.at[block * STEP : (block + 1) * STEP]
    lat = lax.axis_index("lat")
    y, core = lat // 2, lat % 2
    tile, off = shift_of(block, row_count * cols)
    lane = lax.broadcasted_iota(jnp.int32, (STEP, LANES), 1)
    held = ((lane - off) & (LANES - 1)) // row_count
    zero = jnp.zeros((STEP, LANES), jnp.bfloat16)
    parts = []
    for source in sources:
        for k in range(source.shape[0]):
            value = source[k, :, tile * LANES : (tile + 1) * LANES]
            if off + row_count * cols > LANES:
                value = jnp.where(
                    lane >= off, value, source[k, :, (tile + 1) * LANES : (tile + 2) * LANES]
                )
            parts.append(
                jnp.concatenate([jnp.where(held == c, value, zero) for c in range(cols)], axis=0)
            )
    both = jnp.dot(
        jnp.concatenate(parts, axis=1), place_ref[...], preferred_element_type=jnp.float32
    )
    north, south = both[:, :LANES], both[:, LANES:]
    even, odd = north + south, north - south
    far_coefs, near_coefs = jnp.where(y == 0, odd, even), jnp.where(y == 0, even, odd)
    multiply(far_coefs, table, pl.multiple_of((1 - y) * half, LANES), half, far)
    multiply(near_coefs, table, pl.multiple_of(y * half, LANES), half, near)
    pack(far, core, far_sent, far_own)
    pack(near, core, near_sent, near_own)


def final_kernel(base, degrees, cols, limits_ref, near_ref, far_ref, *refs):
    out = refs[-1]
    lat = lax.axis_index("lat")
    first = lat % 2 == 0
    half = degrees // 2
    width = out.shape[2]
    rows = STEP * cols
    value = near_ref[...] + far_ref[...].astype(jnp.float32)
    main0, main1 = value[:rows, :LANES], value[:rows, LANES:]
    tails = []
    for j in range(4):
        tail = value[rows:, (j // 2) * LANES : (j // 2 + 1) * LANES]
        tails.append(pltpu.roll(tail, LANES // 2, 1) if j % 2 else tail)
    tail = jnp.concatenate(tails, axis=0)
    lane_low = lax.broadcasted_iota(jnp.int32, (rows, LANES), 1) < LANES // 2
    turn0, turn1 = pltpu.roll(main0, LANES // 2, 1), pltpu.roll(main1, LANES // 2, 1)
    ordered = jnp.concatenate(
        [
            jnp.where(first, main0, jnp.where(lane_low, tail, turn0)),
            jnp.where(first, main1, jnp.where(lane_low, turn0, turn1)),
            jnp.where(first, tail, turn1),
        ],
        axis=1,
    )
    shape = (STEP, 3 * LANES)
    degree = lat * width + lax.broadcasted_iota(jnp.int32, shape, 1)
    offsets = jnp.where(degree < half, 2 * degree, 2 * (degree - half) + 1)
    limits = limits_ref[base : base + STEP, :]
    limits = jnp.concatenate([limits] * 3, axis=1)
    inside = offsets < limits
    for c in range(cols):
        out[c] = jnp.where(inside, ordered[c * STEP : (c + 1) * STEP], 0.0)[:, :width]


def packed(fourier, wave_table, legendre):
    slots, pairs, degrees = legendre.shape
    row_count, cols, waves = fourier.shape
    wave_count, lat_count = lax.axis_size("wave"), lax.axis_size("lat")
    width = degrees // lat_count
    used = row_count * cols
    params = pltpu.CompilerParams(vmem_limit_bytes=VMEM)
    whole = pl.BlockSpec(memory_space=pltpu.VMEM)
    anywhere = pl.BlockSpec(memory_space=pl.ANY)

    message = -(-(slots // STEP) * used // LANES) * LANES
    low = 2
    high = wave_count // low
    ordered = pl.pallas_call(
        functools.partial(gather_kernel, slots, low),
        out_shape=[jax.ShapeDtypeStruct((low, STEP, message), jnp.bfloat16)] * high,
        in_specs=[whole, whole],
        out_specs=[whole] * high,
        scratch_shapes=[pltpu.VMEM((slots * wave_count, LANES), jnp.float32)],
        compiler_params=params,
        name="gather",
    )(
        wave_table.reshape(-1, LANES),
        jnp.transpose(fourier, (1, 0, 2)).reshape(used, waves),
    )
    turns = [t * low + u for u in range(low) for t in range(high // 2)]
    place, limits = pl.pallas_call(
        functools.partial(place_kernel, turns, lat_count, row_count, pairs, degrees),
        out_shape=[
            jax.ShapeDtypeStruct((wave_count * LANES, 2 * LANES), jnp.bfloat16),
            jax.ShapeDtypeStruct((slots, LANES), jnp.int32),
        ],
        in_specs=[pl.BlockSpec(memory_space=pltpu.SMEM), anywhere],
        out_specs=[whole] * 2,
        compiler_params=params,
        name="place",
    )(wave_table, legendre)

    passed = [ordered[0]] + [
        lax.ppermute(ordered[t], "wave", [(w, w ^ t * low) for w in range(wave_count)])
        for t in range(1, high)
    ]
    lower = lax.axis_index("wave") < wave_count // 2
    sources = []
    for mirrored in (False, True):
        for u in range(low):
            sides = [
                jnp.stack([passed[t][u] for t in range(side * high // 2, (side + 1) * high // 2)])
                for side in (0, 1)
            ]
            block = jnp.where(lower != mirrored, sides[0], sides[1])
            block, place = lax.optimization_barrier((block, place))
            route = []
            for lat in range(lat_count):
                for wave in range(wave_count):
                    to = lat_count - 1 - lat if mirrored else lat
                    route.append((lat * wave_count + wave, to * wave_count + (wave ^ u)))
            if mirrored or u:
                block = lax.ppermute(block, ("lat", "wave"), route)
            sources.append(block)

    rows = STEP * cols
    shape = (rows + rows // 4, 2 * LANES)
    core_route = [(lat, lat ^ 1) for lat in range(lat_count)]
    y_route = [(lat, lat ^ 2) for lat in range(lat_count)]
    scratch = [
        pltpu.VMEM((rows, degrees // 2), jnp.float32),
        pltpu.VMEM((rows, degrees // 2), jnp.float32),
    ]
    cost = pl.CostEstimate(flops=0, bytes_accessed=1024, transcendentals=0)
    pair_of_sums = [
        jax.ShapeDtypeStruct(shape, jnp.bfloat16),
        jax.ShapeDtypeStruct(shape, jnp.float32),
    ]
    count = slots // STEP

    def settle(sent, kept):
        return kept + lax.ppermute(sent, "lat", core_route).astype(jnp.float32)

    crossed, settled = [], []
    ties = []
    for block in range(count):
        sources, ties = lax.optimization_barrier((sources, ties))
        far_sent, far_own, near_sent, near_own = pl.pallas_call(
            functools.partial(product_kernel, block, row_count, cols),
            out_shape=pair_of_sums * 2,
            in_specs=[whole] * (2 + len(sources)),
            out_specs=[whole] * 4,
            scratch_shapes=scratch,
            compiler_params=params,
            cost_estimate=cost,
            name="product",
        )(place, legendre, *sources)
        summed = settle(far_sent, far_own).astype(jnp.bfloat16)
        ties = [summed] + settled[-1:]
        crossed.append(lax.ppermute(summed, "lat", y_route))
        settled.append(settle(near_sent, near_own))

    out = None
    for block in range(count):
        carried = [] if out is None else [out]
        out = pl.pallas_call(
            functools.partial(final_kernel, block * STEP, degrees, cols),
            grid=(1,),
            in_specs=[whole] * 3 + [anywhere] * len(carried),
            out_specs=pl.BlockSpec((cols, STEP, width), lambda g, at=block: (0, at, 0)),
            out_shape=jax.ShapeDtypeStruct((cols, slots, width), jnp.float32),
            input_output_aliases={3: 0} if carried else {},
            compiler_params=params,
            cost_estimate=cost,
            name="final",
        )(limits, settled[block], crossed[block], *carried)
    return jnp.transpose(out, (1, 0, 2))


def local(fourier, wave_table, legendre):
    slots, pairs, degrees = legendre.shape
    row_count, cols, waves = fourier.shape
    wave_count, lat_count = lax.axis_size("wave"), lax.axis_size("lat")
    fits = (
        lat_count == 4
        and wave_count & (wave_count - 1) == 0
        and slots % STEP == 0
        and degrees // 2 == 5 * LANES
        and row_count & (row_count - 1) == 0
        and LANES // 4 % row_count == 0
        and row_count * cols % (LANES // 4) == 0
        and row_count * cols <= LANES
        and pairs == row_count * wave_count // 2
        and pairs * TILE == 2 * LANES
        and waves % (2 * LANES) == 0
    )
    if not fits:
        return plain(fourier, wave_table, legendre)
    return packed(fourier, wave_table, legendre)


def solution(mesh):
    in_specs = (P(("lat", "wave"), None, None), P(), P("wave", "lat", None))
    out_specs = P("wave", None, "lat")
    return jax.shard_map(local, mesh=mesh, in_specs=in_specs, out_specs=out_specs, check_vma=False)
```

```python
import functools

import jax
import jax.numpy as jnp
from jax import lax
from jax.experimental import pallas as pl
from jax.experimental.pallas import tpu as pltpu
from jax.sharding import PartitionSpec as P

LANES = 128
STEP = 32
TILE = 8
VMEM = 32 * 1024 * 1024


def partner(block, axis, stride):
    count = lax.axis_size(axis)
    route = []
    for low in range(count):
        high = low | 1 << stride
        if high != low and high < count:
            route += [(low, high), (high, low)]
    return lax.ppermute(block, axis, route)


def plain(fourier, wave_table, legendre):
    slot_count, pair_count, degree_count = legendre.shape
    lat_count = lax.axis_size("lat")
    half_degrees = degree_count // 2
    slice_width = degree_count // lat_count
    lat_index = lax.axis_index("lat")
    ordered = jnp.take(fourier, wave_table, axis=2)
    arrived = lax.all_to_all(ordered, "wave", split_axis=2, concat_axis=0, tiled=True)
    local_rows = jnp.transpose(arrived, (2, 1, 0))
    kept_rows = local_rows[:, :, :pair_count]
    received = local_rows[:, :, pair_count:]
    for bit_number in range(lat_count.bit_length() - 1):
        received = partner(received, "lat", bit_number)
    northern = lat_index < lat_count // 2
    north_rows = jnp.where(northern, kept_rows, received).astype(jnp.float32)
    south_rows = jnp.where(northern, jnp.flip(received, 2), jnp.flip(kept_rows, 2)).astype(
        jnp.float32
    )
    even_part = (north_rows + south_rows).astype(jnp.bfloat16)
    odd_part = (north_rows - south_rows).astype(jnp.bfloat16)
    my_waves = lax.dynamic_slice_in_dim(wave_table, lax.axis_index("wave") * slot_count, slot_count)
    even_out = jnp.einsum(
        "mcp,mpk->mck", even_part, legendre[:, :, :half_degrees], preferred_element_type=jnp.float32
    )
    odd_out = jnp.einsum(
        "mcp,mpk->mck", odd_part, legendre[:, :, half_degrees:], preferred_element_type=jnp.float32
    )
    partial_terms = jnp.concatenate([even_out, odd_out], axis=2)
    spectral = lax.psum_scatter(partial_terms, "lat", scatter_dimension=2, tiled=True)
    degree_slot = lat_index * slice_width + jnp.arange(slice_width, dtype=jnp.int32)
    offsets = jnp.where(
        degree_slot < half_degrees, 2 * degree_slot, 2 * (degree_slot - half_degrees) + 1
    )
    inside = offsets[None, None, :] < (degree_count - my_waves)[:, None, None]
    return jnp.where(inside, spectral, jnp.zeros_like(spectral))


def shift_of(block, used):
    return block * used // LANES, block * used % LANES


def gather_kernel(slots, low, table_ref, rows_ref, *refs):
    outs, turned = refs[:-1], refs[-1]
    me = lax.axis_index("wave")
    used, waves = rows_ref.shape
    rows = jnp.concatenate([rows_ref[...], jnp.zeros((LANES - used, waves), jnp.bfloat16)], axis=0)
    number = lax.broadcasted_iota(jnp.int32, (waves, LANES), 0)
    for j in range(0, table_ref.shape[0], 2):
        chosen = jnp.concatenate(
            [(number == table_ref[k : k + 1, :]).astype(jnp.bfloat16) for k in (j, j + 1)], axis=1
        )
        got = jnp.dot(rows, chosen, preferred_element_type=jnp.float32)
        turned[j * LANES : (j + 2) * LANES, :] = got.T
    lane = lax.broadcasted_iota(jnp.int32, (STEP, LANES), 1)
    for t, out in enumerate(outs):
        for u in range(low):
            begin = (me ^ (t * low + u)) * slots
            tiles = [jnp.zeros((STEP, LANES), jnp.float32)] * (out.shape[2] // LANES)
            for block in range(slots // STEP):
                tile, off = shift_of(block, used)
                value = turned[pl.ds(pl.multiple_of(begin + block * STEP, STEP), STEP), :]
                value = pltpu.roll(value, off, 1) if off else value
                tiles[tile] = jnp.where(lane >= off, value, tiles[tile])
                if off + used > LANES:
                    tiles[tile + 1] = jnp.where(lane < off + used - LANES, value, tiles[tile + 1])
            for k, tile in enumerate(tiles):
                out[u, :, k * LANES : (k + 1) * LANES] = tile.astype(jnp.bfloat16)


def place_kernel(turns, lat_count, row_count, pairs, degrees, table_ref, out, limits):
    northern = lax.axis_index("lat") < lat_count // 2
    me = lax.axis_index("wave")
    row = lax.broadcasted_iota(jnp.int32, (LANES, 2 * LANES), 0) & (row_count - 1)
    col = lax.broadcasted_iota(jnp.int32, (LANES, 2 * LANES), 1) & (pairs - 1 | LANES)
    half = len(turns)
    for k in range(2 * half):
        ascending = northern if k < half else jnp.logical_not(northern)
        position = ((me ^ turns[k % half]) % half) * row_count + row
        position = jnp.where(ascending, position, pairs - 1 - position)
        target = position + jnp.where(ascending, 0, LANES)
        out[k * LANES : (k + 1) * LANES, :] = (col == target).astype(jnp.bfloat16)
    slots = limits.shape[0]
    line = lax.broadcasted_iota(jnp.int32, (TILE, LANES), 0)
    for first in range(0, slots, TILE):
        value = jnp.zeros((TILE, LANES), jnp.int32)
        for s in range(TILE):
            value = jnp.where(line == s, degrees - table_ref[me * slots + first + s], value)
        limits[first : first + TILE, :] = value


def multiply(coefs, table, first, half, terms):
    pairs = table.shape[1]
    group = 2 * LANES // pairs
    cols = coefs.shape[0] // STEP
    shape = (cols * group, 2 * LANES)
    diagonal = (lax.broadcasted_iota(jnp.int32, shape, 0) & (group - 1)) == (
        lax.broadcasted_iota(jnp.int32, shape, 1) // pairs
    )
    blank = jnp.zeros(shape, jnp.bfloat16)
    for g in range(STEP // group):
        block = jnp.concatenate(
            [coefs[c * STEP + g * group : c * STEP + (g + 1) * group] for c in range(cols)], axis=0
        ).astype(jnp.bfloat16)
        block = jnp.where(diagonal, jnp.concatenate([block, block], axis=1), blank)
        weights = table[g * group : (g + 1) * group, :, pl.ds(first, half)]
        got = jnp.dot(
            block, weights.reshape(group * pairs, half), preferred_element_type=jnp.float32
        )
        for c in range(cols):
            terms[pl.ds(c * STEP + g * group, group), :] = got[c * group : (c + 1) * group]


def pack(terms, core, sent, kept):
    rows = terms.shape[0]
    part = rows // 4
    lane_low = lax.broadcasted_iota(jnp.int32, (part, LANES), 1) < LANES // 2
    for out, target in ((sent, 1 - core), (kept, core)):
        first = pl.multiple_of(target * 3 * LANES, LANES)
        out[:rows, :] = terms[:, pl.ds(first, 2 * LANES)].astype(out.dtype)
    for j in range(2):
        low = terms[pl.ds(2 * j * part, part), pl.ds(2 * LANES, LANES)]
        high = terms[pl.ds((2 * j + 1) * part, part), pl.ds(2 * LANES, LANES)]
        zeroth = jnp.where(lane_low, low, pltpu.roll(high, LANES // 2, 1))
        other = jnp.where(lane_low, pltpu.roll(low, LANES // 2, 1), high)
        for out, target in ((sent, 1 - core), (kept, core)):
            out[rows:, j * LANES : (j + 1) * LANES] = jnp.where(target == 0, zeroth, other).astype(
                out.dtype
            )


def product_kernel(block, row_count, cols, place_ref, leg_ref, *refs):
    sources = refs[:-6]
    far_sent, far_own, near_sent, near_own, far, near = refs[-6:]
    half = far.shape[1]
    lat = lax.axis_index("lat")
    y, core = lat // 2, lat % 2
    tile, off = shift_of(block, row_count * cols)
    lane = lax.broadcasted_iota(jnp.int32, (STEP, LANES), 1)
    held = ((lane - off) & (LANES - 1)) // row_count
    zero = jnp.zeros((STEP, LANES), jnp.bfloat16)
    parts = []
    for source in sources:
        for k in range(source.shape[0]):
            value = source[k, :, tile * LANES : (tile + 1) * LANES]
            if off + row_count * cols > LANES:
                value = jnp.where(
                    lane >= off, value, source[k, :, (tile + 1) * LANES : (tile + 2) * LANES]
                )
            parts.append(
                jnp.concatenate([jnp.where(held == c, value, zero) for c in range(cols)], axis=0)
            )
    both = jnp.dot(
        jnp.concatenate(parts, axis=1), place_ref[...], preferred_element_type=jnp.float32
    )
    north, south = both[:, :LANES], both[:, LANES:]
    even, odd = north + south, north - south
    far_coefs, near_coefs = jnp.where(y == 0, odd, even), jnp.where(y == 0, even, odd)
    multiply(far_coefs, leg_ref, pl.multiple_of((1 - y) * half, LANES), half, far)
    multiply(near_coefs, leg_ref, pl.multiple_of(y * half, LANES), half, near)
    pack(far, core, far_sent, far_own)
    pack(near, core, near_sent, near_own)


def final_kernel(base, degrees, cols, limits_ref, near_ref, far_ref, *refs):
    out = refs[-1]
    lat = lax.axis_index("lat")
    first = lat % 2 == 0
    half = degrees // 2
    width = out.shape[2]
    rows = STEP * cols
    value = near_ref[...] + far_ref[...].astype(jnp.float32)
    main0, main1 = value[:rows, :LANES], value[:rows, LANES:]
    tails = []
    for j in range(4):
        tail = value[rows:, (j // 2) * LANES : (j // 2 + 1) * LANES]
        tails.append(pltpu.roll(tail, LANES // 2, 1) if j % 2 else tail)
    tail = jnp.concatenate(tails, axis=0)
    lane_low = lax.broadcasted_iota(jnp.int32, (rows, LANES), 1) < LANES // 2
    turn0, turn1 = pltpu.roll(main0, LANES // 2, 1), pltpu.roll(main1, LANES // 2, 1)
    ordered = jnp.concatenate(
        [
            jnp.where(first, main0, jnp.where(lane_low, tail, turn0)),
            jnp.where(first, main1, jnp.where(lane_low, turn0, turn1)),
            jnp.where(first, tail, turn1),
        ],
        axis=1,
    )
    shape = (STEP, 3 * LANES)
    degree = lat * width + lax.broadcasted_iota(jnp.int32, shape, 1)
    offsets = jnp.where(degree < half, 2 * degree, 2 * (degree - half) + 1)
    limits = limits_ref[base : base + STEP, :]
    limits = jnp.concatenate([limits] * 3, axis=1)
    inside = offsets < limits
    for c in range(cols):
        out[c] = jnp.where(inside, ordered[c * STEP : (c + 1) * STEP], 0.0)[:, :width]


def packed(fourier, wave_table, legendre):
    slots, pairs, degrees = legendre.shape
    row_count, cols, waves = fourier.shape
    wave_count, lat_count = lax.axis_size("wave"), lax.axis_size("lat")
    width = degrees // lat_count
    used = row_count * cols
    params = pltpu.CompilerParams(vmem_limit_bytes=VMEM)
    whole = pl.BlockSpec(memory_space=pltpu.VMEM)
    anywhere = pl.BlockSpec(memory_space=pl.ANY)

    message = -(-(slots // STEP) * used // LANES) * LANES
    low = 2
    high = wave_count // low
    ordered = pl.pallas_call(
        functools.partial(gather_kernel, slots, low),
        out_shape=[jax.ShapeDtypeStruct((low, STEP, message), jnp.bfloat16)] * high,
        in_specs=[whole, whole],
        out_specs=[whole] * high,
        scratch_shapes=[pltpu.VMEM((slots * wave_count, LANES), jnp.float32)],
        compiler_params=params,
        name="gather",
    )(
        wave_table.reshape(-1, LANES),
        jnp.transpose(fourier, (1, 0, 2)).reshape(used, waves),
    )
    turns = [t * low + u for u in range(low) for t in range(high // 2)]
    place, limits = pl.pallas_call(
        functools.partial(place_kernel, turns, lat_count, row_count, pairs, degrees),
        out_shape=[
            jax.ShapeDtypeStruct((wave_count * LANES, 2 * LANES), jnp.bfloat16),
            jax.ShapeDtypeStruct((slots, LANES), jnp.int32),
        ],
        in_specs=[pl.BlockSpec(memory_space=pltpu.SMEM)],
        out_specs=[whole] * 2,
        compiler_params=params,
        name="place",
    )(wave_table)

    passed = [ordered[0]] + [
        lax.ppermute(ordered[t], "wave", [(w, w ^ t * low) for w in range(wave_count)])
        for t in range(1, high)
    ]
    count = slots // STEP
    early = count - count // 2
    tables = [legendre[block * STEP : (block + 1) * STEP] for block in range(early)]
    lower = lax.axis_index("wave") < wave_count // 2
    sources = []
    for mirrored in (False, True):
        for u in range(low):
            sides = [
                jnp.stack([passed[t][u] for t in range(side * high // 2, (side + 1) * high // 2)])
                for side in (0, 1)
            ]
            block = jnp.where(lower != mirrored, sides[0], sides[1])
            block, tables = lax.optimization_barrier((block, tables))
            if not mirrored and u == 0:
                later, block = lax.optimization_barrier((legendre, block))
            route = []
            for lat in range(lat_count):
                for wave in range(wave_count):
                    to = lat_count - 1 - lat if mirrored else lat
                    route.append((lat * wave_count + wave, to * wave_count + (wave ^ u)))
            if mirrored or u:
                block = lax.ppermute(block, ("lat", "wave"), route)
            sources.append(block)

    tables += [later[block * STEP : (block + 1) * STEP] for block in range(early, count)]
    sources, tables = lax.optimization_barrier((sources, tables))

    rows = STEP * cols
    shape = (rows + rows // 4, 2 * LANES)
    core_route = [(lat, lat ^ 1) for lat in range(lat_count)]
    y_route = [(lat, lat ^ 2) for lat in range(lat_count)]
    scratch = [
        pltpu.VMEM((rows, degrees // 2), jnp.float32),
        pltpu.VMEM((rows, degrees // 2), jnp.float32),
    ]
    cost = pl.CostEstimate(flops=0, bytes_accessed=1024, transcendentals=0)
    pair_of_sums = [
        jax.ShapeDtypeStruct(shape, jnp.bfloat16),
        jax.ShapeDtypeStruct(shape, jnp.float32),
    ]
    def settle(sent, kept):
        return kept + lax.ppermute(sent, "lat", core_route).astype(jnp.float32)

    crossed, settled = [], []
    ties = []
    for block in range(count):
        sources, ties = lax.optimization_barrier((sources, ties))
        far_sent, far_own, near_sent, near_own = pl.pallas_call(
            functools.partial(product_kernel, block, row_count, cols),
            out_shape=pair_of_sums * 2,
            in_specs=[whole] * (2 + len(sources)),
            out_specs=[whole] * 4,
            scratch_shapes=scratch,
            compiler_params=params,
            cost_estimate=cost,
            name="product",
        )(place, tables[block], *sources)
        summed = settle(far_sent, far_own).astype(jnp.bfloat16)
        ties = [summed] + settled[-1:]
        crossed.append(lax.ppermute(summed, "lat", y_route))
        settled.append(settle(near_sent, near_own))

    out = None
    for block in range(count):
        carried = [] if out is None else [out]
        out = pl.pallas_call(
            functools.partial(final_kernel, block * STEP, degrees, cols),
            grid=(1,),
            in_specs=[whole] * 3 + [anywhere] * len(carried),
            out_specs=pl.BlockSpec((cols, STEP, width), lambda g, at=block: (0, at, 0)),
            out_shape=jax.ShapeDtypeStruct((cols, slots, width), jnp.float32),
            input_output_aliases={3: 0} if carried else {},
            compiler_params=params,
            cost_estimate=cost,
            name="final",
        )(limits, settled[block], crossed[block], *carried)
    return jnp.transpose(out, (1, 0, 2))


def local(fourier, wave_table, legendre):
    slots, pairs, degrees = legendre.shape
    row_count, cols, waves = fourier.shape
    wave_count, lat_count = lax.axis_size("wave"), lax.axis_size("lat")
    fits = (
        lat_count == 4
        and wave_count & (wave_count - 1) == 0
        and slots % STEP == 0
        and degrees // 2 == 5 * LANES
        and row_count & (row_count - 1) == 0
        and LANES // 4 % row_count == 0
        and row_count * cols % (LANES // 4) == 0
        and row_count * cols <= LANES
        and pairs == row_count * wave_count // 2
        and pairs * TILE == 2 * LANES
        and waves % (2 * LANES) == 0
    )
    if not fits:
        return plain(fourier, wave_table, legendre)
    return packed(fourier, wave_table, legendre)


def solution(mesh):
    in_specs = (P(("lat", "wave"), None, None), P(), P("wave", "lat", None))
    out_specs = P("wave", None, "lat")
    return jax.shard_map(local, mesh=mesh, in_specs=in_specs, out_specs=out_specs, check_vma=False)
```

```python
import functools

import jax
import jax.numpy as jnp
from jax import lax
from jax.experimental import pallas as pl
from jax.experimental.pallas import tpu as pltpu
from jax.sharding import PartitionSpec as P

LANES = 128
STEP = 32
TILE = 8
VMEM = 32 * 1024 * 1024


def partner(block, axis, stride):
    count = lax.axis_size(axis)
    route = []
    for low in range(count):
        high = low | 1 << stride
        if high != low and high < count:
            route += [(low, high), (high, low)]
    return lax.ppermute(block, axis, route)


def plain(fourier, wave_table, legendre):
    slot_count, pair_count, degree_count = legendre.shape
    lat_count = lax.axis_size("lat")
    half_degrees = degree_count // 2
    slice_width = degree_count // lat_count
    lat_index = lax.axis_index("lat")
    ordered = jnp.take(fourier, wave_table, axis=2)
    arrived = lax.all_to_all(ordered, "wave", split_axis=2, concat_axis=0, tiled=True)
    local_rows = jnp.transpose(arrived, (2, 1, 0))
    kept_rows = local_rows[:, :, :pair_count]
    received = local_rows[:, :, pair_count:]
    for bit_number in range(lat_count.bit_length() - 1):
        received = partner(received, "lat", bit_number)
    northern = lat_index < lat_count // 2
    north_rows = jnp.where(northern, kept_rows, received).astype(jnp.float32)
    south_rows = jnp.where(northern, jnp.flip(received, 2), jnp.flip(kept_rows, 2)).astype(
        jnp.float32
    )
    even_part = (north_rows + south_rows).astype(jnp.bfloat16)
    odd_part = (north_rows - south_rows).astype(jnp.bfloat16)
    my_waves = lax.dynamic_slice_in_dim(wave_table, lax.axis_index("wave") * slot_count, slot_count)
    even_out = jnp.einsum(
        "mcp,mpk->mck", even_part, legendre[:, :, :half_degrees], preferred_element_type=jnp.float32
    )
    odd_out = jnp.einsum(
        "mcp,mpk->mck", odd_part, legendre[:, :, half_degrees:], preferred_element_type=jnp.float32
    )
    partial_terms = jnp.concatenate([even_out, odd_out], axis=2)
    spectral = lax.psum_scatter(partial_terms, "lat", scatter_dimension=2, tiled=True)
    degree_slot = lat_index * slice_width + jnp.arange(slice_width, dtype=jnp.int32)
    offsets = jnp.where(
        degree_slot < half_degrees, 2 * degree_slot, 2 * (degree_slot - half_degrees) + 1
    )
    inside = offsets[None, None, :] < (degree_count - my_waves)[:, None, None]
    return jnp.where(inside, spectral, jnp.zeros_like(spectral))


def shift_of(block, used):
    return block * used // LANES, block * used % LANES


def gather_kernel(slots, low, table_ref, rows_ref, *refs):
    outs, turned = refs[:-1], refs[-1]
    me = lax.axis_index("wave")
    used, waves = rows_ref.shape
    rows = jnp.concatenate([rows_ref[...], jnp.zeros((LANES - used, waves), jnp.bfloat16)], axis=0)
    number = lax.broadcasted_iota(jnp.int32, (waves, LANES), 0)
    for j in range(0, table_ref.shape[0], 2):
        chosen = jnp.concatenate(
            [(number == table_ref[k : k + 1, :]).astype(jnp.bfloat16) for k in (j, j + 1)], axis=1
        )
        got = jnp.dot(rows, chosen, preferred_element_type=jnp.float32)
        turned[j * LANES : (j + 2) * LANES, :] = got.T
    lane = lax.broadcasted_iota(jnp.int32, (STEP, LANES), 1)
    for t, out in enumerate(outs):
        for u in range(low):
            begin = (me ^ (t * low + u)) * slots
            tiles = [jnp.zeros((STEP, LANES), jnp.float32)] * (out.shape[2] // LANES)
            for block in range(slots // STEP):
                tile, off = shift_of(block, used)
                value = turned[pl.ds(pl.multiple_of(begin + block * STEP, STEP), STEP), :]
                value = pltpu.roll(value, off, 1) if off else value
                tiles[tile] = jnp.where(lane >= off, value, tiles[tile])
                if off + used > LANES:
                    tiles[tile + 1] = jnp.where(lane < off + used - LANES, value, tiles[tile + 1])
            for k, tile in enumerate(tiles):
                out[u, :, k * LANES : (k + 1) * LANES] = tile.astype(jnp.bfloat16)


def place_kernel(turns, lat_count, row_count, pairs, degrees, table_ref, out, limits):
    northern = lax.axis_index("lat") < lat_count // 2
    me = lax.axis_index("wave")
    row = lax.broadcasted_iota(jnp.int32, (LANES, 2 * LANES), 0) & (row_count - 1)
    col = lax.broadcasted_iota(jnp.int32, (LANES, 2 * LANES), 1) & (pairs - 1 | LANES)
    half = len(turns) // 2
    for k, turn in enumerate(turns):
        source = me ^ turn
        ascending = (source < half) == northern
        position = (source % half) * row_count + row
        position = jnp.where(ascending, position, pairs - 1 - position)
        target = position + jnp.where(ascending, 0, LANES)
        out[k * LANES : (k + 1) * LANES, :] = (col == target).astype(jnp.bfloat16)
    slots = limits.shape[0]
    line = lax.broadcasted_iota(jnp.int32, (TILE, LANES), 0)
    for first in range(0, slots, TILE):
        value = jnp.zeros((TILE, LANES), jnp.int32)
        for s in range(TILE):
            value = jnp.where(line == s, degrees - table_ref[me * slots + first + s], value)
        limits[first : first + TILE, :] = value


def multiply(coefs, table, first, half, terms):
    pairs = table.shape[1]
    group = 2 * LANES // pairs
    cols = coefs.shape[0] // STEP
    shape = (cols * group, 2 * LANES)
    diagonal = (lax.broadcasted_iota(jnp.int32, shape, 0) & (group - 1)) == (
        lax.broadcasted_iota(jnp.int32, shape, 1) // pairs
    )
    blank = jnp.zeros(shape, jnp.bfloat16)
    for g in range(STEP // group):
        block = jnp.concatenate(
            [coefs[c * STEP + g * group : c * STEP + (g + 1) * group] for c in range(cols)], axis=0
        ).astype(jnp.bfloat16)
        block = jnp.where(diagonal, jnp.concatenate([block, block], axis=1), blank)
        weights = table[g * group : (g + 1) * group, :, pl.ds(first, half)]
        got = jnp.dot(
            block, weights.reshape(group * pairs, half), preferred_element_type=jnp.float32
        )
        for c in range(cols):
            terms[pl.ds(c * STEP + g * group, group), :] = got[c * group : (c + 1) * group]


def pack(terms, core, sent, kept):
    rows = terms.shape[0]
    part = rows // 4
    lane_low = lax.broadcasted_iota(jnp.int32, (part, LANES), 1) < LANES // 2
    for out, target in ((sent, 1 - core), (kept, core)):
        first = pl.multiple_of(target * 3 * LANES, LANES)
        out[:rows, :] = terms[:, pl.ds(first, 2 * LANES)].astype(out.dtype)
    for j in range(2):
        low = terms[pl.ds(2 * j * part, part), pl.ds(2 * LANES, LANES)]
        high = terms[pl.ds((2 * j + 1) * part, part), pl.ds(2 * LANES, LANES)]
        zeroth = jnp.where(lane_low, low, pltpu.roll(high, LANES // 2, 1))
        other = jnp.where(lane_low, pltpu.roll(low, LANES // 2, 1), high)
        for out, target in ((sent, 1 - core), (kept, core)):
            out[rows:, j * LANES : (j + 1) * LANES] = jnp.where(target == 0, zeroth, other).astype(
                out.dtype
            )


def product_kernel(block, row_count, cols, place_ref, leg_ref, *refs):
    sources = refs[:-6]
    far_sent, far_own, near_sent, near_own, far, near = refs[-6:]
    half = far.shape[1]
    lat = lax.axis_index("lat")
    y, core = lat // 2, lat % 2
    tile, off = shift_of(block, row_count * cols)
    lane = lax.broadcasted_iota(jnp.int32, (STEP, LANES), 1)
    held = ((lane - off) & (LANES - 1)) // row_count
    zero = jnp.zeros((STEP, LANES), jnp.bfloat16)
    parts = []
    for source in sources:
        for k in range(source.shape[0]):
            value = source[k, :, tile * LANES : (tile + 1) * LANES]
            if off + row_count * cols > LANES:
                value = jnp.where(
                    lane >= off, value, source[k, :, (tile + 1) * LANES : (tile + 2) * LANES]
                )
            parts.append(
                jnp.concatenate([jnp.where(held == c, value, zero) for c in range(cols)], axis=0)
            )
    both = jnp.dot(
        jnp.concatenate(parts, axis=1), place_ref[...], preferred_element_type=jnp.float32
    )
    north, south = both[:, :LANES], both[:, LANES:]
    even, odd = north + south, north - south
    far_coefs, near_coefs = jnp.where(y == 0, odd, even), jnp.where(y == 0, even, odd)
    multiply(far_coefs, leg_ref, pl.multiple_of((1 - y) * half, LANES), half, far)
    multiply(near_coefs, leg_ref, pl.multiple_of(y * half, LANES), half, near)
    pack(far, core, far_sent, far_own)
    pack(near, core, near_sent, near_own)


def final_kernel(base, degrees, cols, limits_ref, near_ref, far_ref, *refs):
    out = refs[-1]
    lat = lax.axis_index("lat")
    first = lat % 2 == 0
    half = degrees // 2
    width = out.shape[2]
    rows = STEP * cols
    value = near_ref[...] + far_ref[...].astype(jnp.float32)
    main0, main1 = value[:rows, :LANES], value[:rows, LANES:]
    tails = []
    for j in range(4):
        tail = value[rows:, (j // 2) * LANES : (j // 2 + 1) * LANES]
        tails.append(pltpu.roll(tail, LANES // 2, 1) if j % 2 else tail)
    tail = jnp.concatenate(tails, axis=0)
    lane_low = lax.broadcasted_iota(jnp.int32, (rows, LANES), 1) < LANES // 2
    turn0, turn1 = pltpu.roll(main0, LANES // 2, 1), pltpu.roll(main1, LANES // 2, 1)
    ordered = jnp.concatenate(
        [
            jnp.where(first, main0, jnp.where(lane_low, tail, turn0)),
            jnp.where(first, main1, jnp.where(lane_low, turn0, turn1)),
            jnp.where(first, tail, turn1),
        ],
        axis=1,
    )
    shape = (STEP, 3 * LANES)
    degree = lat * width + lax.broadcasted_iota(jnp.int32, shape, 1)
    offsets = jnp.where(degree < half, 2 * degree, 2 * (degree - half) + 1)
    limits = limits_ref[base : base + STEP, :]
    limits = jnp.concatenate([limits] * 3, axis=1)
    inside = offsets < limits
    for c in range(cols):
        out[c] = jnp.where(inside, ordered[c * STEP : (c + 1) * STEP], 0.0)[:, :width]


def packed(fourier, wave_table, legendre):
    slots, pairs, degrees = legendre.shape
    row_count, cols, waves = fourier.shape
    wave_count, lat_count = lax.axis_size("wave"), lax.axis_size("lat")
    width = degrees // lat_count
    used = row_count * cols
    params = pltpu.CompilerParams(vmem_limit_bytes=VMEM)
    whole = pl.BlockSpec(memory_space=pltpu.VMEM)
    anywhere = pl.BlockSpec(memory_space=pl.ANY)

    message = -(-(slots // STEP) * used // LANES) * LANES
    low = 2
    high = wave_count // low
    ordered = pl.pallas_call(
        functools.partial(gather_kernel, slots, low),
        out_shape=[jax.ShapeDtypeStruct((low, STEP, message), jnp.bfloat16)] * high,
        in_specs=[whole, whole],
        out_specs=[whole] * high,
        scratch_shapes=[pltpu.VMEM((slots * wave_count, LANES), jnp.float32)],
        compiler_params=params,
        name="gather",
    )(
        wave_table.reshape(-1, LANES),
        jnp.transpose(fourier, (1, 0, 2)).reshape(used, waves),
    )
    turns = [
        t * low + u
        for u in range(low)
        for side in (0, 1)
        for t in range(side * high // 2, (side + 1) * high // 2)
    ]
    place, limits = pl.pallas_call(
        functools.partial(place_kernel, turns, lat_count, row_count, pairs, degrees),
        out_shape=[
            jax.ShapeDtypeStruct((wave_count * LANES, 2 * LANES), jnp.bfloat16),
            jax.ShapeDtypeStruct((slots, LANES), jnp.int32),
        ],
        in_specs=[pl.BlockSpec(memory_space=pltpu.SMEM)],
        out_specs=[whole] * 2,
        compiler_params=params,
        name="place",
    )(wave_table)

    passed = [ordered[0]] + [
        lax.ppermute(ordered[t], "wave", [(w, w ^ t * low) for w in range(wave_count)])
        for t in range(1, high)
    ]
    count = slots // STEP
    early = count - count // 2
    tables = [legendre[block * STEP : (block + 1) * STEP] for block in range(early)]
    sources = []
    for u in range(low):
        for side in (0, 1):
            block = jnp.stack([passed[t][u] for t in range(side * high // 2, (side + 1) * high // 2)])
            route = []
            for lat in range(lat_count):
                for wave in range(wave_count):
                    began = (wave >= wave_count // 2) != (side == 1)
                    to = lat_count - 1 - lat if began else lat
                    route.append((lat * wave_count + wave, to * wave_count + (wave ^ u)))
            block, tables = lax.optimization_barrier((block, tables))
            sources.append(lax.ppermute(block, ("lat", "wave"), route))

    rows = STEP * cols
    shape = (rows + rows // 4, 2 * LANES)
    core_route = [(lat, lat ^ 1) for lat in range(lat_count)]
    y_route = [(lat, lat ^ 2) for lat in range(lat_count)]
    scratch = [
        pltpu.VMEM((rows, degrees // 2), jnp.float32),
        pltpu.VMEM((rows, degrees // 2), jnp.float32),
    ]
    cost = pl.CostEstimate(flops=0, bytes_accessed=1024, transcendentals=0)
    pair_of_sums = [
        jax.ShapeDtypeStruct(shape, jnp.bfloat16),
        jax.ShapeDtypeStruct(shape, jnp.float32),
    ]
    def settle(sent, kept):
        return kept + lax.ppermute(sent, "lat", core_route).astype(jnp.float32)

    crossed, settled = [], []
    ties = []
    for block in range(count):
        if block == early - 1:
            legendre, sources, ties = lax.optimization_barrier((legendre, sources, ties))
            tables = tables + [legendre[k * STEP : (k + 1) * STEP] for k in range(early, count)]
        else:
            sources, ties = lax.optimization_barrier((sources, ties))
        far_sent, far_own, near_sent, near_own = pl.pallas_call(
            functools.partial(product_kernel, block, row_count, cols),
            out_shape=pair_of_sums * 2,
            in_specs=[whole] * (2 + len(sources)),
            out_specs=[whole] * 4,
            scratch_shapes=scratch,
            compiler_params=params,
            cost_estimate=cost,
            name="product",
        )(place, tables[block], *sources)
        summed = settle(far_sent, far_own).astype(jnp.bfloat16)
        ties = [summed] + settled[-1:]
        crossed.append(lax.ppermute(summed, "lat", y_route))
        settled.append(settle(near_sent, near_own))

    out = None
    for block in range(count):
        carried = [] if out is None else [out]
        out = pl.pallas_call(
            functools.partial(final_kernel, block * STEP, degrees, cols),
            grid=(1,),
            in_specs=[whole] * 3 + [anywhere] * len(carried),
            out_specs=pl.BlockSpec((cols, STEP, width), lambda g, at=block: (0, at, 0)),
            out_shape=jax.ShapeDtypeStruct((cols, slots, width), jnp.float32),
            input_output_aliases={3: 0} if carried else {},
            compiler_params=params,
            cost_estimate=cost,
            name="final",
        )(limits, settled[block], crossed[block], *carried)
    return jnp.transpose(out, (1, 0, 2))


def local(fourier, wave_table, legendre):
    slots, pairs, degrees = legendre.shape
    row_count, cols, waves = fourier.shape
    wave_count, lat_count = lax.axis_size("wave"), lax.axis_size("lat")
    fits = (
        lat_count == 4
        and wave_count & (wave_count - 1) == 0
        and slots % STEP == 0
        and degrees // 2 == 5 * LANES
        and row_count & (row_count - 1) == 0
        and LANES // 4 % row_count == 0
        and row_count * cols % (LANES // 4) == 0
        and row_count * cols <= LANES
        and pairs == row_count * wave_count // 2
        and pairs * TILE == 2 * LANES
        and waves % (2 * LANES) == 0
    )
    if not fits:
        return plain(fourier, wave_table, legendre)
    return packed(fourier, wave_table, legendre)


def solution(mesh):
    in_specs = (P(("lat", "wave"), None, None), P(), P("wave", "lat", None))
    out_specs = P("wave", None, "lat")
    return jax.shard_map(local, mesh=mesh, in_specs=in_specs, out_specs=out_specs, check_vma=False)
```

```python
import functools

import jax
import jax.numpy as jnp
from jax import lax
from jax.experimental import pallas as pl
from jax.experimental.pallas import tpu as pltpu
from jax.sharding import PartitionSpec as P

LANES = 128
STEP = 32
TILE = 8
VMEM = 20 * 1024 * 1024


def partner(block, axis, stride):
    count = lax.axis_size(axis)
    route = []
    for low in range(count):
        high = low | 1 << stride
        if high != low and high < count:
            route += [(low, high), (high, low)]
    return lax.ppermute(block, axis, route)


def plain(fourier, wave_table, legendre):
    slot_count, pair_count, degree_count = legendre.shape
    lat_count = lax.axis_size("lat")
    half_degrees = degree_count // 2
    slice_width = degree_count // lat_count
    lat_index = lax.axis_index("lat")
    ordered = jnp.take(fourier, wave_table, axis=2)
    arrived = lax.all_to_all(ordered, "wave", split_axis=2, concat_axis=0, tiled=True)
    local_rows = jnp.transpose(arrived, (2, 1, 0))
    kept_rows = local_rows[:, :, :pair_count]
    received = local_rows[:, :, pair_count:]
    for bit_number in range(lat_count.bit_length() - 1):
        received = partner(received, "lat", bit_number)
    northern = lat_index < lat_count // 2
    north_rows = jnp.where(northern, kept_rows, received).astype(jnp.float32)
    south_rows = jnp.where(northern, jnp.flip(received, 2), jnp.flip(kept_rows, 2)).astype(
        jnp.float32
    )
    even_part = (north_rows + south_rows).astype(jnp.bfloat16)
    odd_part = (north_rows - south_rows).astype(jnp.bfloat16)
    my_waves = lax.dynamic_slice_in_dim(wave_table, lax.axis_index("wave") * slot_count, slot_count)
    even_out = jnp.einsum(
        "mcp,mpk->mck", even_part, legendre[:, :, :half_degrees], preferred_element_type=jnp.float32
    )
    odd_out = jnp.einsum(
        "mcp,mpk->mck", odd_part, legendre[:, :, half_degrees:], preferred_element_type=jnp.float32
    )
    partial_terms = jnp.concatenate([even_out, odd_out], axis=2)
    spectral = lax.psum_scatter(partial_terms, "lat", scatter_dimension=2, tiled=True)
    degree_slot = lat_index * slice_width + jnp.arange(slice_width, dtype=jnp.int32)
    offsets = jnp.where(
        degree_slot < half_degrees, 2 * degree_slot, 2 * (degree_slot - half_degrees) + 1
    )
    inside = offsets[None, None, :] < (degree_count - my_waves)[:, None, None]
    return jnp.where(inside, spectral, jnp.zeros_like(spectral))


def shift_of(block, used):
    return block * used // LANES, block * used % LANES


def gather_kernel(slots, low, table_ref, rows_ref, *refs):
    outs, turned = refs[:-1], refs[-1]
    me = lax.axis_index("wave")
    used, waves = rows_ref.shape
    rows = jnp.concatenate([rows_ref[...], jnp.zeros((LANES - used, waves), jnp.bfloat16)], axis=0)
    number = lax.broadcasted_iota(jnp.int32, (waves, LANES), 0)
    for j in range(0, table_ref.shape[0], 2):
        chosen = jnp.concatenate(
            [(number == table_ref[k : k + 1, :]).astype(jnp.bfloat16) for k in (j, j + 1)], axis=1
        )
        got = jnp.dot(rows, chosen, preferred_element_type=jnp.float32)
        turned[j * LANES : (j + 2) * LANES, :] = got.T
    lane = lax.broadcasted_iota(jnp.int32, (STEP, LANES), 1)
    for t, out in enumerate(outs):
        for u in range(low):
            begin = (me ^ (t * low + u)) * slots
            tiles = [jnp.zeros((STEP, LANES), jnp.float32)] * (out.shape[2] // LANES)
            for block in range(slots // STEP):
                tile, off = shift_of(block, used)
                value = turned[pl.ds(pl.multiple_of(begin + block * STEP, STEP), STEP), :]
                value = pltpu.roll(value, off, 1) if off else value
                tiles[tile] = jnp.where(lane >= off, value, tiles[tile])
                if off + used > LANES:
                    tiles[tile + 1] = jnp.where(lane < off + used - LANES, value, tiles[tile + 1])
            for k, tile in enumerate(tiles):
                out[u, :, k * LANES : (k + 1) * LANES] = tile.astype(jnp.bfloat16)


def place_kernel(turns, lat_count, row_count, pairs, degrees, table_ref, out, limits):
    northern = lax.axis_index("lat") < lat_count // 2
    me = lax.axis_index("wave")
    row = lax.broadcasted_iota(jnp.int32, (LANES, 2 * LANES), 0) & (row_count - 1)
    col = lax.broadcasted_iota(jnp.int32, (LANES, 2 * LANES), 1) & (pairs - 1 | LANES)
    half = len(turns)
    for k in range(2 * half):
        ascending = northern if k < half else jnp.logical_not(northern)
        position = ((me ^ turns[k % half]) % half) * row_count + row
        position = jnp.where(ascending, position, pairs - 1 - position)
        target = position + jnp.where(ascending, 0, LANES)
        out[k * LANES : (k + 1) * LANES, :] = (col == target).astype(jnp.bfloat16)
    slots = limits.shape[0]
    line = lax.broadcasted_iota(jnp.int32, (TILE, LANES), 0)
    for first in range(0, slots, TILE):
        value = jnp.zeros((TILE, LANES), jnp.int32)
        for s in range(TILE):
            value = jnp.where(line == s, degrees - table_ref[me * slots + first + s], value)
        limits[first : first + TILE, :] = value


def multiply(coefs, table, first, half, terms):
    pairs = table.shape[1]
    group = 2 * LANES // pairs
    cols = coefs.shape[0] // STEP
    shape = (cols * group, 2 * LANES)
    diagonal = (lax.broadcasted_iota(jnp.int32, shape, 0) & (group - 1)) == (
        lax.broadcasted_iota(jnp.int32, shape, 1) // pairs
    )
    blank = jnp.zeros(shape, jnp.bfloat16)
    for g in range(STEP // group):
        block = jnp.concatenate(
            [coefs[c * STEP + g * group : c * STEP + (g + 1) * group] for c in range(cols)], axis=0
        ).astype(jnp.bfloat16)
        block = jnp.where(diagonal, jnp.concatenate([block, block], axis=1), blank)
        weights = table[g * group : (g + 1) * group, :, pl.ds(first, half)]
        got = jnp.dot(
            block, weights.reshape(group * pairs, half), preferred_element_type=jnp.float32
        )
        for c in range(cols):
            terms[pl.ds(c * STEP + g * group, group), :] = got[c * group : (c + 1) * group]


def pack(terms, core, sent, kept):
    rows = terms.shape[0]
    part = rows // 4
    lane_low = lax.broadcasted_iota(jnp.int32, (part, LANES), 1) < LANES // 2
    for out, target in ((sent, 1 - core), (kept, core)):
        first = pl.multiple_of(target * 3 * LANES, LANES)
        out[:rows, :] = terms[:, pl.ds(first, 2 * LANES)].astype(out.dtype)
    for j in range(2):
        low = terms[pl.ds(2 * j * part, part), pl.ds(2 * LANES, LANES)]
        high = terms[pl.ds((2 * j + 1) * part, part), pl.ds(2 * LANES, LANES)]
        zeroth = jnp.where(lane_low, low, pltpu.roll(high, LANES // 2, 1))
        other = jnp.where(lane_low, pltpu.roll(low, LANES // 2, 1), high)
        for out, target in ((sent, 1 - core), (kept, core)):
            out[rows:, j * LANES : (j + 1) * LANES] = jnp.where(target == 0, zeroth, other).astype(
                out.dtype
            )


def product_kernel(block, held_at, row_count, cols, place_ref, leg_ref, *refs):
    sources = refs[:-6]
    far_sent, far_own, near_sent, near_own, far, near = refs[-6:]
    half = far.shape[1]
    table = leg_ref.at[held_at * STEP : (held_at + 1) * STEP]
    lat = lax.axis_index("lat")
    y, core = lat // 2, lat % 2
    tile, off = shift_of(block, row_count * cols)
    lane = lax.broadcasted_iota(jnp.int32, (STEP, LANES), 1)
    held = ((lane - off) & (LANES - 1)) // row_count
    zero = jnp.zeros((STEP, LANES), jnp.bfloat16)
    parts = []
    for source in sources:
        for k in range(source.shape[0]):
            value = source[k, :, tile * LANES : (tile + 1) * LANES]
            if off + row_count * cols > LANES:
                value = jnp.where(
                    lane >= off, value, source[k, :, (tile + 1) * LANES : (tile + 2) * LANES]
                )
            parts.append(
                jnp.concatenate([jnp.where(held == c, value, zero) for c in range(cols)], axis=0)
            )
    both = jnp.dot(
        jnp.concatenate(parts, axis=1), place_ref[...], preferred_element_type=jnp.float32
    )
    north, south = both[:, :LANES], both[:, LANES:]
    even, odd = north + south, north - south
    far_coefs, near_coefs = jnp.where(y == 0, odd, even), jnp.where(y == 0, even, odd)
    multiply(far_coefs, table, pl.multiple_of((1 - y) * half, LANES), half, far)
    multiply(near_coefs, table, pl.multiple_of(y * half, LANES), half, near)
    pack(far, core, far_sent, far_own)
    pack(near, core, near_sent, near_own)


def final_kernel(base, degrees, cols, limits_ref, near_ref, far_ref, *refs):
    out = refs[-1]
    lat = lax.axis_index("lat")
    first = lat % 2 == 0
    half = degrees // 2
    width = out.shape[2]
    rows = STEP * cols
    value = near_ref[...] + far_ref[...].astype(jnp.float32)
    main0, main1 = value[:rows, :LANES], value[:rows, LANES:]
    tails = []
    for j in range(4):
        tail = value[rows:, (j // 2) * LANES : (j // 2 + 1) * LANES]
        tails.append(pltpu.roll(tail, LANES // 2, 1) if j % 2 else tail)
    tail = jnp.concatenate(tails, axis=0)
    lane_low = lax.broadcasted_iota(jnp.int32, (rows, LANES), 1) < LANES // 2
    turn0, turn1 = pltpu.roll(main0, LANES // 2, 1), pltpu.roll(main1, LANES // 2, 1)
    ordered = jnp.concatenate(
        [
            jnp.where(first, main0, jnp.where(lane_low, tail, turn0)),
            jnp.where(first, main1, jnp.where(lane_low, turn0, turn1)),
            jnp.where(first, tail, turn1),
        ],
        axis=1,
    )
    shape = (STEP, 3 * LANES)
    degree = lat * width + lax.broadcasted_iota(jnp.int32, shape, 1)
    offsets = jnp.where(degree < half, 2 * degree, 2 * (degree - half) + 1)
    limits = limits_ref[base : base + STEP, :]
    limits = jnp.concatenate([limits] * 3, axis=1)
    inside = offsets < limits
    for c in range(cols):
        out[c] = jnp.where(inside, ordered[c * STEP : (c + 1) * STEP], 0.0)[:, :width]


def packed(fourier, wave_table, legendre):
    slots, pairs, degrees = legendre.shape
    row_count, cols, waves = fourier.shape
    wave_count, lat_count = lax.axis_size("wave"), lax.axis_size("lat")
    width = degrees // lat_count
    used = row_count * cols
    params = pltpu.CompilerParams(vmem_limit_bytes=VMEM)
    whole = pl.BlockSpec(memory_space=pltpu.VMEM)
    anywhere = pl.BlockSpec(memory_space=pl.ANY)

    message = -(-(slots // STEP) * used // LANES) * LANES
    low = 2
    high = wave_count // low
    ordered = pl.pallas_call(
        functools.partial(gather_kernel, slots, low),
        out_shape=[jax.ShapeDtypeStruct((low, STEP, message), jnp.bfloat16)] * high,
        in_specs=[whole, whole],
        out_specs=[whole] * high,
        scratch_shapes=[pltpu.VMEM((slots * wave_count, LANES), jnp.float32)],
        compiler_params=params,
        name="gather",
    )(
        wave_table.reshape(-1, LANES),
        jnp.transpose(fourier, (1, 0, 2)).reshape(used, waves),
    )
    turns = [t * low + u for u in range(low) for t in range(high // 2)]
    passed = [ordered[0]] + [
        lax.ppermute(ordered[t], "wave", [(w, w ^ t * low) for w in range(wave_count)])
        for t in range(1, high)
    ]
    lower = lax.axis_index("wave") < wave_count // 2
    count = slots // STEP
    early = count - count // 2
    first = legendre[: early * STEP]
    sources = []
    for mirrored in (False, True):
        for u in range(low):
            sides = [
                jnp.stack([passed[t][u] for t in range(side * high // 2, (side + 1) * high // 2)])
                for side in (0, 1)
            ]
            block = jnp.where(lower != mirrored, sides[0], sides[1])
            block, first = lax.optimization_barrier((block, first))
            route = []
            for lat in range(lat_count):
                for wave in range(wave_count):
                    to = lat_count - 1 - lat if mirrored else lat
                    route.append((lat * wave_count + wave, to * wave_count + (wave ^ u)))
            if mirrored or u:
                block = lax.ppermute(block, ("lat", "wave"), route)
            sources.append(block)

    place, limits = pl.pallas_call(
        functools.partial(place_kernel, turns, lat_count, row_count, pairs, degrees),
        out_shape=[
            jax.ShapeDtypeStruct((wave_count * LANES, 2 * LANES), jnp.bfloat16),
            jax.ShapeDtypeStruct((slots, LANES), jnp.int32),
        ],
        in_specs=[pl.BlockSpec(memory_space=pltpu.SMEM)],
        out_specs=[whole] * 2,
        compiler_params=params,
        name="place",
    )(wave_table)

    rows = STEP * cols
    shape = (rows + rows // 4, 2 * LANES)
    core_route = [(lat, lat ^ 1) for lat in range(lat_count)]
    y_route = [(lat, lat ^ 2) for lat in range(lat_count)]
    scratch = [
        pltpu.VMEM((rows, degrees // 2), jnp.float32),
        pltpu.VMEM((rows, degrees // 2), jnp.float32),
    ]
    cost = pl.CostEstimate(flops=0, bytes_accessed=1024, transcendentals=0)
    pair_of_sums = [
        jax.ShapeDtypeStruct(shape, jnp.bfloat16),
        jax.ShapeDtypeStruct(shape, jnp.float32),
    ]
    def settle(sent, kept):
        return kept + lax.ppermute(sent, "lat", core_route).astype(jnp.float32)

    crossed, settled = [], []
    ties = []
    for block in range(count):
        if block == early - 1:
            legendre, sources, ties = lax.optimization_barrier((legendre, sources, ties))
            rest = legendre[early * STEP :]
        else:
            sources, ties = lax.optimization_barrier((sources, ties))
        far_sent, far_own, near_sent, near_own = pl.pallas_call(
            functools.partial(product_kernel, block, block - early * (block >= early), row_count, cols),
            out_shape=pair_of_sums * 2,
            in_specs=[whole] * (2 + len(sources)),
            out_specs=[whole] * 4,
            scratch_shapes=scratch,
            compiler_params=params,
            cost_estimate=cost,
            name="product",
        )(place, first if block < early else rest, *sources)
        summed = settle(far_sent, far_own).astype(jnp.bfloat16)
        ties = [summed] + settled[-1:]
        crossed.append(lax.ppermute(summed, "lat", y_route))
        settled.append(settle(near_sent, near_own))

    out = None
    for block in range(count):
        carried = [] if out is None else [out]
        out = pl.pallas_call(
            functools.partial(final_kernel, block * STEP, degrees, cols),
            grid=(1,),
            in_specs=[whole] * 3 + [anywhere] * len(carried),
            out_specs=pl.BlockSpec((cols, STEP, width), lambda g, at=block: (0, at, 0)),
            out_shape=jax.ShapeDtypeStruct((cols, slots, width), jnp.float32),
            input_output_aliases={3: 0} if carried else {},
            compiler_params=params,
            cost_estimate=cost,
            name="final",
        )(limits, settled[block], crossed[block], *carried)
    return jnp.transpose(out, (1, 0, 2))


def local(fourier, wave_table, legendre):
    slots, pairs, degrees = legendre.shape
    row_count, cols, waves = fourier.shape
    wave_count, lat_count = lax.axis_size("wave"), lax.axis_size("lat")
    fits = (
        lat_count == 4
        and wave_count & (wave_count - 1) == 0
        and slots % STEP == 0
        and degrees // 2 == 5 * LANES
        and row_count & (row_count - 1) == 0
        and LANES // 4 % row_count == 0
        and row_count * cols % (LANES // 4) == 0
        and row_count * cols <= LANES
        and pairs == row_count * wave_count // 2
        and pairs * TILE == 2 * LANES
        and waves % (2 * LANES) == 0
    )
    if not fits:
        return plain(fourier, wave_table, legendre)
    return packed(fourier, wave_table, legendre)


def solution(mesh):
    in_specs = (P(("lat", "wave"), None, None), P(), P("wave", "lat", None))
    out_specs = P("wave", None, "lat")
    return jax.shard_map(local, mesh=mesh, in_specs=in_specs, out_specs=out_specs, check_vma=False)
```

```python
import functools

import jax
import jax.numpy as jnp
from jax import lax
from jax.experimental import pallas as pl
from jax.experimental.pallas import tpu as pltpu
from jax.sharding import PartitionSpec as P

LANES = 128
STEP = 32
TILE = 8
VMEM = 16 * 1024 * 1024


def partner(block, axis, stride):
    count = lax.axis_size(axis)
    route = []
    for low in range(count):
        high = low | 1 << stride
        if high != low and high < count:
            route += [(low, high), (high, low)]
    return lax.ppermute(block, axis, route)


def plain(fourier, wave_table, legendre):
    slot_count, pair_count, degree_count = legendre.shape
    lat_count = lax.axis_size("lat")
    half_degrees = degree_count // 2
    slice_width = degree_count // lat_count
    lat_index = lax.axis_index("lat")
    ordered = jnp.take(fourier, wave_table, axis=2)
    arrived = lax.all_to_all(ordered, "wave", split_axis=2, concat_axis=0, tiled=True)
    local_rows = jnp.transpose(arrived, (2, 1, 0))
    kept_rows = local_rows[:, :, :pair_count]
    received = local_rows[:, :, pair_count:]
    for bit_number in range(lat_count.bit_length() - 1):
        received = partner(received, "lat", bit_number)
    northern = lat_index < lat_count // 2
    north_rows = jnp.where(northern, kept_rows, received).astype(jnp.float32)
    south_rows = jnp.where(northern, jnp.flip(received, 2), jnp.flip(kept_rows, 2)).astype(
        jnp.float32
    )
    even_part = (north_rows + south_rows).astype(jnp.bfloat16)
    odd_part = (north_rows - south_rows).astype(jnp.bfloat16)
    my_waves = lax.dynamic_slice_in_dim(wave_table, lax.axis_index("wave") * slot_count, slot_count)
    even_out = jnp.einsum(
        "mcp,mpk->mck", even_part, legendre[:, :, :half_degrees], preferred_element_type=jnp.float32
    )
    odd_out = jnp.einsum(
        "mcp,mpk->mck", odd_part, legendre[:, :, half_degrees:], preferred_element_type=jnp.float32
    )
    partial_terms = jnp.concatenate([even_out, odd_out], axis=2)
    spectral = lax.psum_scatter(partial_terms, "lat", scatter_dimension=2, tiled=True)
    degree_slot = lat_index * slice_width + jnp.arange(slice_width, dtype=jnp.int32)
    offsets = jnp.where(
        degree_slot < half_degrees, 2 * degree_slot, 2 * (degree_slot - half_degrees) + 1
    )
    inside = offsets[None, None, :] < (degree_count - my_waves)[:, None, None]
    return jnp.where(inside, spectral, jnp.zeros_like(spectral))


def shift_of(block, used):
    return block * used // LANES, block * used % LANES


def gather_kernel(slots, low, table_ref, rows_ref, *refs):
    outs, turned = refs[:-1], refs[-1]
    me = lax.axis_index("wave")
    used, waves = rows_ref.shape
    rows = jnp.concatenate([rows_ref[...], jnp.zeros((LANES - used, waves), jnp.bfloat16)], axis=0)
    number = lax.broadcasted_iota(jnp.int32, (waves, LANES), 0)
    for j in range(0, table_ref.shape[0], 2):
        chosen = jnp.concatenate(
            [(number == table_ref[k : k + 1, :]).astype(jnp.bfloat16) for k in (j, j + 1)], axis=1
        )
        got = jnp.dot(rows, chosen, preferred_element_type=jnp.float32)
        turned[j * LANES : (j + 2) * LANES, :] = got.T
    lane = lax.broadcasted_iota(jnp.int32, (STEP, LANES), 1)
    for t, out in enumerate(outs):
        for u in range(low):
            begin = (me ^ (t * low + u)) * slots
            tiles = [jnp.zeros((STEP, LANES), jnp.float32)] * (out.shape[2] // LANES)
            for block in range(slots // STEP):
                tile, off = shift_of(block, used)
                value = turned[pl.ds(pl.multiple_of(begin + block * STEP, STEP), STEP), :]
                value = pltpu.roll(value, off, 1) if off else value
                tiles[tile] = jnp.where(lane >= off, value, tiles[tile])
                if off + used > LANES:
                    tiles[tile + 1] = jnp.where(lane < off + used - LANES, value, tiles[tile + 1])
            for k, tile in enumerate(tiles):
                out[u, :, k * LANES : (k + 1) * LANES] = tile.astype(jnp.bfloat16)


def place_kernel(turns, lat_count, row_count, pairs, degrees, table_ref, out, limits):
    northern = lax.axis_index("lat") < lat_count // 2
    me = lax.axis_index("wave")
    row = lax.broadcasted_iota(jnp.int32, (LANES, 2 * LANES), 0) & (row_count - 1)
    col = lax.broadcasted_iota(jnp.int32, (LANES, 2 * LANES), 1) & (pairs - 1 | LANES)
    half = len(turns)
    for k in range(2 * half):
        ascending = northern if k < half else jnp.logical_not(northern)
        position = ((me ^ turns[k % half]) % half) * row_count + row
        position = jnp.where(ascending, position, pairs - 1 - position)
        target = position + jnp.where(ascending, 0, LANES)
        out[k * LANES : (k + 1) * LANES, :] = (col == target).astype(jnp.bfloat16)
    slots = limits.shape[0]
    line = lax.broadcasted_iota(jnp.int32, (TILE, LANES), 0)
    for first in range(0, slots, TILE):
        value = jnp.zeros((TILE, LANES), jnp.int32)
        for s in range(TILE):
            value = jnp.where(line == s, degrees - table_ref[me * slots + first + s], value)
        limits[first : first + TILE, :] = value


def multiply(coefs, table, first, half, terms):
    pairs = table.shape[1]
    group = 2 * LANES // pairs
    cols = coefs.shape[0] // STEP
    shape = (cols * group, 2 * LANES)
    diagonal = (lax.broadcasted_iota(jnp.int32, shape, 0) & (group - 1)) == (
        lax.broadcasted_iota(jnp.int32, shape, 1) // pairs
    )
    blank = jnp.zeros(shape, jnp.bfloat16)
    for g in range(STEP // group):
        block = jnp.concatenate(
            [coefs[c * STEP + g * group : c * STEP + (g + 1) * group] for c in range(cols)], axis=0
        ).astype(jnp.bfloat16)
        block = jnp.where(diagonal, jnp.concatenate([block, block], axis=1), blank)
        weights = table[g * group : (g + 1) * group, :, pl.ds(first, half)]
        got = jnp.dot(
            block, weights.reshape(group * pairs, half), preferred_element_type=jnp.float32
        )
        for c in range(cols):
            terms[pl.ds(c * STEP + g * group, group), :] = got[c * group : (c + 1) * group]


def pack(terms, core, sent, kept):
    rows = terms.shape[0]
    part = rows // 4
    lane_low = lax.broadcasted_iota(jnp.int32, (part, LANES), 1) < LANES // 2
    for out, target in ((sent, 1 - core), (kept, core)):
        first = pl.multiple_of(target * 3 * LANES, LANES)
        out[:rows, :] = terms[:, pl.ds(first, 2 * LANES)].astype(out.dtype)
    for j in range(2):
        low = terms[pl.ds(2 * j * part, part), pl.ds(2 * LANES, LANES)]
        high = terms[pl.ds((2 * j + 1) * part, part), pl.ds(2 * LANES, LANES)]
        zeroth = jnp.where(lane_low, low, pltpu.roll(high, LANES // 2, 1))
        other = jnp.where(lane_low, pltpu.roll(low, LANES // 2, 1), high)
        for out, target in ((sent, 1 - core), (kept, core)):
            out[rows:, j * LANES : (j + 1) * LANES] = jnp.where(target == 0, zeroth, other).astype(
                out.dtype
            )


def product_kernel(block, row_count, cols, place_ref, leg_ref, *refs):
    sources = refs[:-6]
    far_sent, far_own, near_sent, near_own, far, near = refs[-6:]
    half = far.shape[1]
    lat = lax.axis_index("lat")
    y, core = lat // 2, lat % 2
    tile, off = shift_of(block, row_count * cols)
    lane = lax.broadcasted_iota(jnp.int32, (STEP, LANES), 1)
    held = ((lane - off) & (LANES - 1)) // row_count
    zero = jnp.zeros((STEP, LANES), jnp.bfloat16)
    parts = []
    for source in sources:
        for k in range(source.shape[0]):
            value = source[k, :, tile * LANES : (tile + 1) * LANES]
            if off + row_count * cols > LANES:
                value = jnp.where(
                    lane >= off, value, source[k, :, (tile + 1) * LANES : (tile + 2) * LANES]
                )
            parts.append(
                jnp.concatenate([jnp.where(held == c, value, zero) for c in range(cols)], axis=0)
            )
    both = jnp.dot(
        jnp.concatenate(parts, axis=1), place_ref[...], preferred_element_type=jnp.float32
    )
    north, south = both[:, :LANES], both[:, LANES:]
    even, odd = north + south, north - south
    far_coefs, near_coefs = jnp.where(y == 0, odd, even), jnp.where(y == 0, even, odd)
    multiply(far_coefs, leg_ref, pl.multiple_of((1 - y) * half, LANES), half, far)
    multiply(near_coefs, leg_ref, pl.multiple_of(y * half, LANES), half, near)
    pack(far, core, far_sent, far_own)
    pack(near, core, near_sent, near_own)


def final_kernel(base, degrees, cols, limits_ref, near_ref, far_ref, *refs):
    out = refs[-1]
    lat = lax.axis_index("lat")
    first = lat % 2 == 0
    half = degrees // 2
    width = out.shape[2]
    rows = STEP * cols
    value = near_ref[...] + far_ref[...].astype(jnp.float32)
    main0, main1 = value[:rows, :LANES], value[:rows, LANES:]
    tails = []
    for j in range(4):
        tail = value[rows:, (j // 2) * LANES : (j // 2 + 1) * LANES]
        tails.append(pltpu.roll(tail, LANES // 2, 1) if j % 2 else tail)
    tail = jnp.concatenate(tails, axis=0)
    lane_low = lax.broadcasted_iota(jnp.int32, (rows, LANES), 1) < LANES // 2
    turn0, turn1 = pltpu.roll(main0, LANES // 2, 1), pltpu.roll(main1, LANES // 2, 1)
    ordered = jnp.concatenate(
        [
            jnp.where(first, main0, jnp.where(lane_low, tail, turn0)),
            jnp.where(first, main1, jnp.where(lane_low, turn0, turn1)),
            jnp.where(first, tail, turn1),
        ],
        axis=1,
    )
    shape = (STEP, 3 * LANES)
    degree = lat * width + lax.broadcasted_iota(jnp.int32, shape, 1)
    offsets = jnp.where(degree < half, 2 * degree, 2 * (degree - half) + 1)
    limits = limits_ref[base : base + STEP, :]
    limits = jnp.concatenate([limits] * 3, axis=1)
    inside = offsets < limits
    for c in range(cols):
        out[c] = jnp.where(inside, ordered[c * STEP : (c + 1) * STEP], 0.0)[:, :width]


def packed(fourier, wave_table, legendre):
    slots, pairs, degrees = legendre.shape
    row_count, cols, waves = fourier.shape
    wave_count, lat_count = lax.axis_size("wave"), lax.axis_size("lat")
    width = degrees // lat_count
    used = row_count * cols
    params = pltpu.CompilerParams(vmem_limit_bytes=VMEM)
    whole = pl.BlockSpec(memory_space=pltpu.VMEM)
    anywhere = pl.BlockSpec(memory_space=pl.ANY)

    message = -(-(slots // STEP) * used // LANES) * LANES
    low = 2
    high = wave_count // low
    ordered = pl.pallas_call(
        functools.partial(gather_kernel, slots, low),
        out_shape=[jax.ShapeDtypeStruct((low, STEP, message), jnp.bfloat16)] * high,
        in_specs=[whole, whole],
        out_specs=[whole] * high,
        scratch_shapes=[pltpu.VMEM((slots * wave_count, LANES), jnp.float32)],
        compiler_params=params,
        name="gather",
    )(
        wave_table.reshape(-1, LANES),
        jnp.transpose(fourier, (1, 0, 2)).reshape(used, waves),
    )
    turns = [t * low + u for u in range(low) for t in range(high // 2)]
    place, limits = pl.pallas_call(
        functools.partial(place_kernel, turns, lat_count, row_count, pairs, degrees),
        out_shape=[
            jax.ShapeDtypeStruct((wave_count * LANES, 2 * LANES), jnp.bfloat16),
            jax.ShapeDtypeStruct((slots, LANES), jnp.int32),
        ],
        in_specs=[pl.BlockSpec(memory_space=pltpu.SMEM)],
        out_specs=[whole] * 2,
        compiler_params=params,
        name="place",
    )(wave_table)

    passed = [ordered[0]] + [
        lax.ppermute(ordered[t], "wave", [(w, w ^ t * low) for w in range(wave_count)])
        for t in range(1, high)
    ]
    count = slots // STEP
    early = count - count // 2
    tables = [legendre[block * STEP : (block + 1) * STEP] for block in range(early)]
    lower = lax.axis_index("wave") < wave_count // 2
    sources = []
    for mirrored in (False, True):
        for u in range(low):
            sides = [
                jnp.stack([passed[t][u] for t in range(side * high // 2, (side + 1) * high // 2)])
                for side in (0, 1)
            ]
            block = jnp.where(lower != mirrored, sides[0], sides[1])
            block, tables = lax.optimization_barrier((block, tables))
            if not mirrored and u == 0:
                later, block = lax.optimization_barrier((legendre, block))
            route = []
            for lat in range(lat_count):
                for wave in range(wave_count):
                    to = lat_count - 1 - lat if mirrored else lat
                    route.append((lat * wave_count + wave, to * wave_count + (wave ^ u)))
            if mirrored or u:
                block = lax.ppermute(block, ("lat", "wave"), route)
            sources.append(block)

    tables += [later[block * STEP : (block + 1) * STEP] for block in range(early, count)]
    sources, tables = lax.optimization_barrier((sources, tables))

    rows = STEP * cols
    shape = (rows + rows // 4, 2 * LANES)
    core_route = [(lat, lat ^ 1) for lat in range(lat_count)]
    y_route = [(lat, lat ^ 2) for lat in range(lat_count)]
    scratch = [
        pltpu.VMEM((rows, degrees // 2), jnp.float32),
        pltpu.VMEM((rows, degrees // 2), jnp.float32),
    ]
    cost = pl.CostEstimate(flops=0, bytes_accessed=1024, transcendentals=0)
    pair_of_sums = [
        jax.ShapeDtypeStruct(shape, jnp.bfloat16),
        jax.ShapeDtypeStruct(shape, jnp.float32),
    ]
    def settle(sent, kept):
        return kept + lax.ppermute(sent, "lat", core_route).astype(jnp.float32)

    crossed, settled = [], []
    ties = []
    for block in range(count):
        sources, ties = lax.optimization_barrier((sources, ties))
        far_sent, far_own, near_sent, near_own = pl.pallas_call(
            functools.partial(product_kernel, block, row_count, cols),
            out_shape=pair_of_sums * 2,
            in_specs=[whole] * (2 + len(sources)),
            out_specs=[whole] * 4,
            scratch_shapes=scratch,
            compiler_params=params,
            cost_estimate=cost,
            name="product",
        )(place, tables[block], *sources)
        summed = settle(far_sent, far_own).astype(jnp.bfloat16)
        ties = [summed] + settled[-1:]
        crossed.append(lax.ppermute(summed, "lat", y_route))
        settled.append(settle(near_sent, near_own))

    out = None
    for block in range(count):
        carried = [] if out is None else [out]
        out = pl.pallas_call(
            functools.partial(final_kernel, block * STEP, degrees, cols),
            grid=(1,),
            in_specs=[whole] * 3 + [anywhere] * len(carried),
            out_specs=pl.BlockSpec((cols, STEP, width), lambda g, at=block: (0, at, 0)),
            out_shape=jax.ShapeDtypeStruct((cols, slots, width), jnp.float32),
            input_output_aliases={3: 0} if carried else {},
            compiler_params=params,
            cost_estimate=cost,
            name="final",
        )(limits, settled[block], crossed[block], *carried)
    return jnp.transpose(out, (1, 0, 2))


def local(fourier, wave_table, legendre):
    slots, pairs, degrees = legendre.shape
    row_count, cols, waves = fourier.shape
    wave_count, lat_count = lax.axis_size("wave"), lax.axis_size("lat")
    fits = (
        lat_count == 4
        and wave_count & (wave_count - 1) == 0
        and slots % STEP == 0
        and degrees // 2 == 5 * LANES
        and row_count & (row_count - 1) == 0
        and LANES // 4 % row_count == 0
        and row_count * cols % (LANES // 4) == 0
        and row_count * cols <= LANES
        and pairs == row_count * wave_count // 2
        and pairs * TILE == 2 * LANES
        and waves % (2 * LANES) == 0
    )
    if not fits:
        return plain(fourier, wave_table, legendre)
    return packed(fourier, wave_table, legendre)


def solution(mesh):
    in_specs = (P(("lat", "wave"), None, None), P(), P("wave", "lat", None))
    out_specs = P("wave", None, "lat")
    return jax.shard_map(local, mesh=mesh, in_specs=in_specs, out_specs=out_specs, check_vma=False)
```
